128 devices in a mesh: rep: 4 (over y), ty: 4 (over z), tx: 8 (over x, core).
Axes of the slice: x: 4, y: 4, z: 4, core: 2. Of those that a mesh axis runs over, the one named last changes fastest.
Arguments:
- inputs: bfloat16 [4, 256, 384, 256], P('rep', None, 'ty', 'tx'), may hold values from -6 to 6
- targets: bfloat16 [4, 256, 384, 256], P('rep', None, 'ty', 'tx'), may hold values from -6 to 6
- kern_one: float32 [3, 3, 256], replicated, may hold values from -2 to 2
- point_one: float32 [256, 512], replicated, may hold values from -0.375 to 0.375
- coarsening_taps: float32 [2, 2, 512, 512], replicated, may hold values from -0.125 to 0.125
- kern_two: float32 [3, 3, 512], replicated, may hold values from -2 to 2
- point_two: float32 [512, 256], replicated, may hold values from -0.25 to 0.25
Outputs:
- expected_precip_map: bfloat16 [4, 256, 384, 256], P('rep', None, 'ty', 'tx')
- new_kern_one: float32 [3, 3, 256], replicated
- new_point_one: float32 [256, 512], replicated
- new_stride: float32 [2, 2, 512, 512], replicated
- new_kern_two: float32 [3, 3, 512], replicated
- new_point_two: float32 [512, 256], replicated
- step_kern_one: float32 [3, 3, 256], replicated
- step_point_one: float32 [256, 512], replicated
- step_stride: float32 [2, 2, 512, 512], replicated
- step_kern_two: float32 [3, 3, 512], replicated
- step_point_two: float32 [512, 256], replicated
The draws below stay inside these ranges and needn't reach their ends.
All inputs are finite; a program needn't handle non-finite values.
Results may differ from the reference program's by a relative error of at most 0.008.
Values may be sent and summed in bfloat16 or wider, within the bound.
No kernel may reach another device: no remote copies, remote signals or barrier semaphores. Data moves between devices by JAX's collectives and lax.ppermute only.
A program may use at most 128 MiB of HBM per device.

```python
import jax
import jax.numpy as jnp
from jax import lax

C0 = 256
C1 = 512
BATCH = 4
H = 384
W = 256


def levels(key, dims, pieces, smallest, largest):
    loudness, own = 1.0, jax.random.fold_in(key, 6)
    for axis_at, parts in pieces:
        draws = jnp.exp(jax.random.uniform(jax.random.fold_in(own, axis_at), (parts,), jnp.float32, smallest / len(pieces), largest / len(pieces)))
        loudness = loudness * jnp.repeat(draws, dims[axis_at] // parts).reshape([-1 if axis == axis_at else 1 for axis in range(len(dims))])
    return loudness


def bell_draw(own_key, shape, width, bound, split=(), held_as=jnp.bfloat16):
    array = jax.random.normal(own_key, shape, jnp.float32) * width
    if len(split) > 0:
        array = levels(own_key, shape, split, -0.22, 0.18) * array
    return jnp.clip(array, min=-bound, max=bound).astype(held_as)


def setup_inputs(seed: int = 0) -> dict:
    keys = jax.random.split(jax.random.key(seed), 8)
    inputs = bell_draw(keys[0], (BATCH, C0, H, W), 1.0, 6.0, ((0, 4), (2, 4), (3, 8)))
    targets = bell_draw(keys[1], (BATCH, C0, H, W), 1.0, 6.0, ((0, 4), (2, 4), (3, 8)))
    kern_one = bell_draw(keys[2], (3, 3, C0), 9 ** -0.5, 2.0, (), jnp.float32)
    point_one = bell_draw(keys[3], (C0, C1), C0 ** -0.5, 0.375, (), jnp.float32)
    coarsening_taps = bell_draw(keys[4], (2, 2, C1, C1), (4 * C1) ** -0.5, 0.125, (), jnp.float32)
    kern_two = bell_draw(keys[5], (3, 3, C1), 9 ** -0.5, 2.0, (), jnp.float32)
    point_two = bell_draw(keys[6], (C1, C0), C1 ** -0.5, 0.25, (), jnp.float32)
    return dict(inputs=inputs, targets=targets, kern_one=kern_one, point_one=point_one, coarsening_taps=coarsening_taps, kern_two=kern_two, point_two=point_two)


EPS = 1e-05
RATE = 0.05

def depthwise(padded, kernel, rows, cols):
    total = jnp.zeros((padded.shape[0], rows, cols), jnp.float32)
    for row_off in range(3):
        for col_off in range(3):
            total = total + kernel[row_off, col_off][:, None, None] * padded[:, row_off:row_off + rows, col_off:col_off + cols]
    return total

def transposed(padded, kernel, rows, cols):
    total = jnp.zeros((padded.shape[0], rows, cols), jnp.float32)
    for row_off in range(3):
        for col_off in range(3):
            total = total + kernel[row_off, col_off][:, None, None] * padded[:, 2 - row_off:2 - row_off + rows, 2 - col_off:2 - col_off + cols]
    return total

def kernel_grad(cotangent, padded, rows, cols):
    return jnp.stack([jnp.stack([lax.optimization_barrier(jnp.sum(cotangent * padded[:, row_off:row_off + rows, col_off:col_off + cols], axis=(1, 2))) for col_off in range(3)]) for row_off in range(3)])

def silu_slope(value):
    sigma = jax.nn.sigmoid(value)
    return sigma * (1.0 + value * (1.0 - sigma))

def to_blocks(field, channels, half_r, half_c):
    return field.reshape(channels, half_r, 2, half_c, 2).transpose(2, 4, 0, 1, 3).reshape(4 * channels, half_r * half_c)

def from_blocks(blocks, channels, half_r, half_c):
    return blocks.reshape(2, 2, channels, half_r, half_c).transpose(2, 3, 0, 4, 1).reshape(channels, 2 * half_r, 2 * half_c)

def pad_one(field):
    return jnp.pad(field, ((0, 0), (1, 1), (1, 1)))

def tier_adjustment(weight, grad):
    normed = grad / jnp.sqrt(jnp.mean(grad * grad) + EPS)
    return (weight - RATE * jnp.sqrt(jnp.mean(weight * weight) + EPS) * normed, normed)

def reference(inputs, targets, kern_one, point_one, coarsening_taps, kern_two, point_two):
    channels = C0
    hidden = C1
    rows, cols = (H, W)
    half_r, half_c = (rows // 2, cols // 2)
    proj_one = point_one.astype(jnp.bfloat16)
    proj_two = point_two.astype(jnp.bfloat16)
    stride_low = coarsening_taps.astype(jnp.bfloat16).reshape(4 * hidden, hidden)
    grad_k1 = jnp.zeros(kern_one.shape, jnp.float32)
    grad_p1 = jnp.zeros(point_one.shape, jnp.float32)
    slope_of_coarsener = jnp.zeros(coarsening_taps.shape, jnp.float32)
    grad_k2 = jnp.zeros(kern_two.shape, jnp.float32)
    grad_p2 = jnp.zeros(point_two.shape, jnp.float32)
    returned_tuple = []
    for sample in range(BATCH):
        input_tile = inputs[sample]
        fine_pad = pad_one(input_tile).astype(jnp.float32)
        pre_one = depthwise(fine_pad, kern_one, rows, cols)
        pre_low = pre_one.astype(jnp.bfloat16).reshape(channels, rows * cols)
        act_one = jnp.dot(proj_one.T, pre_low, preferred_element_type=jnp.float32)
        out_one = jax.nn.silu(act_one).astype(jnp.bfloat16)
        blocks = to_blocks(out_one.reshape(hidden, rows, cols), hidden, half_r, half_c)
        coarse = jnp.dot(stride_low.T, blocks, preferred_element_type=jnp.float32).astype(jnp.bfloat16).reshape(hidden, half_r, half_c)
        coarse_pad = pad_one(coarse).astype(jnp.float32)
        pre_two = depthwise(coarse_pad, kern_two, half_r, half_c)
        out_two = jax.nn.silu(pre_two).astype(jnp.bfloat16).reshape(hidden, half_r * half_c)
        coarse_out = jnp.dot(proj_two.T, out_two, preferred_element_type=jnp.float32).reshape(channels, half_r, half_c)
        network_precip_guess = jnp.repeat(jnp.repeat(coarse_out, 2, axis=1), 2, axis=2) + input_tile.astype(jnp.float32)
        returned_tuple.append(network_precip_guess.astype(jnp.bfloat16))
        error = (network_precip_guess - targets[sample].astype(jnp.float32)) / BATCH
        coarse_err = error.reshape(channels, half_r, 2, half_c, 2).sum(axis=(2, 4)).astype(jnp.bfloat16).reshape(channels, half_r * half_c)
        grad_p2 = grad_p2 + jnp.dot(out_two, coarse_err.T, preferred_element_type=jnp.float32)
        back_two = jnp.dot(proj_two, coarse_err, preferred_element_type=jnp.float32).reshape(hidden, half_r, half_c)
        slope_two = (back_two * silu_slope(pre_two)).astype(jnp.bfloat16)
        grad_k2 = grad_k2 + kernel_grad(slope_two.astype(jnp.float32), coarse_pad, half_r, half_c)
        slope_pad = pad_one(slope_two).astype(jnp.float32)
        back_coarse = transposed(slope_pad, kern_two, half_r, half_c).astype(jnp.bfloat16).reshape(hidden, half_r * half_c)
        slope_of_coarsener = slope_of_coarsener + jnp.dot(blocks, back_coarse.T, preferred_element_type=jnp.float32).reshape(2, 2, hidden, hidden)
        back_blocks = jnp.dot(stride_low, back_coarse, preferred_element_type=jnp.float32)
        back_one = from_blocks(back_blocks, hidden, half_r, half_c).reshape(hidden, rows * cols)
        slope_one = (back_one * silu_slope(act_one)).astype(jnp.bfloat16)
        grad_p1 = grad_p1 + jnp.dot(pre_low, slope_one.T, preferred_element_type=jnp.float32)
        back_pre = jnp.dot(proj_one, slope_one, preferred_element_type=jnp.float32).reshape(channels, rows, cols)
        grad_k1 = grad_k1 + kernel_grad(back_pre, fine_pad, rows, cols)
    expected_precip_map = jnp.stack(returned_tuple)
    moved_leading_spatial, leading_spatial_step = tier_adjustment(kern_one, grad_k1)
    moved_leading_combiner, leading_combiner_step = tier_adjustment(point_one, grad_p1)
    moved_reducer_grid, reducer_grid_step = tier_adjustment(coarsening_taps, slope_of_coarsener)
    moved_trailing_spatial, trailing_spatial_step = tier_adjustment(kern_two, grad_k2)
    moved_trailing_combiner, trailing_combiner_step = tier_adjustment(point_two, grad_p2)
    return (expected_precip_map, moved_leading_spatial, moved_leading_combiner, moved_reducer_grid, moved_trailing_spatial, moved_trailing_combiner, leading_spatial_step, leading_combiner_step, reducer_grid_step, trailing_spatial_step, trailing_combiner_step)
```

```python
import jax
import jax.numpy as jnp
from jax import lax
from jax.experimental import pallas as pl
from jax.experimental.pallas import tpu as pltpu
from jax.sharding import PartitionSpec as P

EPS = 1e-05
RATE = 0.05
F32 = jnp.float32
BF16 = jnp.bfloat16
LANES = 128
HALO = 4
ROWS = 6
AXES = ("rep", "ty", "tx")


def mm(a, b):
    return jnp.dot(a, b, preferred_element_type=F32)


def mm_t(a, b):
    return lax.dot_general(a, b, (((1,), (1,)), ((), ())), preferred_element_type=F32)


def t_mm(a, b):
    return lax.dot_general(a, b, (((0,), (0,)), ((), ())), preferred_element_type=F32)


def sigmoid(v):
    return 0.5 + 0.5 * jnp.tanh(0.5 * v)


def tile_kernel(
    limits,
    x_ref,
    t_ref,
    top_ref,
    bot_ref,
    right_ref,
    left_ref,
    k1_ref,
    p1_ref,
    taps_ref,
    k2_ref,
    p2_ref,
    pred_ref,
    gk1_ref,
    gp1_ref,
    gst_ref,
    gk2_ref,
    gp2_ref,
    xf,
    tf,
    d2,
    out_e,
    out_own,
    pre_own,
    co,
    sl,
    cout,
    up,
    ot_own,
    ce_own,
    bc,
    bp,
):
    rows, cols, chan = x_ref.shape
    hid = k2_ref.shape[1]
    hr, hc = rows // 2, cols // 2
    slots = hc + 2 * HALO
    cb1, cb2 = chan // LANES, hid // LANES
    er = hr + 4
    fr = hr + 2

    def lanes(c):
        return slice(c * LANES, (c + 1) * LANES)

    def put(row, count, block, c):
        xf[c, pl.ds(row, count), 8 : 8 + cols, :] = block.astype(F32)

    for c in range(cb1):
        put(0, ROWS, top_ref[0:ROWS, :, lanes(c)], c)
        put(rows + ROWS, ROWS, bot_ref[0:ROWS, :, lanes(c)], c)

    step = 12

    @pl.loop(0, rows // step)
    def _(n):
        for c in range(cb1):
            put(ROWS + n * step, step, x_ref[pl.ds(n * step, step), :, lanes(c)], c)

    @pl.loop(0, (rows + 2 * ROWS) // step)
    def _(n):
        at = pl.ds(n * step, step)
        for c in range(cb1):
            right = right_ref[at, :, lanes(c)].astype(F32)
            left = left_ref[at, :, lanes(c)].astype(F32)
            xf[c, at, 8 + cols : 16 + cols, :] = right
            xf[c, at, 16 + cols : 24 + cols, :] = left
            xf[c, at, 7:8, :] = left[:, 7:8, :]
            xf[c, at, 24 + cols : 25 + cols, :] = xf[c, at, 8:9, :]

    def diff(first, count, block, c):
        e = 2 * first + ROWS
        at = pl.ds(e, 2 * count)
        tf[c, 0 : 2 * count, cols - 5 : cols + 3, :] = right_ref[at, :, lanes(c)].astype(F32)
        tf[c, 0 : 2 * count, cols + 13 : cols + 21, :] = left_ref[at, :, lanes(c)].astype(F32)
        tf[c, 0 : 2 * count, 0:cols, :] = block.astype(F32)
        both = xf[c, at, 8 : 24 + cols, :] - tf[c, 0 : 2 * count, 0 : 16 + cols, :]
        both = both.reshape(count, 2, 16 + cols, LANES)
        tf[c, 0:count, 0 : 16 + cols, :] = both[:, 0] + both[:, 1]
        even = tf[c, 0:count, pl.ds(0, slots, stride=2), :]
        odd = tf[c, 0:count, pl.ds(1, slots, stride=2), :]
        d2[c, pl.ds(first + 1, count), :, :] = (even + odd) * 0.25

    for c in range(cb1):
        diff(-1, 1, top_ref[ROWS : ROWS + 2, :, lanes(c)], c)
        diff(hr, 1, bot_ref[ROWS : ROWS + 2, :, lanes(c)], c)

    @pl.loop(0, hr // 4)
    def _(n):
        for c in range(cb1):
            diff(n * 4, 4, t_ref[pl.ds(n * 8, 8), :, lanes(c)], c)

    take = 4

    @pl.loop(0, er // take)
    def _(n):
        pres = []
        for c in range(cb1):
            k = k1_ref[:, lanes(c)]
            per = [[None] * take for _ in range(4)]
            for i in range(take):
                e = 2 * (n * take + i) + ROWS - 4
                for r in range(2):
                    total = [None, None]
                    for a in range(3):
                        at = e + r + a - 1
                        col = [xf[c, at, pl.ds(7 + o, slots, stride=2), :] for o in range(4)]
                        for q in range(2):
                            for b in range(3):
                                term = k[3 * a + b : 3 * a + b + 1, :] * col[q + b]
                                total[q] = term if total[q] is None else total[q] + term
                    for q in range(2):
                        per[2 * r + q][i] = total[q]
            pres.append([jnp.stack(p) for p in per])
        for ph in range(4):
            for c in range(cb1):
                own = pres[c][ph][:, 0:hc, :].reshape(take * hc, LANES).astype(BF16)
                pre_own[ph, pl.ds(n * (take * hc), take * hc), lanes(c)] = own
        low = [
            jnp.concatenate(
                [pres[c][ph].reshape(take * slots, LANES).astype(BF16) for c in range(cb1)], axis=1
            )
            for ph in range(4)
        ]
        for ph in range(4):
            act = mm(low[ph], p1_ref[...])
            out = act * sigmoid(act)
            out_e[ph, pl.ds(n * (take * slots), take * slots), :] = out.astype(BF16)
            own = out.reshape(take, slots, hid)[:, 0:hc, :].reshape(take * hc, hid)
            out_own[ph, pl.ds(n * (take * hc), take * hc), :] = own.astype(BF16)

    row_lo, row_hi, col_lo, col_hi = limits[0], limits[1], limits[2], limits[3]

    def inside(first, count):
        row = lax.broadcasted_iota(jnp.int32, (count, slots, LANES), 0) + first
        slot = lax.broadcasted_iota(jnp.int32, (count, slots, LANES), 1)
        col = jnp.where(slot < hc + HALO, slot, slot - slots)
        ok = (row >= row_lo) & (row < row_hi) & (col >= col_lo) & (col < col_hi)
        return jnp.where(ok, 1.0, 0.0).astype(F32)

    def wrapped(ref, c, at, value):
        ref[c, at, 8 : 8 + slots, :] = value
        ref[c, at, 7:8, :] = value[:, slots - 1 : slots, :]
        ref[c, at, 8 + slots : 9 + slots, :] = value[:, 0:1, :]

    half = er // 2

    @pl.loop(0, 2)
    def _(n):
        ok = inside(n * half - 2, half)
        for m in range(hid // 256):
            acc = None
            for ph in range(4):
                term = mm(
                    out_e[ph, pl.ds(n * (half * slots), half * slots), :],
                    taps_ref[ph, :, m * 256 : (m + 1) * 256],
                )
                acc = term if acc is None else acc + term
            acc = acc.astype(BF16).astype(F32).reshape(half, slots, 256)
            for j in range(2):
                wrapped(co, 2 * m + j, pl.ds(n * half, half), acc[:, :, lanes(j)] * ok)

    part = 10

    @pl.loop(0, fr // part)
    def _(n):
        pre = []
        for c in range(cb2):
            k = k2_ref[:, lanes(c)]
            total = None
            for a in range(3):
                for b in range(3):
                    at = pl.ds(n * part + a, part)
                    term = k[3 * a + b : 3 * a + b + 1, :] * co[c, at, 7 + b : 7 + b + slots, :]
                    total = term if total is None else total + term
            pre.append(total.reshape(part * slots, LANES))
        gate = [sigmoid(p) for p in pre]
        out = [p * g for p, g in zip(pre, gate)]
        low = jnp.concatenate([o.astype(BF16) for o in out], axis=1)
        for c in range(cb2):
            own = out[c].reshape(part, slots, LANES)[:, 0:hc, :].reshape(part * hc, LANES)
            ot_own[pl.ds(n * (part * hc), part * hc), lanes(c)] = own.astype(BF16)
        back = mm(low, p2_ref[...]).reshape(part, slots, chan)
        errs = []
        for c in range(cb1):
            own = back[:, :, lanes(c)]
            cout[c, pl.ds(n * part, part), :, :] = own[:, 0:hc, :]
            err = own + d2[c, pl.ds(n * part, part), :, :]
            errs.append(err.reshape(part * slots, LANES).astype(BF16))
            ce_own[pl.ds(n * (part * hc), part * hc), lanes(c)] = (
                err[:, 0:hc, :].reshape(part * hc, LANES).astype(BF16)
            )
        err = jnp.concatenate(errs, axis=1)
        ok = inside(n * part - 1, part)
        back_two = mm_t(err, p2_ref[...])
        for c in range(cb2):
            slope = back_two[:, lanes(c)] * (gate[c] * (1.0 + pre[c] * (1.0 - gate[c])))
            slope = slope.astype(BF16).astype(F32).reshape(part, slots, LANES) * ok
            wrapped(sl, c, pl.ds(n * part, part), slope)

    gp2_ref[...] = t_mm(ot_own[hc : hc + hr * hc, :], ce_own[hc : hc + hr * hc, :])

    @pl.loop(0, hr // 4)
    def _(n):
        for c in range(cb1):
            block = cout[c, pl.ds(n * 4 + 1, 4), :, :]
            up[c, :, pl.ds(0, hc, stride=2), :] = block
            up[c, :, pl.ds(1, hc, stride=2), :] = block
            wide = up[c, :, :, :]
            wide = jnp.stack([wide, wide], axis=1).reshape(8, cols, LANES)
            fine = xf[c, pl.ds(n * 8 + ROWS, 8), 8 : 8 + cols, :]
            pred_ref[pl.ds(n * 8, 8), :, lanes(c)] = (wide + fine).astype(BF16)

    for c in range(cb2):
        k = k2_ref[:, lanes(c)]

        def body(n, acc, c=c, k=k):
            acc = list(acc)
            for i in range(2):
                row = n * 2 + i
                slope = sl[c, row + 1, 8 : 8 + hc, :]
                total = None
                for a in range(3):
                    for b in range(3):
                        p = slope * co[c, row + 1 + a, 7 + b : 7 + b + hc, :]
                        acc[3 * a + b] = acc[3 * a + b] + (p[0:8] + p[8:16])
                        term = k[3 * a + b : 3 * a + b + 1, :] * sl[c, row + 2 - a, 9 - b : 9 - b + hc, :]
                        total = term if total is None else total + term
                bc[pl.ds(row * hc, hc), lanes(c)] = total.astype(BF16)
            return tuple(acc)

        acc = lax.fori_loop(0, hr // 2, body, tuple(jnp.zeros((8, LANES), F32) for _ in range(9)))
        for j in range(9):
            gk2_ref[j : j + 1, lanes(c)] = jnp.sum(acc[j], axis=0, keepdims=True)

    skip = 2 * hc
    own_rows = slice(skip, skip + hr * hc)
    for ph in range(4):
        gst_ref[ph] = t_mm(out_own[ph, own_rows, :], bc[...]).astype(gst_ref.dtype)
        back = mm_t(bc[...], taps_ref[ph])
        act = mm(pre_own[ph, own_rows, :], p1_ref[...])
        gate = sigmoid(act)
        slope = (back * (gate * (1.0 + act * (1.0 - gate)))).astype(BF16)
        gp1 = t_mm(pre_own[ph, own_rows, :], slope)
        if ph == 0:
            gp1_ref[...] = gp1
        else:
            gp1_ref[...] += gp1
        back_pre = mm_t(slope, p1_ref[...])
        for c in range(cb1):
            bp[ph, c] = back_pre[:, lanes(c)].reshape(hr, hc, LANES)

    for c in range(cb1):

        def body(n, acc, c=c):
            acc = list(acc)
            grads = [bp[ph, c, n] for ph in range(4)]
            for s in range(4):
                e = 2 * n + ROWS + s - 1
                col = [xf[c, e, pl.ds(7 + o, hc, stride=2), :] for o in range(4)]
                for r in range(2):
                    a = s - r
                    if 0 <= a < 3:
                        for q in range(2):
                            for b in range(3):
                                p = grads[2 * r + q] * col[q + b]
                                acc[3 * a + b] = acc[3 * a + b] + (p[0:8] + p[8:16])
            return tuple(acc)

        acc = lax.fori_loop(0, hr, body, tuple(jnp.zeros((8, LANES), F32) for _ in range(9)))
        for j in range(9):
            gk1_ref[j : j + 1, lanes(c)] = jnp.sum(acc[j], axis=0, keepdims=True)


def tile_step(limits, x, t, top, bot, right, left, k1, p1, taps, k2, p2):
    rows, cols, chan = x.shape
    hid = k2.shape[1]
    hr, hc = rows // 2, cols // 2
    slots = hc + 2 * HALO
    cb1, cb2 = chan // LANES, hid // LANES
    vm = pl.BlockSpec(memory_space=pltpu.VMEM)
    return pl.pallas_call(
        tile_kernel,
        out_shape=(
            jax.ShapeDtypeStruct(x.shape, BF16),
            jax.ShapeDtypeStruct(k1.shape, F32),
            jax.ShapeDtypeStruct(p1.shape, F32),
            jax.ShapeDtypeStruct(taps.shape, F32),
            jax.ShapeDtypeStruct(k2.shape, F32),
            jax.ShapeDtypeStruct(p2.shape, F32),
        ),
        in_specs=[pl.BlockSpec(memory_space=pltpu.SMEM)] + [vm] * 11,
        out_specs=[vm] * 6,
        scratch_shapes=[
            pltpu.VMEM((cb1, rows + 2 * ROWS, cols + 32, LANES), F32),
            pltpu.VMEM((cb1, 8, cols + 32, LANES), F32),
            pltpu.VMEM((cb1, hr + 2, slots, LANES), F32),
            pltpu.VMEM((4, (hr + 4) * slots, hid), BF16),
            pltpu.VMEM((4, (hr + 4) * hc, hid), BF16),
            pltpu.VMEM((4, (hr + 4) * hc, chan), BF16),
            pltpu.VMEM((cb2, hr + 4, slots + 16, LANES), F32),
            pltpu.VMEM((cb2, hr + 2, slots + 16, LANES), F32),
            pltpu.VMEM((cb1, hr + 2, hc, LANES), F32),
            pltpu.VMEM((cb1, 4, cols, LANES), F32),
            pltpu.VMEM(((hr + 2) * hc, hid), BF16),
            pltpu.VMEM(((hr + 2) * hc, chan), BF16),
            pltpu.VMEM((hr * hc, hid), BF16),
            pltpu.VMEM((4, cb1, hr, hc, LANES), F32),
        ],
        compiler_params=pltpu.CompilerParams(vmem_limit_bytes=63 * 1024 * 1024),
    )(limits, x, t, top, bot, right, left, k1, p1, taps, k2, p2)


def shift(block, axis, step):
    count = lax.axis_size(axis)
    return lax.ppermute(
        block, axis, [(i, i + step) for i in range(count) if 0 <= i + step < count]
    )


def adjusted(weight, grad):
    normed = grad / jnp.sqrt(jnp.mean(grad * grad) + EPS)
    return weight - RATE * jnp.sqrt(jnp.mean(weight * weight) + EPS) * normed, normed


def per_device(inputs, targets, kern_one, point_one, coarsening_taps, kern_two, point_two):
    x = jnp.transpose(inputs[0], (1, 2, 0))
    t = jnp.transpose(targets[0], (1, 2, 0))
    rows, cols, chan = x.shape
    hid = point_one.shape[1]
    hr, hc = rows // 2, cols // 2
    top = shift(jnp.concatenate([x[rows - ROWS :], t[rows - 2 :]], axis=0), "ty", 1)
    bot = shift(jnp.concatenate([x[:ROWS], t[:2]], axis=0), "ty", -1)

    def edge(cut):
        e = jnp.concatenate([top[:ROWS, cut], x[:, cut], bot[:ROWS, cut]], axis=0)
        z = jnp.zeros((ROWS - 2,) + e.shape[1:], BF16)
        f = jnp.concatenate([z, top[ROWS:, cut], t[:, cut], bot[ROWS:, cut], z], axis=0)
        return e, f

    e, f = edge(slice(0, 8))
    right = shift(jnp.concatenate([e[:, :5], f[:, :2], e[:, 7:]], axis=1), "tx", -1)
    e, f = edge(slice(cols - 8, cols))
    left = shift(jnp.concatenate([e[:, :1], f[:, 6:], e[:, 3:]], axis=1), "tx", 1)
    ty, tx = lax.axis_index("ty"), lax.axis_index("tx")
    big = 1 << 20
    limits = jnp.stack(
        [
            jnp.where(ty == 0, 0, -big),
            jnp.where(ty == lax.axis_size("ty") - 1, hr, big),
            jnp.where(tx == 0, 0, -big),
            jnp.where(tx == lax.axis_size("tx") - 1, hc, big),
        ]
    ).astype(jnp.int32)
    pred, gk1, gp1, gst, gk2, gp2 = tile_step(
        limits,
        x,
        t,
        top,
        bot,
        right,
        left,
        kern_one.reshape(9, chan),
        point_one.astype(BF16),
        coarsening_taps.astype(BF16).reshape(4, hid, hid),
        kern_two.reshape(9, hid),
        point_two.astype(BF16),
    )
    weights = (kern_one, point_one, coarsening_taps, kern_two, point_two)
    grads = lax.psum((gk1, gp1, gst, gk2, gp2), AXES)
    pairs = [adjusted(w, g.reshape(w.shape)) for w, g in zip(weights, grads)]
    return (
        jnp.transpose(pred, (2, 0, 1))[None],
        *[p[0] for p in pairs],
        *[p[1] for p in pairs],
    )


def solution(mesh):
    tile = P("rep", None, "ty", "tx")
    return jax.shard_map(
        per_device,
        mesh=mesh,
        in_specs=(tile, tile, P(), P(), P(), P(), P()),
        out_specs=(tile,) + (P(),) * 10,
        check_vma=False,
    )
```

```python
import jax
import jax.numpy as jnp
from jax import lax
from jax.experimental import pallas as pl
from jax.experimental.pallas import tpu as pltpu
from jax.sharding import PartitionSpec as P

EPS = 1e-05
RATE = 0.05
F32 = jnp.float32
BF16 = jnp.bfloat16
LANES = 128
HALO = 4
ROWS = 6
SMALL = 64


def mm(a, b):
    return jnp.dot(a, b, preferred_element_type=F32)


def mm_t(a, b):
    return lax.dot_general(a, b, (((1,), (1,)), ((), ())), preferred_element_type=F32)


def t_mm(a, b):
    return lax.dot_general(a, b, (((0,), (0,)), ((), ())), preferred_element_type=F32)


def sigmoid(v):
    return 0.5 + 0.5 * jnp.tanh(0.5 * v)


def tile_kernel(
    limits,
    x_ref,
    t_ref,
    top_ref,
    bot_ref,
    right_ref,
    left_ref,
    k1_ref,
    p1_ref,
    taps_ref,
    k2_ref,
    p2_ref,
    pred_ref,
    keep_ref,
    send_ref,
    xf,
    tf,
    d2,
    out_e,
    out_own,
    pre_own,
    co,
    sl,
    cout,
    up,
    ot_own,
    ce_own,
    bc,
    bp,
    small,
):
    rows, cols, chan = x_ref.shape
    hid = k2_ref.shape[2]
    hr, hc = rows // 2, cols // 2
    slots = hc + 2 * HALO
    cb1, cb2 = chan // LANES, hid // LANES
    er = hr + 4
    fr = hr + 2

    def lanes(c):
        return slice(c * LANES, (c + 1) * LANES)

    core = limits[4]
    st_rows, p1_rows, p2_rows = hid * (hid // LANES), chan * (hid // LANES), hid * (chan // LANES)
    p1_at = 2 * st_rows
    p2_at = p1_at + p1_rows // 2
    small_at = p2_at + p2_rows // 2

    def emit(half, at, value):
        value = value.astype(BF16)

        @pl.when(core == half)
        def _():
            keep_ref[at : at + value.shape[0], :] = value

        @pl.when(core != half)
        def _():
            send_ref[at : at + value.shape[0], :] = value

    small[...] = jnp.zeros_like(small)

    def put(row, count, block, c):
        xf[c, pl.ds(row, count), 8 : 8 + cols, :] = block.astype(F32)

    for c in range(cb1):
        put(0, ROWS, top_ref[0:ROWS, :, lanes(c)], c)
        put(rows + ROWS, ROWS, bot_ref[0:ROWS, :, lanes(c)], c)

    step = 12

    @pl.loop(0, rows // step)
    def _(n):
        for c in range(cb1):
            put(ROWS + n * step, step, x_ref[pl.ds(n * step, step), :, lanes(c)], c)

    @pl.loop(0, (rows + 2 * ROWS) // step)
    def _(n):
        at = pl.ds(n * step, step)
        for c in range(cb1):
            right = right_ref[at, :, lanes(c)].astype(F32)
            left = left_ref[at, :, lanes(c)].astype(F32)
            xf[c, at, 8 + cols : 16 + cols, :] = right
            xf[c, at, 16 + cols : 24 + cols, :] = left
            xf[c, at, 7:8, :] = left[:, 7:8, :]
            xf[c, at, 24 + cols : 25 + cols, :] = xf[c, at, 8:9, :]

    def diff(first, count, block, c):
        e = 2 * first + ROWS
        at = pl.ds(e, 2 * count)
        tf[c, 0 : 2 * count, cols - 5 : cols + 3, :] = right_ref[at, :, lanes(c)].astype(F32)
        tf[c, 0 : 2 * count, cols + 13 : cols + 21, :] = left_ref[at, :, lanes(c)].astype(F32)
        tf[c, 0 : 2 * count, 0:cols, :] = block.astype(F32)
        both = xf[c, at, 8 : 24 + cols, :] - tf[c, 0 : 2 * count, 0 : 16 + cols, :]
        both = both.reshape(count, 2, 16 + cols, LANES)
        tf[c, 0:count, 0 : 16 + cols, :] = both[:, 0] + both[:, 1]
        even = tf[c, 0:count, pl.ds(0, slots, stride=2), :]
        odd = tf[c, 0:count, pl.ds(1, slots, stride=2), :]
        d2[c, pl.ds(first + 1, count), :, :] = (even + odd) * 0.25

    for c in range(cb1):
        diff(-1, 1, top_ref[ROWS : ROWS + 2, :, lanes(c)], c)
        diff(hr, 1, bot_ref[ROWS : ROWS + 2, :, lanes(c)], c)

    @pl.loop(0, hr // 4)
    def _(n):
        for c in range(cb1):
            diff(n * 4, 4, t_ref[pl.ds(n * 8, 8), :, lanes(c)], c)

    take = 4

    @pl.loop(0, er // take)
    def _(n):
        pres = []
        for c in range(cb1):
            per = [[None] * take for _ in range(4)]
            for i in range(take):
                e = 2 * (n * take + i) + ROWS - 4
                for r in range(2):
                    total = [None, None]
                    for a in range(3):
                        at = e + r + a - 1
                        col = [xf[c, at, pl.ds(7 + o, slots, stride=2), :] for o in range(4)]
                        for q in range(2):
                            for b in range(3):
                                term = k1_ref[a, b : b + 1, lanes(c)] * col[q + b]
                                total[q] = term if total[q] is None else total[q] + term
                    for q in range(2):
                        per[2 * r + q][i] = total[q]
            pres.append([jnp.stack(p) for p in per])
        for ph in range(4):
            for c in range(cb1):
                own = pres[c][ph][:, 0:hc, :].reshape(take * hc, LANES).astype(BF16)
                pre_own[ph, pl.ds(n * (take * hc), take * hc), lanes(c)] = own
        low = [
            jnp.concatenate(
                [pres[c][ph].reshape(take * slots, LANES).astype(BF16) for c in range(cb1)], axis=1
            )
            for ph in range(4)
        ]
        for ph in range(4):
            act = mm(low[ph], p1_ref[...])
            out = act * sigmoid(act)
            out_e[ph, pl.ds(n * (take * slots), take * slots), :] = out.astype(BF16)
            own = out.reshape(take, slots, hid)[:, 0:hc, :].reshape(take * hc, hid)
            out_own[ph, pl.ds(n * (take * hc), take * hc), :] = own.astype(BF16)

    row_lo, row_hi, col_lo, col_hi = limits[0], limits[1], limits[2], limits[3]

    def inside(first, count):
        row = lax.broadcasted_iota(jnp.int32, (count, slots, LANES), 0) + first
        slot = lax.broadcasted_iota(jnp.int32, (count, slots, LANES), 1)
        col = jnp.where(slot < hc + HALO, slot, slot - slots)
        ok = (row >= row_lo) & (row < row_hi) & (col >= col_lo) & (col < col_hi)
        return jnp.where(ok, 1.0, 0.0).astype(F32)

    def wrapped(ref, c, at, value):
        ref[c, at, 8 : 8 + slots, :] = value
        ref[c, at, 7:8, :] = value[:, slots - 1 : slots, :]
        ref[c, at, 8 + slots : 9 + slots, :] = value[:, 0:1, :]

    half = er // 2

    @pl.loop(0, 2)
    def _(n):
        ok = inside(n * half - 2, half)
        for m in range(hid // 256):
            acc = None
            for ph in range(4):
                term = mm(
                    out_e[ph, pl.ds(n * (half * slots), half * slots), :],
                    taps_ref[ph, :, m * 256 : (m + 1) * 256],
                )
                acc = term if acc is None else acc + term
            acc = acc.astype(BF16).astype(F32).reshape(half, slots, 256)
            for j in range(2):
                wrapped(co, 2 * m + j, pl.ds(n * half, half), acc[:, :, lanes(j)] * ok)

    part = 10

    @pl.loop(0, fr // part)
    def _(n):
        pre = []
        for c in range(cb2):
            total = None
            for a in range(3):
                for b in range(3):
                    at = pl.ds(n * part + a, part)
                    term = k2_ref[a, b : b + 1, lanes(c)] * co[c, at, 7 + b : 7 + b + slots, :]
                    total = term if total is None else total + term
            pre.append(total.reshape(part * slots, LANES))
        gate = [sigmoid(p) for p in pre]
        out = [p * g for p, g in zip(pre, gate)]
        low = jnp.concatenate([o.astype(BF16) for o in out], axis=1)
        for c in range(cb2):
            own = out[c].reshape(part, slots, LANES)[:, 0:hc, :].reshape(part * hc, LANES)
            ot_own[pl.ds(n * (part * hc), part * hc), lanes(c)] = own.astype(BF16)
        back = mm(low, p2_ref[...]).reshape(part, slots, chan)
        errs = []
        for c in range(cb1):
            own = back[:, :, lanes(c)]
            cout[c, pl.ds(n * part, part), :, :] = own[:, 0:hc, :]
            err = own + d2[c, pl.ds(n * part, part), :, :]
            errs.append(err.reshape(part * slots, LANES).astype(BF16))
            ce_own[pl.ds(n * (part * hc), part * hc), lanes(c)] = (
                err[:, 0:hc, :].reshape(part * hc, LANES).astype(BF16)
            )
        err = jnp.concatenate(errs, axis=1)
        ok = inside(n * part - 1, part)
        back_two = mm_t(err, p2_ref[...])
        for c in range(cb2):
            slope = back_two[:, lanes(c)] * (gate[c] * (1.0 + pre[c] * (1.0 - gate[c])))
            slope = slope.astype(BF16).astype(F32).reshape(part, slots, LANES) * ok
            wrapped(sl, c, pl.ds(n * part, part), slope)

    gp2 = t_mm(ot_own[hc : hc + hr * hc, :], ce_own[hc : hc + hr * hc, :])
    for c in range(cb1):
        emit(2 * c // cb1, p2_at + (c % (cb1 // 2)) * hid, gp2[:, lanes(c)])

    @pl.loop(0, hr // 4)
    def _(n):
        for c in range(cb1):
            block = cout[c, pl.ds(n * 4 + 1, 4), :, :]
            up[c, :, pl.ds(0, hc, stride=2), :] = block
            up[c, :, pl.ds(1, hc, stride=2), :] = block
            wide = up[c, :, :, :]
            wide = jnp.stack([wide, wide], axis=1).reshape(8, cols, LANES)
            fine = xf[c, pl.ds(n * 8 + ROWS, 8), 8 : 8 + cols, :]
            pred_ref[pl.ds(n * 8, 8), :, lanes(c)] = (wide + fine).astype(BF16)

    for c in range(cb2):
        def body(n, acc, c=c):
            acc = list(acc)
            for i in range(2):
                row = n * 2 + i
                slope = sl[c, row + 1, 8 : 8 + hc, :]
                total = None
                for a in range(3):
                    for b in range(3):
                        p = slope * co[c, row + 1 + a, 7 + b : 7 + b + hc, :]
                        acc[3 * a + b] = acc[3 * a + b] + (p[0:8] + p[8:16])
                        term = k2_ref[a, b : b + 1, lanes(c)] * sl[c, row + 2 - a, 9 - b : 9 - b + hc, :]
                        total = term if total is None else total + term
                bc[pl.ds(row * hc, hc), lanes(c)] = total.astype(BF16)
            return tuple(acc)

        acc = lax.fori_loop(0, hr // 2, body, tuple(jnp.zeros((8, LANES), F32) for _ in range(9)))
        for j in range(9):
            at = 9 * (cb1 + c) + j
            small[at : at + 1, :] = jnp.sum(acc[j], axis=0, keepdims=True)

    skip = 2 * hc
    own_rows = slice(skip, skip + hr * hc)
    for ph in range(4):
        gst = t_mm(out_own[ph, own_rows, :], bc[...])
        for c in range(cb2):
            emit(ph // 2, (ph % 2) * st_rows + c * hid, gst[:, lanes(c)])
        back = mm_t(bc[...], taps_ref[ph])
        act = mm(pre_own[ph, own_rows, :], p1_ref[...])
        gate = sigmoid(act)
        slope = (back * (gate * (1.0 + act * (1.0 - gate)))).astype(BF16)
        term = t_mm(pre_own[ph, own_rows, :], slope)
        gp1 = term if ph == 0 else gp1 + term
        back_pre = mm_t(slope, p1_ref[...])
        for c in range(cb1):
            bp[ph, c] = back_pre[:, lanes(c)].reshape(hr, hc, LANES)

    for c in range(cb2):
        emit(2 * c // cb2, p1_at + (c % (cb2 // 2)) * chan, gp1[:, lanes(c)])

    for c in range(cb1):

        def body(n, acc, c=c):
            acc = list(acc)
            grads = [bp[ph, c, n] for ph in range(4)]
            for s in range(4):
                e = 2 * n + ROWS + s - 1
                col = [xf[c, e, pl.ds(7 + o, hc, stride=2), :] for o in range(4)]
                for r in range(2):
                    a = s - r
                    if 0 <= a < 3:
                        for q in range(2):
                            for b in range(3):
                                p = grads[2 * r + q] * col[q + b]
                                acc[3 * a + b] = acc[3 * a + b] + (p[0:8] + p[8:16])
            return tuple(acc)

        acc = lax.fori_loop(0, hr, body, tuple(jnp.zeros((8, LANES), F32) for _ in range(9)))
        for j in range(9):
            at = 9 * c + j
            small[at : at + 1, :] = jnp.sum(acc[j], axis=0, keepdims=True)


    for ref in (keep_ref, send_ref):
        ref[small_at : small_at + SMALL, :] = small[...].astype(BF16)


def vmem():
    return pl.BlockSpec(memory_space=pltpu.VMEM)


def smem():
    return pl.BlockSpec(memory_space=pltpu.SMEM)


def tile_step(limits, x, t, top, bot, right, left, k1, p1, taps, k2, p2):
    rows, cols, chan = x.shape
    hid = k2.shape[2]
    hr, hc = rows // 2, cols // 2
    slots = hc + 2 * HALO
    cb1, cb2 = chan // LANES, hid // LANES
    grads = (p1.size + taps.size + p2.size) // (2 * LANES) + SMALL
    return pl.pallas_call(
        tile_kernel,
        out_shape=(
            jax.ShapeDtypeStruct(x.shape, BF16),
            jax.ShapeDtypeStruct((grads, LANES), BF16),
            jax.ShapeDtypeStruct((grads, LANES), BF16),
        ),
        in_specs=[smem()] + [vmem()] * 11,
        out_specs=[vmem()] * 3,
        scratch_shapes=[
            pltpu.VMEM((cb1, rows + 2 * ROWS, cols + 32, LANES), F32),
            pltpu.VMEM((cb1, 8, cols + 32, LANES), F32),
            pltpu.VMEM((cb1, hr + 2, slots, LANES), F32),
            pltpu.VMEM((4, (hr + 4) * slots, hid), BF16),
            pltpu.VMEM((4, (hr + 4) * hc, hid), BF16),
            pltpu.VMEM((4, (hr + 4) * hc, chan), BF16),
            pltpu.VMEM((cb2, hr + 4, slots + 16, LANES), F32),
            pltpu.VMEM((cb2, hr + 2, slots + 16, LANES), F32),
            pltpu.VMEM((cb1, hr + 2, hc, LANES), F32),
            pltpu.VMEM((cb1, 4, cols, LANES), F32),
            pltpu.VMEM(((hr + 2) * hc, hid), BF16),
            pltpu.VMEM(((hr + 2) * hc, chan), BF16),
            pltpu.VMEM((hr * hc, hid), BF16),
            pltpu.VMEM((4, cb1, hr, hc, LANES), F32),
            pltpu.VMEM((SMALL, LANES), F32),
        ],
        compiler_params=pltpu.CompilerParams(vmem_limit_bytes=63 * 1024 * 1024),
        cost_estimate=pl.CostEstimate(flops=9_000_000_000, bytes_accessed=20_000_000, transcendentals=0),
    )(limits, x, t, top, bot, right, left, k1, p1, taps, k2, p2)


def norm_kernel(p1_ref, st_ref, p2_ref, k1_ref, k2_ref, out_ref):
    @pl.when(pl.program_id(0) == 0)
    def _():
        for j, ref in ((0, k1_ref), (1, p1_ref), (3, k2_ref), (4, p2_ref)):
            out_ref[j] = jnp.sum(ref[...] * ref[...])
        out_ref[2] = 0.0

    out_ref[2] += jnp.sum(st_ref[...] * st_ref[...])


def norms(k1, p1, taps, k2, p2):
    parts = taps.shape[0]
    return pl.pallas_call(
        norm_kernel,
        grid=(parts,),
        out_shape=jax.ShapeDtypeStruct((5,), F32),
        in_specs=[
            pl.BlockSpec(p1.shape, lambda n: (0, 0)),
            pl.BlockSpec((1,) + taps.shape[1:], lambda n: (n, 0, 0)),
            pl.BlockSpec(p2.shape, lambda n: (0, 0)),
            pl.BlockSpec(k1.shape, lambda n: (0, 0, 0)),
            pl.BlockSpec(k2.shape, lambda n: (0, 0, 0)),
        ],
        out_specs=smem(),
        cost_estimate=pl.CostEstimate(flops=3_000_000, bytes_accessed=5_300_000, transcendentals=0),
    )(p1, taps, p2, k1, k2)


def update_kernel(
    where,
    sums,
    own_ref,
    other_ref,
    k1_ref,
    p1_ref,
    st_ref,
    k2_ref,
    p2_ref,
    nk1_ref,
    np1_ref,
    nst_ref,
    nk2_ref,
    np2_ref,
    sk1_ref,
    sp1_ref,
    sst_ref,
    sk2_ref,
    sp2_ref,
    g,
    small,
    scale,
):
    chan, hid = p1_ref.shape
    cb1, cb2 = chan // LANES, hid // LANES
    parts, block = 4, st_ref.shape[1]
    step = pl.program_id(0)
    core = where[0]
    st_rows, p1_rows, p2_rows = hid * cb2, chan * cb2, hid * cb1
    p1_at = 2 * st_rows
    p2_at = p1_at + p1_rows // 2
    small_at = p2_at + p2_rows // 2
    sizes = (9 * chan, chan * hid, parts * hid * hid, 9 * hid, chan * hid)

    def root(v):
        v = jnp.full((8, LANES), v, F32)
        r = lax.rsqrt(v)
        r = r * (1.5 - 0.5 * v * r * r)
        return (v * r)[0, 0]

    def squares(at, count):
        acc = jnp.zeros((8, LANES), F32)
        for half in range(2):

            def body(n, acc, half=half):
                v = g[half, pl.ds(at + n * 128, 128), :].astype(F32)
                return acc + jnp.sum((v * v).reshape(16, 8, LANES), axis=0)

            acc = lax.fori_loop(0, count // 128, body, acc)
        return jnp.sum(acc)

    def set_scale(j, total):
        scale[j] = 1.0 / root(total / sizes[j] + EPS)
        scale[5 + j] = RATE * root(sums[j] / sizes[j] + EPS)

    @pl.when(step == 0)
    def _():
        g[core] = own_ref[0:small_at, :]
        g[1 - core] = other_ref[...]
        small[...] = own_ref[small_at : small_at + SMALL, :].astype(F32)
        v = small[0 : 9 * cb1, :]
        set_scale(0, jnp.sum(v * v))
        v = small[9 * cb1 : 9 * (cb1 + cb2), :]
        set_scale(3, jnp.sum(v * v))
        set_scale(1, squares(p1_at, p1_rows // 2))
        set_scale(2, squares(0, 2 * st_rows))
        set_scale(4, squares(p2_at, p2_rows // 2))
        for j, first, blocks, w, new, out in (
            (0, 0, cb1, k1_ref, nk1_ref, sk1_ref),
            (3, 9 * cb1, cb2, k2_ref, nk2_ref, sk2_ref),
        ):
            for c in range(blocks):
                cut = slice(c * LANES, (c + 1) * LANES)
                for r in range(3):
                    at = first + 9 * c + 3 * r
                    normed = small[at : at + 3, :] * scale[j]
                    out[r, :, cut] = normed
                    new[r, :, cut] = w[r, :, cut] - scale[5 + j] * normed
        for c in range(cb2):
            cut = slice(c * LANES, (c + 1) * LANES)
            at = p1_at + (c % (cb2 // 2)) * chan
            normed = g[2 * c // cb2, at : at + chan, :].astype(F32) * scale[1]
            sp1_ref[:, cut] = normed
            np1_ref[:, cut] = p1_ref[:, cut] - scale[6] * normed
        for c in range(cb1):
            cut = slice(c * LANES, (c + 1) * LANES)
            at = p2_at + (c % (cb1 // 2)) * hid
            normed = g[2 * c // cb1, at : at + hid, :].astype(F32) * scale[4]
            sp2_ref[:, cut] = normed
            np2_ref[:, cut] = p2_ref[:, cut] - scale[9] * normed

    per = hid // block
    ph = step // per
    for c in range(cb2):
        cut = slice(c * LANES, (c + 1) * LANES)
        at = (ph % 2) * st_rows + c * hid + (step % per) * block
        normed = g[ph // 2, pl.ds(at, block), :].astype(F32) * scale[2]
        sst_ref[0, :, cut] = normed
        nst_ref[0, :, cut] = st_ref[0, :, cut] - scale[7] * normed


def update(where, sums, own, other, k1, p1, taps, k2, p2):
    hid = taps.shape[1]
    block = hid // 4
    per = hid // block

    def whole(w):
        return pl.BlockSpec(w.shape, lambda n: (0,) * w.ndim)

    st = pl.BlockSpec((1, block, hid), lambda n: (n // per, n % per, 0))
    specs = [whole(k1), whole(p1), st, whole(k2), whole(p2)]
    shapes = [jax.ShapeDtypeStruct(w.shape, F32) for w in (k1, p1, taps, k2, p2)]
    return pl.pallas_call(
        update_kernel,
        grid=(4 * per,),
        out_shape=shapes + shapes,
        in_specs=[smem(), smem(), whole(own), whole(other)] + specs,
        out_specs=specs + specs,
        scratch_shapes=[
            pltpu.VMEM((2,) + other.shape, BF16),
            pltpu.VMEM((SMALL, LANES), F32),
            pltpu.SMEM((10,), F32),
        ],
        compiler_params=pltpu.CompilerParams(vmem_limit_bytes=40 * 1024 * 1024),
    )(where, sums, own, other, k1, p1, taps, k2, p2)


def shift(block, axis, step):
    count = lax.axis_size(axis)
    return lax.ppermute(
        block, axis, [(i, i + step) for i in range(count) if 0 <= i + step < count]
    )


class Ring:
    def __init__(self, name):
        axis = {"x": "tx", "y": "rep", "z": "ty"}[name]
        inner = 2 if name == "x" else 1
        self.axis, self.inner = axis, inner
        self.count = lax.axis_size(axis) // inner
        self.me = lax.axis_index(axis) // inner

    def send(self, block, step):
        n, inner = self.count, self.inner
        pairs = [
            (i * inner + k, (i + step) % n * inner + k) for i in range(n) for k in range(inner)
        ]
        return lax.ppermute(block, self.axis, pairs)

    def scatter(self, block, extra):
        n = self.count
        shares = block.reshape((n, -1, LANES))
        share = lax.dynamic_index_in_dim(shares, self.me, 0, False)
        cut = share.shape[0]
        got = []
        for d in range(1, n):
            out = lax.dynamic_index_in_dim(shares, (self.me + d) % n, 0, False)
            if extra is not None:
                out = jnp.concatenate([out, extra], axis=0)
            got.append(self.send(out, d))
        total = sum([g[:cut].astype(F32) for g in got], share.astype(F32)).astype(BF16)
        if extra is not None:
            extra = sum([g[cut:].astype(F32) for g in got], extra.astype(F32)).astype(BF16)
        return total, extra

    def gather(self, share):
        n = self.count
        out = jnp.zeros((n,) + share.shape, share.dtype)
        out = lax.dynamic_update_index_in_dim(out, share, self.me, 0)
        for d in range(1, n):
            got = self.send(share, d)
            out = lax.dynamic_update_index_in_dim(out, got, (self.me + n - d) % n, 0)
        return out.reshape(-1, LANES)


def reduced(keep, send):
    x, y, z = Ring("x"), Ring("y"), Ring("z")
    cores = [(i, i ^ 1) for i in range(lax.axis_size("tx"))]
    got = lax.ppermute(send, "tx", cores)
    both = (keep.astype(F32) + got.astype(F32)).astype(BF16)
    size = both.shape[0] - SMALL
    first, second, small = both[: size // 2], both[size // 2 : size], both[size:]
    first, small = x.scatter(first, small)
    second, _ = y.scatter(second, None)
    first, small = y.scatter(first, small)
    second, _ = x.scatter(second, None)
    share, small = z.scatter(jnp.concatenate([first, second], axis=0), small)
    both = z.gather(share)
    size = both.shape[0]
    first, second = y.gather(both[: size // 2]), x.gather(both[size // 2 :])
    first, second = x.gather(first), y.gather(second)
    half = jnp.concatenate([first, second], axis=0)
    other = lax.ppermute(half, "tx", cores)
    return jnp.concatenate([half, small], axis=0), other


def per_device(inputs, targets, kern_one, point_one, coarsening_taps, kern_two, point_two):
    x = jnp.transpose(inputs[0], (1, 2, 0))
    t = jnp.transpose(targets[0], (1, 2, 0))
    rows, cols, chan = x.shape
    hid = point_one.shape[1]
    hr, hc = rows // 2, cols // 2
    top = shift(jnp.concatenate([x[rows - ROWS :], t[rows - 2 :]], axis=0), "ty", 1)
    bot = shift(jnp.concatenate([x[:ROWS], t[:2]], axis=0), "ty", -1)

    def edge(cut):
        e = jnp.concatenate([top[:ROWS, cut], x[:, cut], bot[:ROWS, cut]], axis=0)
        z = jnp.zeros((ROWS - 2,) + e.shape[1:], BF16)
        f = jnp.concatenate([z, top[ROWS:, cut], t[:, cut], bot[ROWS:, cut], z], axis=0)
        return e, f

    e, f = edge(slice(0, 8))
    right = shift(jnp.concatenate([e[:, :5], f[:, :2], e[:, 7:]], axis=1), "tx", -1)
    e, f = edge(slice(cols - 8, cols))
    left = shift(jnp.concatenate([e[:, :1], f[:, 6:], e[:, 3:]], axis=1), "tx", 1)
    ty, tx = lax.axis_index("ty"), lax.axis_index("tx")
    big = 1 << 20
    limits = jnp.stack(
        [
            jnp.where(ty == 0, 0, -big),
            jnp.where(ty == lax.axis_size("ty") - 1, hr, big),
            jnp.where(tx == 0, 0, -big),
            jnp.where(tx == lax.axis_size("tx") - 1, hc, big),
            tx % 2,
        ]
    ).astype(jnp.int32)
    taps = coarsening_taps.reshape(4, hid, hid)
    pred, keep, send = tile_step(
        limits,
        x,
        t,
        top,
        bot,
        right,
        left,
        kern_one,
        point_one.astype(BF16),
        taps.astype(BF16),
        kern_two,
        point_two.astype(BF16),
    )
    weights, send = lax.optimization_barrier(((kern_one, point_one, taps, kern_two, point_two), send))
    sums = norms(*weights)
    own, other = reduced(keep, send)
    outs = update((tx % 2)[None].astype(jnp.int32), sums, own, other, *weights)
    outs = [o.reshape(coarsening_taps.shape) if o.shape == taps.shape else o for o in outs]
    return (jnp.transpose(pred, (2, 0, 1))[None], *outs)


def solution(mesh):
    tile = P("rep", None, "ty", "tx")
    return jax.shard_map(
        per_device,
        mesh=mesh,
        in_specs=(tile, tile, P(), P(), P(), P(), P()),
        out_specs=(tile,) + (P(),) * 10,
        check_vma=False,
    )
```

```python
import jax
import jax.numpy as jnp
from jax import lax
from jax.experimental import pallas as pl
from jax.experimental.pallas import tpu as pltpu
from jax.sharding import PartitionSpec as P

EPS = 1e-05
RATE = 0.05
F32 = jnp.float32
BF16 = jnp.bfloat16
LANES = 128
HALO = 4
ROWS = 6
SMALL = 64


def mm(a, b):
    return jnp.dot(a, b, preferred_element_type=F32)


def mm_t(a, b):
    return lax.dot_general(a, b, (((1,), (1,)), ((), ())), preferred_element_type=F32)


def t_mm(a, b):
    return lax.dot_general(a, b, (((0,), (0,)), ((), ())), preferred_element_type=F32)


def sigmoid(v):
    return 0.5 + 0.5 * jnp.tanh(0.5 * v)


def tile_kernel(
    limits,
    x_ref,
    t_ref,
    top_ref,
    bot_ref,
    right_ref,
    left_ref,
    k1_ref,
    p1_ref,
    taps_ref,
    k2_ref,
    p2_ref,
    pred_ref,
    keep_ref,
    send_ref,
    xf,
    tf,
    d2,
    out_e,
    out_own,
    pre_own,
    co,
    sl,
    cout,
    up,
    ot_own,
    ce_own,
    bc,
    bp,
    small,
):
    rows, cols, chan = x_ref.shape
    hid = k2_ref.shape[2]
    hr, hc = rows // 2, cols // 2
    slots = hc + 2 * HALO
    cb1, cb2 = chan // LANES, hid // LANES
    er = hr + 4
    fr = hr + 2

    def lanes(c):
        return slice(c * LANES, (c + 1) * LANES)

    core = limits[4]
    st_rows, p1_rows, p2_rows = hid * (hid // LANES), chan * (hid // LANES), hid * (chan // LANES)
    p1_at = 2 * st_rows
    p2_at = p1_at + p1_rows // 2
    small_at = p2_at + p2_rows // 2

    def emit(half, at, value):
        value = value.astype(BF16)

        @pl.when(core == half)
        def _():
            keep_ref[at : at + value.shape[0], :] = value

        @pl.when(core != half)
        def _():
            send_ref[at : at + value.shape[0], :] = value

    small[...] = jnp.zeros_like(small)

    def put(row, count, block, c):
        xf[c, pl.ds(row, count), 8 : 8 + cols, :] = block.astype(F32)

    for c in range(cb1):
        put(0, ROWS, top_ref[0:ROWS, :, lanes(c)], c)
        put(rows + ROWS, ROWS, bot_ref[0:ROWS, :, lanes(c)], c)

    step = 12

    @pl.loop(0, rows // step)
    def _(n):
        for c in range(cb1):
            put(ROWS + n * step, step, x_ref[pl.ds(n * step, step), :, lanes(c)], c)

    def put_sides(row, count, right, left, c):
        at = pl.ds(row, count)
        right, left = right.astype(F32), left.astype(F32)
        xf[c, at, 8 + cols : 16 + cols, :] = right
        xf[c, at, 16 + cols : 24 + cols, :] = left
        xf[c, at, 7:8, :] = left[:, 7:8, :]
        xf[c, at, 24 + cols : 25 + cols, :] = xf[c, at, 8:9, :]

    @pl.loop(0, (rows + 2 * ROWS) // step)
    def _(n):
        at = pl.ds(n * step, step)
        for c in range(cb1):
            put_sides(n * step, step, right_ref[at, :, lanes(c)], left_ref[at, :, lanes(c)], c)

    def diff(first, count, block, c):
        at = pl.ds(2 * first + ROWS, 2 * count)
        tf[c, 0 : 2 * count, cols - 5 : cols + 3, :] = right_ref[at, :, lanes(c)].astype(F32)
        tf[c, 0 : 2 * count, cols + 13 : cols + 21, :] = left_ref[at, :, lanes(c)].astype(F32)
        tf[c, 0 : 2 * count, 0:cols, :] = block.astype(F32)
        both = xf[c, at, 8 : 24 + cols, :] - tf[c, 0 : 2 * count, 0 : 16 + cols, :]
        both = both.reshape(count, 2, 16 + cols, LANES)
        tf[c, 0:count, 0 : 16 + cols, :] = both[:, 0] + both[:, 1]
        even = tf[c, 0:count, pl.ds(0, slots, stride=2), :]
        odd = tf[c, 0:count, pl.ds(1, slots, stride=2), :]
        d2[c, pl.ds(first + 1, count), :, :] = (even + odd) * 0.25

    for c in range(cb1):
        diff(-1, 1, top_ref[ROWS : ROWS + 2, :, lanes(c)], c)
        diff(hr, 1, bot_ref[ROWS : ROWS + 2, :, lanes(c)], c)

    @pl.loop(0, hr // 4)
    def _(n):
        for c in range(cb1):
            diff(n * 4, 4, t_ref[pl.ds(n * 8, 8), :, lanes(c)], c)

    take = 4

    @pl.loop(0, er // take)
    def _(n):
        pres = []
        for c in range(cb1):
            per = [[None] * take for _ in range(4)]
            for i in range(take):
                e = 2 * (n * take + i) + ROWS - 4
                for r in range(2):
                    total = [None, None]
                    for a in range(3):
                        at = e + r + a - 1
                        col = [xf[c, at, pl.ds(7 + o, slots, stride=2), :] for o in range(4)]
                        for q in range(2):
                            for b in range(3):
                                term = k1_ref[a, b : b + 1, lanes(c)] * col[q + b]
                                total[q] = term if total[q] is None else total[q] + term
                    for q in range(2):
                        per[2 * r + q][i] = total[q]
            pres.append([jnp.stack(p) for p in per])
        for ph in range(4):
            for c in range(cb1):
                own = pres[c][ph][:, 0:hc, :].reshape(take * hc, LANES).astype(BF16)
                pre_own[ph, pl.ds(n * (take * hc), take * hc), lanes(c)] = own
        low = [
            jnp.concatenate(
                [pres[c][ph].reshape(take * slots, LANES).astype(BF16) for c in range(cb1)], axis=1
            )
            for ph in range(4)
        ]
        for ph in range(4):
            act = mm(low[ph], p1_ref[...])
            out = act * sigmoid(act)
            out_e[ph, pl.ds(n * (take * slots), take * slots), :] = out.astype(BF16)
            own = out.reshape(take, slots, hid)[:, 0:hc, :].reshape(take * hc, hid)
            out_own[ph, pl.ds(n * (take * hc), take * hc), :] = own.astype(BF16)

    row_lo, row_hi, col_lo, col_hi = limits[0], limits[1], limits[2], limits[3]

    def inside(first, count):
        row = lax.broadcasted_iota(jnp.int32, (count, slots, LANES), 0) + first
        slot = lax.broadcasted_iota(jnp.int32, (count, slots, LANES), 1)
        col = jnp.where(slot < hc + HALO, slot, slot - slots)
        ok = (row >= row_lo) & (row < row_hi) & (col >= col_lo) & (col < col_hi)
        return jnp.where(ok, 1.0, 0.0).astype(F32)

    def wrapped(ref, c, at, value):
        ref[c, at, 8 : 8 + slots, :] = value
        ref[c, at, 7:8, :] = value[:, slots - 1 : slots, :]
        ref[c, at, 8 + slots : 9 + slots, :] = value[:, 0:1, :]

    half = er // 2

    @pl.loop(0, 2)
    def _(n):
        ok = inside(n * half - 2, half)
        for m in range(hid // 256):
            acc = None
            for ph in range(4):
                term = mm(
                    out_e[ph, pl.ds(n * (half * slots), half * slots), :],
                    taps_ref[ph, :, m * 256 : (m + 1) * 256],
                )
                acc = term if acc is None else acc + term
            acc = acc.astype(BF16).astype(F32).reshape(half, slots, 256)
            for j in range(2):
                wrapped(co, 2 * m + j, pl.ds(n * half, half), acc[:, :, lanes(j)] * ok)

    part = 10

    @pl.loop(0, fr // part)
    def _(n):
        pre = []
        for c in range(cb2):
            total = None
            for a in range(3):
                for b in range(3):
                    at = pl.ds(n * part + a, part)
                    term = k2_ref[a, b : b + 1, lanes(c)] * co[c, at, 7 + b : 7 + b + slots, :]
                    total = term if total is None else total + term
            pre.append(total.reshape(part * slots, LANES))
        gate = [sigmoid(p) for p in pre]
        out = [p * g for p, g in zip(pre, gate)]
        low = jnp.concatenate([o.astype(BF16) for o in out], axis=1)
        for c in range(cb2):
            own = out[c].reshape(part, slots, LANES)[:, 0:hc, :].reshape(part * hc, LANES)
            ot_own[pl.ds(n * (part * hc), part * hc), lanes(c)] = own.astype(BF16)
        back = mm(low, p2_ref[...]).reshape(part, slots, chan)
        errs = []
        for c in range(cb1):
            own = back[:, :, lanes(c)]
            cout[c, pl.ds(n * part, part), :, :] = own[:, 0:hc, :]
            err = own + d2[c, pl.ds(n * part, part), :, :]
            errs.append(err.reshape(part * slots, LANES).astype(BF16))
            ce_own[pl.ds(n * (part * hc), part * hc), lanes(c)] = (
                err[:, 0:hc, :].reshape(part * hc, LANES).astype(BF16)
            )
        err = jnp.concatenate(errs, axis=1)
        ok = inside(n * part - 1, part)
        back_two = mm_t(err, p2_ref[...])
        for c in range(cb2):
            slope = back_two[:, lanes(c)] * (gate[c] * (1.0 + pre[c] * (1.0 - gate[c])))
            slope = slope.astype(BF16).astype(F32).reshape(part, slots, LANES) * ok
            wrapped(sl, c, pl.ds(n * part, part), slope)

    gp2 = t_mm(ot_own[hc : hc + hr * hc, :], ce_own[hc : hc + hr * hc, :])
    for c in range(cb1):
        emit(2 * c // cb1, p2_at + (c % (cb1 // 2)) * hid, gp2[:, lanes(c)])

    @pl.loop(0, hr // 4)
    def _(n):
        for c in range(cb1):
            block = cout[c, pl.ds(n * 4 + 1, 4), :, :]
            up[c, :, pl.ds(0, hc, stride=2), :] = block
            up[c, :, pl.ds(1, hc, stride=2), :] = block
            wide = up[c, :, :, :]
            wide = jnp.stack([wide, wide], axis=1).reshape(8, cols, LANES)
            fine = xf[c, pl.ds(n * 8 + ROWS, 8), 8 : 8 + cols, :]
            pred_ref[pl.ds(n * 8, 8), :, lanes(c)] = (wide + fine).astype(BF16)

    for c in range(cb2):
        def body(n, acc, c=c):
            acc = list(acc)
            for i in range(2):
                row = n * 2 + i
                slope = sl[c, row + 1, 8 : 8 + hc, :]
                total = None
                for a in range(3):
                    for b in range(3):
                        p = slope * co[c, row + 1 + a, 7 + b : 7 + b + hc, :]
                        acc[3 * a + b] = acc[3 * a + b] + (p[0:8] + p[8:16])
                        term = k2_ref[a, b : b + 1, lanes(c)] * sl[c, row + 2 - a, 9 - b : 9 - b + hc, :]
                        total = term if total is None else total + term
                bc[pl.ds(row * hc, hc), lanes(c)] = total.astype(BF16)
            return tuple(acc)

        acc = lax.fori_loop(0, hr // 2, body, tuple(jnp.zeros((8, LANES), F32) for _ in range(9)))
        for j in range(9):
            at = 9 * (cb1 + c) + j
            small[at : at + 1, :] = jnp.sum(acc[j], axis=0, keepdims=True)

    skip = 2 * hc
    own_rows = slice(skip, skip + hr * hc)
    for ph in range(4):
        gst = t_mm(out_own[ph, own_rows, :], bc[...])
        for c in range(cb2):
            emit(ph // 2, (ph % 2) * st_rows + c * hid, gst[:, lanes(c)])
        back = mm_t(bc[...], taps_ref[ph])
        act = mm(pre_own[ph, own_rows, :], p1_ref[...])
        gate = sigmoid(act)
        slope = (back * (gate * (1.0 + act * (1.0 - gate)))).astype(BF16)
        term = t_mm(pre_own[ph, own_rows, :], slope)
        gp1 = term if ph == 0 else gp1 + term
        back_pre = mm_t(slope, p1_ref[...])
        for c in range(cb1):
            bp[ph, c] = back_pre[:, lanes(c)].reshape(hr, hc, LANES)

    for c in range(cb2):
        emit(2 * c // cb2, p1_at + (c % (cb2 // 2)) * chan, gp1[:, lanes(c)])

    for c in range(cb1):

        def body(n, acc, c=c):
            acc = list(acc)
            grads = [bp[ph, c, n] for ph in range(4)]
            for s in range(4):
                e = 2 * n + ROWS + s - 1
                col = [xf[c, e, pl.ds(7 + o, hc, stride=2), :] for o in range(4)]
                for r in range(2):
                    a = s - r
                    if 0 <= a < 3:
                        for q in range(2):
                            for b in range(3):
                                p = grads[2 * r + q] * col[q + b]
                                acc[3 * a + b] = acc[3 * a + b] + (p[0:8] + p[8:16])
            return tuple(acc)

        acc = lax.fori_loop(0, hr, body, tuple(jnp.zeros((8, LANES), F32) for _ in range(9)))
        for j in range(9):
            at = 9 * c + j
            small[at : at + 1, :] = jnp.sum(acc[j], axis=0, keepdims=True)


    for ref in (keep_ref, send_ref):
        ref[small_at : small_at + SMALL, :] = small[...].astype(BF16)


def vmem():
    return pl.BlockSpec(memory_space=pltpu.VMEM)


def smem():
    return pl.BlockSpec(memory_space=pltpu.SMEM)


def tile_step(limits, x, t, halos, k1, p1, taps, k2, p2):
    rows, cols, chan = x.shape
    hid = k2.shape[2]
    hr, hc = rows // 2, cols // 2
    slots = hc + 2 * HALO
    cb1, cb2 = chan // LANES, hid // LANES
    grads = (p1.size + taps.size + p2.size) // (2 * LANES) + SMALL
    return pl.pallas_call(
        tile_kernel,
        out_shape=(
            jax.ShapeDtypeStruct(x.shape, BF16),
            jax.ShapeDtypeStruct((grads, LANES), BF16),
            jax.ShapeDtypeStruct((grads, LANES), BF16),
        ),
        in_specs=[smem()] + [vmem()] * (7 + len(halos)),
        out_specs=[vmem()] * 3,
        scratch_shapes=[
            pltpu.VMEM((cb1, rows + 2 * ROWS, cols + 32, LANES), F32),
            pltpu.VMEM((cb1, 8, cols + 32, LANES), F32),
            pltpu.VMEM((cb1, hr + 2, slots, LANES), F32),
            pltpu.VMEM((4, (hr + 4) * slots, hid), BF16),
            pltpu.VMEM((4, (hr + 4) * hc, hid), BF16),
            pltpu.VMEM((4, (hr + 4) * hc, chan), BF16),
            pltpu.VMEM((cb2, hr + 4, slots + 16, LANES), F32),
            pltpu.VMEM((cb2, hr + 2, slots + 16, LANES), F32),
            pltpu.VMEM((cb1, hr + 2, hc, LANES), F32),
            pltpu.VMEM((cb1, 4, cols, LANES), F32),
            pltpu.VMEM(((hr + 2) * hc, hid), BF16),
            pltpu.VMEM(((hr + 2) * hc, chan), BF16),
            pltpu.VMEM((hr * hc, hid), BF16),
            pltpu.VMEM((4, cb1, hr, hc, LANES), F32),
            pltpu.VMEM((SMALL, LANES), F32),
        ],
        compiler_params=pltpu.CompilerParams(vmem_limit_bytes=63 * 1024 * 1024),
        cost_estimate=pl.CostEstimate(flops=9_000_000_000, bytes_accessed=20_000_000, transcendentals=0),
    )(limits, x, t, *halos, k1, p1, taps, k2, p2)


def prepare_kernel(p1_ref, st_ref, p2_ref, k1_ref, k2_ref, lp1_ref, lst_ref, lp2_ref, out_ref, acc):
    step = pl.program_id(0)

    @pl.when(step == 0)
    def _():
        for j, ref in ((0, k1_ref), (1, p1_ref), (3, k2_ref), (4, p2_ref)):
            out_ref[j] = jnp.sum(ref[...] * ref[...])
        lp1_ref[...] = p1_ref[...].astype(BF16)
        lp2_ref[...] = p2_ref[...].astype(BF16)
        acc[...] = jnp.zeros_like(acc)

    w = st_ref[0]
    lst_ref[0] = w.astype(BF16)
    acc[...] += jnp.sum((w * w).reshape(-1, 8, w.shape[1]), axis=0)

    @pl.when(step == pl.num_programs(0) - 1)
    def _():
        out_ref[2] = jnp.sum(acc[...])


def prepared(k1, p1, taps, k2, p2):
    parts, hid = taps.shape[:2]
    p1_spec = pl.BlockSpec(p1.shape, lambda n: (0, 0))
    st_spec = pl.BlockSpec((1,) + taps.shape[1:], lambda n: (n, 0, 0))
    p2_spec = pl.BlockSpec(p2.shape, lambda n: (0, 0))
    return pl.pallas_call(
        prepare_kernel,
        grid=(parts,),
        out_shape=[jax.ShapeDtypeStruct(w.shape, BF16) for w in (p1, taps, p2)]
        + [jax.ShapeDtypeStruct((5,), F32)],
        in_specs=[
            p1_spec,
            st_spec,
            p2_spec,
            pl.BlockSpec(k1.shape, lambda n: (0, 0, 0)),
            pl.BlockSpec(k2.shape, lambda n: (0, 0, 0)),
        ],
        out_specs=[p1_spec, st_spec, p2_spec, smem()],
        scratch_shapes=[pltpu.VMEM((8, hid), F32)],
        cost_estimate=pl.CostEstimate(flops=3_000_000, bytes_accessed=8_000_000, transcendentals=0),
    )(p1, taps, p2, k1, k2)


def update_kernel(
    where,
    sums,
    small_ref,
    own_ref,
    other_ref,
    *refs,
):
    (
        k1_ref,
        p1_ref,
        st_ref,
        k2_ref,
        p2_ref,
        nk1_ref,
        np1_ref,
        nst_ref,
        nk2_ref,
        np2_ref,
        sk1_ref,
        sp1_ref,
        sst_ref,
        sk2_ref,
        sp2_ref,
        g,
        small,
        scale,
    ) = refs
    chan, hid = p1_ref.shape
    cb1, cb2 = chan // LANES, hid // LANES
    parts, block = 4, st_ref.shape[1]
    step = pl.program_id(0)
    core = where[0]
    st_rows, p1_rows, p2_rows = hid * cb2, chan * cb2, hid * cb1
    p1_at = 2 * st_rows
    p2_at = p1_at + p1_rows // 2
    small_at = p2_at + p2_rows // 2
    sizes = (9 * chan, chan * hid, parts * hid * hid, 9 * hid, chan * hid)

    def root(v):
        v = jnp.full((8, LANES), v, F32)
        r = lax.rsqrt(v)
        r = r * (1.5 - 0.5 * v * r * r)
        return (v * r)[0, 0]

    def squares(at, count):
        acc = jnp.zeros((8, LANES), F32)
        for half in range(2):

            def body(n, acc, half=half):
                v = g[half, pl.ds(at + n * 128, 128), :].astype(F32)
                return acc + jnp.sum((v * v).reshape(16, 8, LANES), axis=0)

            acc = lax.fori_loop(0, count // 128, body, acc)
        return jnp.sum(acc)

    def set_scale(j, total):
        scale[j] = 1.0 / root(total / sizes[j] + EPS)
        scale[5 + j] = RATE * root(sums[j] / sizes[j] + EPS)

    @pl.when(step == 0)
    def _():
        g[core] = own_ref[...]
        g[1 - core] = other_ref[...]
        small[...] = small_ref[...].astype(F32)
        v = small[0 : 9 * cb1, :]
        set_scale(0, jnp.sum(v * v))
        v = small[9 * cb1 : 9 * (cb1 + cb2), :]
        set_scale(3, jnp.sum(v * v))
        set_scale(1, squares(p1_at, p1_rows // 2))
        set_scale(2, squares(0, 2 * st_rows))
        set_scale(4, squares(p2_at, p2_rows // 2))
        for j, first, blocks, w, new, out in (
            (0, 0, cb1, k1_ref, nk1_ref, sk1_ref),
            (3, 9 * cb1, cb2, k2_ref, nk2_ref, sk2_ref),
        ):
            for c in range(blocks):
                cut = slice(c * LANES, (c + 1) * LANES)
                for r in range(3):
                    at = first + 9 * c + 3 * r
                    normed = small[at : at + 3, :] * scale[j]
                    out[r, :, cut] = normed
                    new[r, :, cut] = w[r, :, cut] - scale[5 + j] * normed
        for c in range(cb2):
            cut = slice(c * LANES, (c + 1) * LANES)
            at = p1_at + (c % (cb2 // 2)) * chan
            normed = g[2 * c // cb2, at : at + chan, :].astype(F32) * scale[1]
            sp1_ref[:, cut] = normed
            np1_ref[:, cut] = p1_ref[:, cut] - scale[6] * normed
        for c in range(cb1):
            cut = slice(c * LANES, (c + 1) * LANES)
            at = p2_at + (c % (cb1 // 2)) * hid
            normed = g[2 * c // cb1, at : at + hid, :].astype(F32) * scale[4]
            sp2_ref[:, cut] = normed
            np2_ref[:, cut] = p2_ref[:, cut] - scale[9] * normed

    per = hid // block
    ph = step // per
    for c in range(cb2):
        cut = slice(c * LANES, (c + 1) * LANES)
        at = (ph % 2) * st_rows + c * hid + (step % per) * block
        normed = g[ph // 2, pl.ds(at, block), :].astype(F32) * scale[2]
        sst_ref[0, :, cut] = normed
        nst_ref[0, :, cut] = st_ref[0, :, cut] - scale[7] * normed


def update(where, sums, small, own, other, k1, p1, taps, k2, p2):
    hid = taps.shape[1]
    block = hid // 2
    per = hid // block

    def whole(w):
        return pl.BlockSpec(w.shape, lambda n: (0,) * w.ndim)

    st = pl.BlockSpec((1, block, hid), lambda n: (n // per, n % per, 0))
    specs = [whole(k1), whole(p1), st, whole(k2), whole(p2)]
    shapes = [jax.ShapeDtypeStruct(w.shape, F32) for w in (k1, p1, taps, k2, p2)]
    return pl.pallas_call(
        update_kernel,
        grid=(4 * per,),
        out_shape=shapes + shapes,
        in_specs=[smem(), smem(), whole(small)] + [whole(own), whole(other)] + specs,
        out_specs=specs + specs,
        scratch_shapes=[
            pltpu.VMEM((2,) + own.shape, BF16),
            pltpu.VMEM((SMALL, LANES), F32),
            pltpu.SMEM((10,), F32),
        ],
        compiler_params=pltpu.CompilerParams(vmem_limit_bytes=40 * 1024 * 1024),
    )(where, sums, small, own, other, k1, p1, taps, k2, p2)


def shift(block, down, right):
    n, m = lax.axis_size("ty"), lax.axis_size("tx")
    pairs = [
        (i * m + j, (i + down) * m + j + right)
        for i in range(n)
        for j in range(m)
        if 0 <= i + down < n and 0 <= j + right < m
    ]
    return lax.ppermute(block, ("ty", "tx"), pairs)


class Ring:
    def __init__(self, names):
        sizes = {"x": lax.axis_size("tx") // 2, "y": lax.axis_size("rep"), "z": lax.axis_size("ty")}
        place = {"x": lax.axis_index("tx") // 2, "y": lax.axis_index("rep"), "z": lax.axis_index("ty")}
        self.names, self.sizes = names, sizes
        self.count = sizes[names[0]]
        assert sizes[names[1]] == self.count
        self.me = jnp.where(lax.axis_index("tx") % 2 == 0, place[names[0]], place[names[1]])

    def send(self, block, step):
        sizes = self.sizes

        def flat(at, core):
            return ((at["y"] * sizes["z"] + at["z"]) * sizes["x"] + at["x"]) * 2 + core

        pairs = []
        for i in range(sizes["y"]):
            for j in range(sizes["z"]):
                for k in range(sizes["x"]):
                    for core in range(2):
                        at = {"y": i, "z": j, "x": k}
                        to = dict(at)
                        name = self.names[core]
                        to[name] = (at[name] + step) % sizes[name]
                        pairs.append((flat(at, core), flat(to, core)))
        return lax.ppermute(block, ("rep", "ty", "tx"), pairs)

    def scatter(self, block, extra):
        n = self.count
        shares = block.reshape((n, -1, LANES))
        share = lax.dynamic_index_in_dim(shares, self.me, 0, False)
        cut = share.shape[0]
        got = []
        for d in range(1, n):
            out = lax.dynamic_index_in_dim(shares, (self.me + d) % n, 0, False)
            got.append(self.send(jnp.concatenate([out, extra], axis=0), d))
        total = sum([g[:cut].astype(F32) for g in got], share.astype(F32))
        extra = sum([g[cut:].astype(F32) for g in got], extra.astype(F32))
        return total.astype(BF16), extra.astype(BF16)

    def gather(self, share):
        n = self.count
        out = jnp.zeros((n,) + share.shape, share.dtype)
        out = lax.dynamic_update_index_in_dim(out, share, self.me, 0)
        for d in range(1, n):
            got = self.send(share, d)
            out = lax.dynamic_update_index_in_dim(out, got, (self.me + n - d) % n, 0)
        return out.reshape(-1, LANES)


def reduced(keep, send):
    rings = (Ring("yx"), Ring("xy"), Ring("zz"))
    cores = [(i, i ^ 1) for i in range(lax.axis_size("tx"))]
    got = lax.ppermute(send, "tx", cores)
    both = (keep.astype(F32) + got.astype(F32)).astype(BF16)
    share, small = both[: both.shape[0] - SMALL], both[both.shape[0] - SMALL :]
    for ring in rings:
        share, small = ring.scatter(share, small)
    for ring in rings[::-1]:
        share = ring.gather(share)
    return small, share, lax.ppermute(share, "tx", cores)


def per_device(inputs, targets, kern_one, point_one, coarsening_taps, kern_two, point_two):
    x = jnp.transpose(inputs[0], (1, 2, 0))
    t = jnp.transpose(targets[0], (1, 2, 0))
    rows, cols, chan = x.shape
    hid = point_one.shape[1]
    hr, hc = rows // 2, cols // 2
    up = jnp.concatenate([x[:ROWS], t[:2]], axis=0)
    down = jnp.concatenate([x[rows - ROWS :], t[rows - 2 :]], axis=0)
    top, bot = shift(down, 1, 0), shift(up, -1, 0)
    taps = coarsening_taps.reshape(4, hid, hid)
    weights = (kern_one, point_one, taps, kern_two, point_two)
    weights, top, bot = lax.optimization_barrier((weights, top, bot))
    low_one, low_taps, low_two, sums = prepared(*weights)

    def edge(cut):
        e = jnp.concatenate([top[:ROWS, cut], x[:, cut], bot[:ROWS, cut]], axis=0)
        z = jnp.zeros((ROWS - 2,) + e.shape[1:], BF16)
        f = jnp.concatenate([z, top[ROWS:, cut], t[:, cut], bot[ROWS:, cut], z], axis=0)
        return e, f

    e, f = edge(slice(0, 8))
    right = shift(jnp.concatenate([e[:, :5], f[:, :2], e[:, 7:]], axis=1), 0, -1)
    e, f = edge(slice(cols - 8, cols))
    left = shift(jnp.concatenate([e[:, :1], f[:, 6:], e[:, 3:]], axis=1), 0, 1)
    halos = [top, bot, right, left]
    ty, tx = lax.axis_index("ty"), lax.axis_index("tx")
    big = 1 << 20
    limits = jnp.stack(
        [
            jnp.where(ty == 0, 0, -big),
            jnp.where(ty == lax.axis_size("ty") - 1, hr, big),
            jnp.where(tx == 0, 0, -big),
            jnp.where(tx == lax.axis_size("tx") - 1, hc, big),
            tx % 2,
        ]
    ).astype(jnp.int32)
    pred, keep, send = tile_step(
        limits, x, t, halos, kern_one, low_one, low_taps, kern_two, low_two
    )
    small, own, other = reduced(keep, send)
    outs = update((tx % 2)[None].astype(jnp.int32), sums, small, own, other, *weights)
    outs = [o.reshape(coarsening_taps.shape) if o.shape == taps.shape else o for o in outs]
    return (jnp.transpose(pred, (2, 0, 1))[None], *outs)


def solution(mesh):
    tile = P("rep", None, "ty", "tx")
    return jax.shard_map(
        per_device,
        mesh=mesh,
        in_specs=(tile, tile, P(), P(), P(), P(), P()),
        out_specs=(tile,) + (P(),) * 10,
        check_vma=False,
    )
```

```python
import jax
import jax.numpy as jnp
from jax import lax
from jax.experimental import pallas as pl
from jax.experimental.pallas import tpu as pltpu
from jax.sharding import PartitionSpec as P

EPS = 1e-05
RATE = 0.05
F32 = jnp.float32
BF16 = jnp.bfloat16
LANES = 128
HALO = 4
ROWS = 6
SMALL = 64


def mm(a, b):
    return jnp.dot(a, b, preferred_element_type=F32)


def mm_t(a, b):
    return lax.dot_general(a, b, (((1,), (1,)), ((), ())), preferred_element_type=F32)


def t_mm(a, b):
    return lax.dot_general(a, b, (((0,), (0,)), ((), ())), preferred_element_type=F32)


def sigmoid(v):
    return 0.5 + 0.5 * jnp.tanh(0.5 * v)


def tile_kernel(
    limits,
    x_ref,
    t_hbm,
    top_ref,
    bot_ref,
    right_ref,
    left_ref,
    right_ends,
    left_ends,
    k1_ref,
    p1_full,
    taps_hbm,
    k2_ref,
    p2_full,
    pred_hbm,
    keep_ref,
    send_ref,
    sums_ref,
    t_ref,
    taps_full,
    p1_ref,
    taps_ref,
    p2_ref,
    pred_ref,
    sems,
    xf,
    tf,
    d2,
    out_e,
    out_own,
    pre_own,
    co,
    sl,
    cout,
    up,
    ot_own,
    ce_own,
    bc,
    bp,
    small,
):
    rows, cols, chan = x_ref.shape
    hid = k2_ref.shape[2]
    hr, hc = rows // 2, cols // 2
    slots = hc + 2 * HALO
    cb1, cb2 = chan // LANES, hid // LANES
    er = hr + 4
    fr = hr + 2

    def lanes(c):
        return slice(c * LANES, (c + 1) * LANES)

    core = limits[4]
    st_rows, p1_rows, p2_rows = hid * (hid // LANES), chan * (hid // LANES), hid * (chan // LANES)
    p1_at = 2 * st_rows
    p2_at = p1_at + p1_rows // 2
    small_at = p2_at + p2_rows // 2

    def emit(half, at, value):
        value = value.astype(BF16)

        @pl.when(core == half)
        def _():
            keep_ref[at : at + value.shape[0], :] = value

        @pl.when(core != half)
        def _():
            send_ref[at : at + value.shape[0], :] = value

    copies = [
        pltpu.make_async_copy(t_hbm, t_ref, sems.at[0]),
        pltpu.make_async_copy(taps_hbm, taps_full, sems.at[1]),
        pltpu.make_async_copy(pred_ref, pred_hbm, sems.at[2]),
    ]
    copies[0].start()
    copies[1].start()
    small[...] = jnp.zeros_like(small)
    p1_ref[...] = p1_full[...].astype(BF16)
    p2_ref[...] = p2_full[...].astype(BF16)

    def put(row, count, block, c):
        xf[c, pl.ds(row, count), 8 : 8 + cols, :] = block.astype(F32)

    for c in range(cb1):
        put(0, ROWS, top_ref[0:ROWS, :, lanes(c)], c)
        put(rows + ROWS, ROWS, bot_ref[0:ROWS, :, lanes(c)], c)

    step = 12

    @pl.loop(0, rows // step)
    def _(n):
        for c in range(cb1):
            put(ROWS + n * step, step, x_ref[pl.ds(n * step, step), :, lanes(c)], c)

    def put_sides(row, count, right, left, c):
        at = pl.ds(row, count)
        right, left = right.astype(F32), left.astype(F32)
        xf[c, at, 8 + cols : 16 + cols, :] = right
        xf[c, at, 16 + cols : 24 + cols, :] = left
        xf[c, at, 7:8, :] = left[:, 7:8, :]
        xf[c, at, 24 + cols : 25 + cols, :] = xf[c, at, 8:9, :]

    for c in range(cb1):
        put_sides(0, ROWS, right_ends[0:ROWS, :, lanes(c)], left_ends[0:ROWS, :, lanes(c)], c)
        cut = (slice(ROWS + 2, 2 * ROWS + 2), slice(None), lanes(c))
        put_sides(rows + ROWS, ROWS, right_ends[cut], left_ends[cut], c)

    @pl.loop(0, rows // step)
    def _(n):
        at = pl.ds(n * step, step)
        for c in range(cb1):
            put_sides(ROWS + n * step, step, right_ref[at, :, lanes(c)], left_ref[at, :, lanes(c)], c)

    copies[0].wait()

    def diff(first, count, block, right, left, ends, c):
        at = pl.ds(2 * first + ROWS, 2 * count)
        rcol, lcol = (cols, cols + 8) if ends else (cols - 5, cols + 13)
        tf[c, 0 : 2 * count, rcol : rcol + 8, :] = right.astype(F32)
        tf[c, 0 : 2 * count, lcol : lcol + 8, :] = left.astype(F32)
        tf[c, 0 : 2 * count, 0:cols, :] = block.astype(F32)
        both = xf[c, at, 8 : 24 + cols, :] - tf[c, 0 : 2 * count, 0 : 16 + cols, :]
        both = both.reshape(count, 2, 16 + cols, LANES)
        tf[c, 0:count, 0 : 16 + cols, :] = both[:, 0] + both[:, 1]
        even = tf[c, 0:count, pl.ds(0, slots, stride=2), :]
        odd = tf[c, 0:count, pl.ds(1, slots, stride=2), :]
        d2[c, pl.ds(first + 1, count), :, :] = (even + odd) * 0.25

    for c in range(cb1):
        own = (slice(ROWS, ROWS + 2), slice(None), lanes(c))
        diff(-1, 1, top_ref[own], right_ends[own], left_ends[own], True, c)
        cut = (slice(2 * ROWS + 2, 2 * ROWS + 4), slice(None), lanes(c))
        diff(hr, 1, bot_ref[own], right_ends[cut], left_ends[cut], True, c)

    @pl.loop(0, hr // 4)
    def _(n):
        for c in range(cb1):
            cut = (pl.ds(n * 8, 8), slice(None), lanes(c))
            diff(n * 4, 4, t_ref[cut], right_ref[cut], left_ref[cut], False, c)

    take = 4

    @pl.loop(0, er // take)
    def _(n):
        pres = []
        for c in range(cb1):
            per = [[None] * take for _ in range(4)]
            for i in range(take):
                e = 2 * (n * take + i) + ROWS - 4
                for r in range(2):
                    total = [None, None]
                    for a in range(3):
                        at = e + r + a - 1
                        col = [xf[c, at, pl.ds(7 + o, slots, stride=2), :] for o in range(4)]
                        for q in range(2):
                            for b in range(3):
                                term = k1_ref[a, b : b + 1, lanes(c)] * col[q + b]
                                total[q] = term if total[q] is None else total[q] + term
                    for q in range(2):
                        per[2 * r + q][i] = total[q]
            pres.append([jnp.stack(p) for p in per])
        for ph in range(4):
            for c in range(cb1):
                own = pres[c][ph][:, 0:hc, :].reshape(take * hc, LANES).astype(BF16)
                pre_own[ph, pl.ds(n * (take * hc), take * hc), lanes(c)] = own
        low = [
            jnp.concatenate(
                [pres[c][ph].reshape(take * slots, LANES).astype(BF16) for c in range(cb1)], axis=1
            )
            for ph in range(4)
        ]
        for ph in range(4):
            act = mm(low[ph], p1_ref[...])
            out = act * sigmoid(act)
            out_e[ph, pl.ds(n * (take * slots), take * slots), :] = out.astype(BF16)
            own = out.reshape(take, slots, hid)[:, 0:hc, :].reshape(take * hc, hid)
            out_own[ph, pl.ds(n * (take * hc), take * hc), :] = own.astype(BF16)

    row_lo, row_hi, col_lo, col_hi = limits[0], limits[1], limits[2], limits[3]

    def inside(first, count):
        row = lax.broadcasted_iota(jnp.int32, (count, slots, LANES), 0) + first
        slot = lax.broadcasted_iota(jnp.int32, (count, slots, LANES), 1)
        col = jnp.where(slot < hc + HALO, slot, slot - slots)
        ok = (row >= row_lo) & (row < row_hi) & (col >= col_lo) & (col < col_hi)
        return jnp.where(ok, 1.0, 0.0).astype(F32)

    def wrapped(ref, c, at, value):
        ref[c, at, 8 : 8 + slots, :] = value
        ref[c, at, 7:8, :] = value[:, slots - 1 : slots, :]
        ref[c, at, 8 + slots : 9 + slots, :] = value[:, 0:1, :]

    copies[1].wait()

    piece = 128

    def cast(n, acc):
        ph, at = n // (hid // piece), pl.ds(n % (hid // piece) * piece, piece)
        w = taps_full[ph, at, :]
        taps_ref[ph, at, :] = w.astype(BF16)
        return acc + jnp.sum((w * w).reshape(piece // 8, 8, hid), axis=0)

    sums_ref[2] = jnp.sum(lax.fori_loop(0, 4 * hid // piece, cast, jnp.zeros((8, hid), F32)))
    for j, ref in ((0, k1_ref), (1, p1_full), (3, k2_ref), (4, p2_full)):
        sums_ref[j] = jnp.sum(ref[...] * ref[...])
    half = er // 2

    @pl.loop(0, 2)
    def _(n):
        ok = inside(n * half - 2, half)
        for m in range(hid // 256):
            acc = None
            for ph in range(4):
                term = mm(
                    out_e[ph, pl.ds(n * (half * slots), half * slots), :],
                    taps_ref[ph, :, m * 256 : (m + 1) * 256],
                )
                acc = term if acc is None else acc + term
            acc = acc.astype(BF16).astype(F32).reshape(half, slots, 256)
            for j in range(2):
                wrapped(co, 2 * m + j, pl.ds(n * half, half), acc[:, :, lanes(j)] * ok)

    part = 10

    @pl.loop(0, fr // part)
    def _(n):
        pre = []
        for c in range(cb2):
            total = None
            for a in range(3):
                for b in range(3):
                    at = pl.ds(n * part + a, part)
                    term = k2_ref[a, b : b + 1, lanes(c)] * co[c, at, 7 + b : 7 + b + slots, :]
                    total = term if total is None else total + term
            pre.append(total.reshape(part * slots, LANES))
        gate = [sigmoid(p) for p in pre]
        out = [p * g for p, g in zip(pre, gate)]
        low = jnp.concatenate([o.astype(BF16) for o in out], axis=1)
        for c in range(cb2):
            own = out[c].reshape(part, slots, LANES)[:, 0:hc, :].reshape(part * hc, LANES)
            ot_own[pl.ds(n * (part * hc), part * hc), lanes(c)] = own.astype(BF16)
        back = mm(low, p2_ref[...]).reshape(part, slots, chan)
        errs = []
        for c in range(cb1):
            own = back[:, :, lanes(c)]
            cout[c, pl.ds(n * part, part), :, :] = own[:, 0:hc, :]
            err = own + d2[c, pl.ds(n * part, part), :, :]
            errs.append(err.reshape(part * slots, LANES).astype(BF16))
            ce_own[pl.ds(n * (part * hc), part * hc), lanes(c)] = (
                err[:, 0:hc, :].reshape(part * hc, LANES).astype(BF16)
            )
        err = jnp.concatenate(errs, axis=1)
        ok = inside(n * part - 1, part)
        back_two = mm_t(err, p2_ref[...])
        for c in range(cb2):
            slope = back_two[:, lanes(c)] * (gate[c] * (1.0 + pre[c] * (1.0 - gate[c])))
            slope = slope.astype(BF16).astype(F32).reshape(part, slots, LANES) * ok
            wrapped(sl, c, pl.ds(n * part, part), slope)

    gp2 = t_mm(ot_own[hc : hc + hr * hc, :], ce_own[hc : hc + hr * hc, :])
    for c in range(cb1):
        emit(2 * c // cb1, p2_at + (c % (cb1 // 2)) * hid, gp2[:, lanes(c)])

    @pl.loop(0, hr // 4)
    def _(n):
        for c in range(cb1):
            block = cout[c, pl.ds(n * 4 + 1, 4), :, :]
            up[c, :, pl.ds(0, hc, stride=2), :] = block
            up[c, :, pl.ds(1, hc, stride=2), :] = block
            wide = up[c, :, :, :]
            wide = jnp.stack([wide, wide], axis=1).reshape(8, cols, LANES)
            fine = xf[c, pl.ds(n * 8 + ROWS, 8), 8 : 8 + cols, :]
            pred_ref[pl.ds(n * 8, 8), :, lanes(c)] = (wide + fine).astype(BF16)

    copies[2].start()

    for c in range(cb2):
        def body(n, acc, c=c):
            acc = list(acc)
            for i in range(2):
                row = n * 2 + i
                slope = sl[c, row + 1, 8 : 8 + hc, :]
                total = None
                for a in range(3):
                    for b in range(3):
                        p = slope * co[c, row + 1 + a, 7 + b : 7 + b + hc, :]
                        acc[3 * a + b] = acc[3 * a + b] + (p[0:8] + p[8:16])
                        term = k2_ref[a, b : b + 1, lanes(c)] * sl[c, row + 2 - a, 9 - b : 9 - b + hc, :]
                        total = term if total is None else total + term
                bc[pl.ds(row * hc, hc), lanes(c)] = total.astype(BF16)
            return tuple(acc)

        acc = lax.fori_loop(0, hr // 2, body, tuple(jnp.zeros((8, LANES), F32) for _ in range(9)))
        for j in range(9):
            at = 9 * (cb1 + c) + j
            small[at : at + 1, :] = jnp.sum(acc[j], axis=0, keepdims=True)

    skip = 2 * hc
    own_rows = slice(skip, skip + hr * hc)
    for ph in range(4):
        gst = t_mm(out_own[ph, own_rows, :], bc[...])
        for c in range(cb2):
            emit(ph // 2, (ph % 2) * st_rows + c * hid, gst[:, lanes(c)])
        back = mm_t(bc[...], taps_ref[ph])
        act = mm(pre_own[ph, own_rows, :], p1_ref[...])
        gate = sigmoid(act)
        slope = (back * (gate * (1.0 + act * (1.0 - gate)))).astype(BF16)
        term = t_mm(pre_own[ph, own_rows, :], slope)
        gp1 = term if ph == 0 else gp1 + term
        back_pre = mm_t(slope, p1_ref[...])
        for c in range(cb1):
            bp[ph, c] = back_pre[:, lanes(c)].reshape(hr, hc, LANES)

    for c in range(cb2):
        emit(2 * c // cb2, p1_at + (c % (cb2 // 2)) * chan, gp1[:, lanes(c)])

    for c in range(cb1):

        def body(n, acc, c=c):
            acc = list(acc)
            grads = [[bp[ph, c, 2 * n + i] for ph in range(4)] for i in range(2)]
            for s in range(6):
                e = 4 * n + ROWS + s - 1
                col = [xf[c, e, pl.ds(7 + o, hc, stride=2), :] for o in range(4)]
                for i in range(2):
                    for r in range(2):
                        a = s - 2 * i - r
                        if 0 <= a < 3:
                            for q in range(2):
                                for b in range(3):
                                    p = grads[i][2 * r + q] * col[q + b]
                                    acc[3 * a + b] = acc[3 * a + b] + (p[0:8] + p[8:16])
            return tuple(acc)

        acc = lax.fori_loop(0, hr // 2, body, tuple(jnp.zeros((8, LANES), F32) for _ in range(9)))
        for j in range(9):
            at = 9 * c + j
            small[at : at + 1, :] = jnp.sum(acc[j], axis=0, keepdims=True)


    copies[2].wait()
    for ref in (keep_ref, send_ref):
        ref[small_at : small_at + SMALL, :] = small[...].astype(BF16)


def vmem():
    return pl.BlockSpec(memory_space=pltpu.VMEM)


def hbm():
    return pl.BlockSpec(memory_space=pl.ANY)


def smem():
    return pl.BlockSpec(memory_space=pltpu.SMEM)


def tile_step(limits, x, t, halos, k1, p1, taps, k2, p2):
    rows, cols, chan = x.shape
    hid = k2.shape[2]
    hr, hc = rows // 2, cols // 2
    slots = hc + 2 * HALO
    cb1, cb2 = chan // LANES, hid // LANES
    grads = (p1.size + taps.size + p2.size) // (2 * LANES) + SMALL
    return pl.pallas_call(
        tile_kernel,
        out_shape=(
            jax.ShapeDtypeStruct(x.shape, BF16),
            jax.ShapeDtypeStruct((grads, LANES), BF16),
            jax.ShapeDtypeStruct((grads, LANES), BF16),
            jax.ShapeDtypeStruct((5,), F32),
        ),
        in_specs=[smem(), vmem(), hbm()]
        + [vmem()] * (len(halos) + 2)
        + [hbm(), vmem(), vmem()],
        out_specs=[hbm(), vmem(), vmem(), smem()],
        scratch_shapes=[
            pltpu.VMEM(t.shape, BF16),
            pltpu.VMEM(taps.shape, F32),
            pltpu.VMEM(p1.shape, BF16),
            pltpu.VMEM(taps.shape, BF16),
            pltpu.VMEM(p2.shape, BF16),
            pltpu.VMEM(x.shape, BF16),
            pltpu.SemaphoreType.DMA((3,)),
            pltpu.VMEM((cb1, rows + 2 * ROWS, cols + 32, LANES), F32),
            pltpu.VMEM((cb1, 8, cols + 32, LANES), F32),
            pltpu.VMEM((cb1, hr + 2, slots, LANES), F32),
            pltpu.VMEM((4, (hr + 4) * slots, hid), BF16),
            pltpu.VMEM((4, (hr + 4) * hc, hid), BF16),
            pltpu.VMEM((4, (hr + 4) * hc, chan), BF16),
            pltpu.VMEM((cb2, hr + 4, slots + 16, LANES), F32),
            pltpu.VMEM((cb2, hr + 2, slots + 16, LANES), F32),
            pltpu.VMEM((cb1, hr + 2, hc, LANES), F32),
            pltpu.VMEM((cb1, 4, cols, LANES), F32),
            pltpu.VMEM(((hr + 2) * hc, hid), BF16),
            pltpu.VMEM(((hr + 2) * hc, chan), BF16),
            pltpu.VMEM((hr * hc, hid), BF16),
            pltpu.VMEM((4, cb1, hr, hc, LANES), F32),
            pltpu.VMEM((SMALL, LANES), F32),
        ],
        compiler_params=pltpu.CompilerParams(vmem_limit_bytes=63 * 1024 * 1024),
        cost_estimate=pl.CostEstimate(flops=9_000_000_000, bytes_accessed=20_000_000, transcendentals=0),
    )(limits, x, t, *halos, k1, p1, taps, k2, p2)


def edges_kernel(xt, tt, xb, tb, xl, tl, xr, tr, up, down, ahead, back):
    up[...] = jnp.concatenate([xt[0:ROWS], tt[0:2]], axis=0)
    down[...] = jnp.concatenate([xb[8 - ROWS : 8], tb[6:8]], axis=0)
    col = lax.broadcasted_iota(jnp.int32, ahead.shape, 1)
    x, t = xl[...].astype(F32)[:, 0:8], tl[...].astype(F32)[:, 0:8]
    ahead[...] = jnp.where((col >= 5) & (col < 7), pltpu.roll(t, 5, 1), x).astype(BF16)
    x, t = xr[...].astype(F32)[:, 8:16], tr[...].astype(F32)[:, 8:16]
    back[...] = jnp.where((col >= 1) & (col < 3), pltpu.roll(t, 3, 1), x).astype(BF16)


def edges(x, t):
    rows, cols, chan = x.shape
    specs = [
        pl.BlockSpec((8, cols, chan), lambda n: (0, 0, 0)),
        pl.BlockSpec((8, cols, chan), lambda n: (rows // 8 - 1, 0, 0)),
        pl.BlockSpec((rows, 16, chan), lambda n: (0, 0, 0)),
        pl.BlockSpec((rows, 16, chan), lambda n: (0, cols // 16 - 1, 0)),
    ]
    shapes = [(ROWS + 2, cols, chan)] * 2 + [(rows, 8, chan)] * 2
    return pl.pallas_call(
        edges_kernel,
        grid=(1,),
        out_shape=[jax.ShapeDtypeStruct(s, BF16) for s in shapes],
        in_specs=[s for s in specs for _ in range(2)],
        out_specs=[pl.BlockSpec(s, lambda n: (0, 0, 0)) for s in shapes],
    )(*[x, t] * 4)


def update_kernel(
    where,
    sums,
    small_ref,
    own_ref,
    other_ref,
    *refs,
):
    (
        k1_ref,
        p1_ref,
        st_hbm,
        k2_ref,
        p2_ref,
        nk1_ref,
        np1_ref,
        nst_ref,
        nk2_ref,
        np2_ref,
        sk1_ref,
        sp1_ref,
        sst_ref,
        sk2_ref,
        sp2_ref,
        g,
        small,
        scale,
        st_ref,
        sems,
    ) = refs
    chan, hid = p1_ref.shape
    cb1, cb2 = chan // LANES, hid // LANES
    parts, block = 4, st_ref.shape[1]
    step = pl.program_id(0)
    per = hid // block

    def fetch(n):
        at = pl.ds(n % per * block, block)
        return pltpu.make_async_copy(st_hbm.at[n // per, at, :], st_ref.at[n], sems.at[n])

    core = where[0]
    st_rows, p1_rows, p2_rows = hid * cb2, chan * cb2, hid * cb1
    p1_at = 2 * st_rows
    p2_at = p1_at + p1_rows // 2
    small_at = p2_at + p2_rows // 2
    sizes = (9 * chan, chan * hid, parts * hid * hid, 9 * hid, chan * hid)

    def root(v):
        v = jnp.full((8, LANES), v, F32)
        r = lax.rsqrt(v)
        r = r * (1.5 - 0.5 * v * r * r)
        return (v * r)[0, 0]

    def squares(at, count):
        acc = jnp.zeros((8, LANES), F32)
        for half in range(2):

            def body(n, acc, half=half):
                v = g[half, pl.ds(at + n * 128, 128), :].astype(F32)
                return acc + jnp.sum((v * v).reshape(16, 8, LANES), axis=0)

            acc = lax.fori_loop(0, count // 128, body, acc)
        return jnp.sum(acc)

    def set_scale(j, total):
        scale[j] = 1.0 / root(total / sizes[j] + EPS)
        scale[5 + j] = RATE * root(sums[j] / sizes[j] + EPS)

    @pl.when(step == 0)
    def _():
        for n in range(parts * per):
            fetch(n).start()
        g[core] = own_ref[...]
        g[1 - core] = other_ref[...]
        small[...] = small_ref[...].astype(F32)
        v = small[0 : 9 * cb1, :]
        set_scale(0, jnp.sum(v * v))
        v = small[9 * cb1 : 9 * (cb1 + cb2), :]
        set_scale(3, jnp.sum(v * v))
        set_scale(1, squares(p1_at, p1_rows // 2))
        set_scale(2, squares(0, 2 * st_rows))
        set_scale(4, squares(p2_at, p2_rows // 2))
        for j, first, blocks, w, new, out in (
            (0, 0, cb1, k1_ref, nk1_ref, sk1_ref),
            (3, 9 * cb1, cb2, k2_ref, nk2_ref, sk2_ref),
        ):
            for c in range(blocks):
                cut = slice(c * LANES, (c + 1) * LANES)
                for r in range(3):
                    at = first + 9 * c + 3 * r
                    normed = small[at : at + 3, :] * scale[j]
                    out[r, :, cut] = normed
                    new[r, :, cut] = w[r, :, cut] - scale[5 + j] * normed
        for c in range(cb2):
            cut = slice(c * LANES, (c + 1) * LANES)
            at = p1_at + (c % (cb2 // 2)) * chan
            normed = g[2 * c // cb2, at : at + chan, :].astype(F32) * scale[1]
            sp1_ref[:, cut] = normed
            np1_ref[:, cut] = p1_ref[:, cut] - scale[6] * normed
        for c in range(cb1):
            cut = slice(c * LANES, (c + 1) * LANES)
            at = p2_at + (c % (cb1 // 2)) * hid
            normed = g[2 * c // cb1, at : at + hid, :].astype(F32) * scale[4]
            sp2_ref[:, cut] = normed
            np2_ref[:, cut] = p2_ref[:, cut] - scale[9] * normed

    fetch(step).wait()
    ph = step // per
    for c in range(cb2):
        cut = slice(c * LANES, (c + 1) * LANES)
        at = (ph % 2) * st_rows + c * hid + (step % per) * block
        normed = g[ph // 2, pl.ds(at, block), :].astype(F32) * scale[2]
        sst_ref[0, :, cut] = normed
        nst_ref[0, :, cut] = st_ref[step, :, cut] - scale[7] * normed


def update(where, sums, small, own, other, k1, p1, taps, k2, p2):
    hid = taps.shape[1]
    block = hid // 2
    per = hid // block

    def whole(w):
        return pl.BlockSpec(w.shape, lambda n: (0,) * w.ndim)

    st = pl.BlockSpec((1, block, hid), lambda n: (n // per, n % per, 0))
    specs = [whole(k1), whole(p1), st, whole(k2), whole(p2)]
    shapes = [jax.ShapeDtypeStruct(w.shape, F32) for w in (k1, p1, taps, k2, p2)]
    return pl.pallas_call(
        update_kernel,
        grid=(4 * per,),
        out_shape=shapes + shapes,
        in_specs=[smem(), smem(), whole(small)] + [whole(own), whole(other)]
        + specs[:2]
        + [hbm()]
        + specs[3:],
        out_specs=specs + specs,
        scratch_shapes=[
            pltpu.VMEM((2,) + own.shape, BF16),
            pltpu.VMEM((SMALL, LANES), F32),
            pltpu.SMEM((10,), F32),
            pltpu.VMEM((4 * per, block, hid), F32),
            pltpu.SemaphoreType.DMA((4 * per,)),
        ],
        compiler_params=pltpu.CompilerParams(vmem_limit_bytes=40 * 1024 * 1024),
    )(where, sums, small, own, other, k1, p1, taps, k2, p2)


def shift(block, down, right):
    n, m = lax.axis_size("ty"), lax.axis_size("tx")
    pairs = [
        (i * m + j, (i + down) * m + j + right)
        for i in range(n)
        for j in range(m)
        if 0 <= i + down < n and 0 <= j + right < m
    ]
    return lax.ppermute(block, ("ty", "tx"), pairs)


class Ring:
    def __init__(self, names):
        sizes = {"x": lax.axis_size("tx") // 2, "y": lax.axis_size("rep"), "z": lax.axis_size("ty")}
        place = {"x": lax.axis_index("tx") // 2, "y": lax.axis_index("rep"), "z": lax.axis_index("ty")}
        self.names, self.sizes = names, sizes
        self.count = sizes[names[0]]
        assert sizes[names[1]] == self.count
        self.me = jnp.where(lax.axis_index("tx") % 2 == 0, place[names[0]], place[names[1]])

    def send(self, block, step):
        sizes = self.sizes

        def flat(at, core):
            return ((at["y"] * sizes["z"] + at["z"]) * sizes["x"] + at["x"]) * 2 + core

        pairs = []
        for i in range(sizes["y"]):
            for j in range(sizes["z"]):
                for k in range(sizes["x"]):
                    for core in range(2):
                        at = {"y": i, "z": j, "x": k}
                        to = dict(at)
                        name = self.names[core]
                        to[name] = (at[name] + step) % sizes[name]
                        pairs.append((flat(at, core), flat(to, core)))
        return lax.ppermute(block, ("rep", "ty", "tx"), pairs)

    def scatter(self, block, extra):
        n = self.count
        shares = block.reshape((n, -1, LANES))
        share = lax.dynamic_index_in_dim(shares, self.me, 0, False)
        cut = share.shape[0]
        got = []
        for d in range(1, n):
            out = lax.dynamic_index_in_dim(shares, (self.me + d) % n, 0, False)
            got.append(self.send(jnp.concatenate([out, extra], axis=0), d))
        total = sum([g[:cut].astype(F32) for g in got], share.astype(F32))
        return total.astype(BF16), self.added([extra] + [g[cut:] for g in got])

    def added(self, parts):
        n = self.count
        parts = jnp.stack(parts)
        total = None
        for k in range(n):
            part = lax.dynamic_index_in_dim(parts, (self.me + n - k) % n, 0, False).astype(F32)
            total = part if total is None else total + part
        return total.astype(BF16)

    def reduce(self, block):
        return self.added([block] + [self.send(block, d) for d in range(1, self.count)])

    def gather(self, share):
        n = self.count
        out = jnp.zeros((n,) + share.shape, share.dtype)
        out = lax.dynamic_update_index_in_dim(out, share, self.me, 0)
        for d in range(1, n):
            got = self.send(share, d)
            out = lax.dynamic_update_index_in_dim(out, got, (self.me + n - d) % n, 0)
        return out.reshape(-1, LANES)


def reduced(keep, send):
    rings = (Ring("yx"), Ring("xy"))
    cores = [(i, i ^ 1) for i in range(lax.axis_size("tx"))]
    got = lax.ppermute(send, "tx", cores)
    both = (keep.astype(F32) + got.astype(F32)).astype(BF16)
    share, small = both[: both.shape[0] - SMALL], both[both.shape[0] - SMALL :]
    for ring in rings:
        share, small = ring.scatter(share, small)
    both = Ring("zz").reduce(jnp.concatenate([share, small], axis=0))
    share, small = both[: share.shape[0]], both[share.shape[0] :]
    for ring in rings[::-1]:
        share = ring.gather(share)
    return small, share, lax.ppermute(share, "tx", cores)


def per_device(inputs, targets, kern_one, point_one, coarsening_taps, kern_two, point_two):
    x = jnp.transpose(inputs[0], (1, 2, 0))
    t = jnp.transpose(targets[0], (1, 2, 0))
    rows, cols, chan = x.shape
    hid = point_one.shape[1]
    hr, hc = rows // 2, cols // 2
    up, down, ahead, back = edges(x, t)
    top, bot = shift(down, 1, 0), shift(up, -1, 0)
    ends = jnp.concatenate([top, bot], axis=0)
    halos = [
        top,
        bot,
        shift(ahead, 0, -1),
        shift(back, 0, 1),
        shift(ends[:, :8], 0, -1),
        shift(ends[:, cols - 8 :], 0, 1),
    ]
    ty, tx = lax.axis_index("ty"), lax.axis_index("tx")
    big = 1 << 20
    limits = jnp.stack(
        [
            jnp.where(ty == 0, 0, -big),
            jnp.where(ty == lax.axis_size("ty") - 1, hr, big),
            jnp.where(tx == 0, 0, -big),
            jnp.where(tx == lax.axis_size("tx") - 1, hc, big),
            tx % 2,
        ]
    ).astype(jnp.int32)
    taps = coarsening_taps.reshape(4, hid, hid)
    weights = (kern_one, point_one, taps, kern_two, point_two)
    pred, keep, send, sums = tile_step(limits, x, t, halos, *weights)
    small, own, other = reduced(keep, send)
    outs = update((tx % 2)[None].astype(jnp.int32), sums, small, own, other, *weights)
    outs = [o.reshape(coarsening_taps.shape) if o.shape == taps.shape else o for o in outs]
    return (jnp.transpose(pred, (2, 0, 1))[None], *outs)


def solution(mesh):
    tile = P("rep", None, "ty", "tx")
    return jax.shard_map(
        per_device,
        mesh=mesh,
        in_specs=(tile, tile, P(), P(), P(), P(), P()),
        out_specs=(tile,) + (P(),) * 10,
        check_vma=False,
    )
```

```python
import jax
import jax.numpy as jnp
from jax import lax
from jax.experimental import pallas as pl
from jax.experimental.pallas import tpu as pltpu
from jax.sharding import PartitionSpec as P

EPS = 1e-05
RATE = 0.05
F32 = jnp.float32
BF16 = jnp.bfloat16
LANES = 128
HALO = 4
ROWS = 6
SMALL = 64


def mm(a, b):
    return jnp.dot(a, b, preferred_element_type=F32)


def mm_t(a, b):
    return lax.dot_general(a, b, (((1,), (1,)), ((), ())), preferred_element_type=F32)


def t_mm(a, b):
    return lax.dot_general(a, b, (((0,), (0,)), ((), ())), preferred_element_type=F32)


def sigmoid(v):
    return 0.5 + 0.5 * jnp.tanh(0.5 * v)


def tile_kernel(
    limits,
    x_hbm,
    t_hbm,
    top_ref,
    bot_ref,
    right_ref,
    left_ref,
    right_ends,
    left_ends,
    k1_ref,
    p1_full,
    taps_hbm,
    k2_ref,
    p2_full,
    pred_hbm,
    keep_hbm,
    send_hbm,
    sums_ref,
    keep_ref,
    send_ref,
    x_ref,
    t_ref,
    taps_full,
    p1_ref,
    p1_half,
    taps_ref,
    p2_ref,
    pred_ref,
    sems,
    xf,
    tf,
    d2,
    out_e,
    out_own,
    pre_own,
    co,
    sl,
    cout,
    up,
    ot_own,
    ce_own,
    bc,
    bp,
    small,
):
    rows, cols, chan = x_ref.shape
    hid = k2_ref.shape[2]
    hr, hc = rows // 2, cols // 2
    slots = hc + 2 * HALO
    cb1, cb2 = chan // LANES, hid // LANES
    er = hr + 4
    fr = hr + 2

    def lanes(c):
        return slice(c * LANES, (c + 1) * LANES)

    core = limits[4]
    st_rows, p1_rows, p2_rows = hid * (hid // LANES), chan * (hid // LANES), hid * (chan // LANES)
    p1_at = 2 * st_rows
    p2_at = p1_at + p1_rows // 2
    small_at = p2_at + p2_rows // 2

    def emit(half, at, value):
        value = value.astype(BF16)

        @pl.when(core == half)
        def _():
            keep_ref[at : at + value.shape[0], :] = value

        @pl.when(core != half)
        def _():
            send_ref[at : at + value.shape[0], :] = value

    large, last = slice(0, small_at), slice(small_at, small_at + SMALL)
    pairs = [
        (t_hbm, t_ref),
        (taps_hbm, taps_full),
        (pred_ref, pred_hbm),
        (x_hbm, x_ref),
        (keep_ref.at[large], keep_hbm.at[large]),
        (send_ref.at[large], send_hbm.at[large]),
        (keep_ref.at[last], keep_hbm.at[last]),
        (send_ref.at[last], send_hbm.at[last]),
    ]
    copies = [pltpu.make_async_copy(*pair, sems.at[j]) for j, pair in enumerate(pairs)]
    copies[3].start()
    copies[0].start()
    copies[1].start()
    small[...] = jnp.zeros_like(small)
    p1_ref[...] = p1_full[...].astype(BF16)
    p1_half[...] = (p1_full[...].astype(BF16).astype(F32) * 0.5).astype(BF16)
    p2_ref[...] = p2_full[...].astype(BF16)

    def put(row, count, block, c):
        block = block.astype(F32)
        xf[c, pl.ds(row, count), 8 : 8 + cols, :] = block
        xf[c, pl.ds(row, count), 24 + cols : 25 + cols, :] = block[:, 0:1, :]

    def put_sides(row, count, right, left, c):
        at = pl.ds(row, count)
        right, left = right.astype(F32), left.astype(F32)
        xf[c, at, 8 + cols : 16 + cols, :] = right
        xf[c, at, 16 + cols : 24 + cols, :] = left
        xf[c, at, 7:8, :] = left[:, 7:8, :]

    step = 12
    for c in range(cb1):
        put(0, ROWS, top_ref[0:ROWS, :, lanes(c)], c)
        put(rows + ROWS, ROWS, bot_ref[0:ROWS, :, lanes(c)], c)
        put_sides(0, ROWS, right_ends[0:ROWS, :, lanes(c)], left_ends[0:ROWS, :, lanes(c)], c)
        cut = (slice(ROWS + 2, 2 * ROWS + 2), slice(None), lanes(c))
        put_sides(rows + ROWS, ROWS, right_ends[cut], left_ends[cut], c)

    copies[3].wait()

    @pl.loop(0, rows // step)
    def _(n):
        at = pl.ds(n * step, step)
        for c in range(cb1):
            put(ROWS + n * step, step, x_ref[at, :, lanes(c)], c)
            put_sides(ROWS + n * step, step, right_ref[at, :, lanes(c)], left_ref[at, :, lanes(c)], c)

    copies[0].wait()

    def diff(first, count, block, right, left, ends, c):
        at = pl.ds(2 * first + ROWS, 2 * count)
        rcol, lcol = (cols, cols + 8) if ends else (cols - 5, cols + 13)
        tf[c, 0 : 2 * count, rcol : rcol + 8, :] = right.astype(F32)
        tf[c, 0 : 2 * count, lcol : lcol + 8, :] = left.astype(F32)
        tf[c, 0 : 2 * count, 0:cols, :] = block.astype(F32)
        both = xf[c, at, 8 : 24 + cols, :] - tf[c, 0 : 2 * count, 0 : 16 + cols, :]
        both = both.reshape(count, 2, 16 + cols, LANES)
        tf[c, 0:count, 0 : 16 + cols, :] = both[:, 0] + both[:, 1]
        even = tf[c, 0:count, pl.ds(0, slots, stride=2), :]
        odd = tf[c, 0:count, pl.ds(1, slots, stride=2), :]
        d2[c, pl.ds(first + 1, count), :, :] = (even + odd) * 0.25

    for c in range(cb1):
        own = (slice(ROWS, ROWS + 2), slice(None), lanes(c))
        diff(-1, 1, top_ref[own], right_ends[own], left_ends[own], True, c)
        cut = (slice(2 * ROWS + 2, 2 * ROWS + 4), slice(None), lanes(c))
        diff(hr, 1, bot_ref[own], right_ends[cut], left_ends[cut], True, c)

    @pl.loop(0, hr // 4)
    def _(n):
        for c in range(cb1):
            cut = (pl.ds(n * 8, 8), slice(None), lanes(c))
            diff(n * 4, 4, t_ref[cut], right_ref[cut], left_ref[cut], False, c)

    take = 4

    @pl.loop(0, er // take)
    def _(n):
        pres = []
        for c in range(cb1):
            per = [[None] * take for _ in range(4)]
            for i in range(take):
                e = 2 * (n * take + i) + ROWS - 4
                near = [
                    [xf[c, e + s - 1, pl.ds(7 + o, slots, stride=2), :] for o in range(4)]
                    for s in range(4)
                ]
                for r in range(2):
                    total = [None, None]
                    for a in range(3):
                        for q in range(2):
                            for b in range(3):
                                term = k1_ref[a, b : b + 1, lanes(c)] * near[r + a][q + b]
                                total[q] = term if total[q] is None else total[q] + term
                    for q in range(2):
                        per[2 * r + q][i] = total[q]
            pres.append([jnp.stack(p) for p in per])
        for ph in range(4):
            for c in range(cb1):
                own = pres[c][ph][:, 0:hc, :].reshape(take * hc, LANES).astype(BF16)
                pre_own[ph, pl.ds(n * (take * hc), take * hc), lanes(c)] = own
        low = [
            jnp.concatenate(
                [pres[c][ph].reshape(take * slots, LANES).astype(BF16) for c in range(cb1)], axis=1
            )
            for ph in range(4)
        ]
        for ph in range(4):
            act = mm(low[ph], p1_half[...])
            out = act + act * jnp.tanh(act)
            out_e[ph, pl.ds(n * (take * slots), take * slots), :] = out.astype(BF16)
            own = out.reshape(take, slots, hid)[:, 0:hc, :].reshape(take * hc, hid)
            out_own[ph, pl.ds(n * (take * hc), take * hc), :] = own.astype(BF16)

    row_lo, row_hi, col_lo, col_hi = limits[0], limits[1], limits[2], limits[3]

    def inside(first, count):
        row = lax.broadcasted_iota(jnp.int32, (count, slots, LANES), 0) + first
        slot = lax.broadcasted_iota(jnp.int32, (count, slots, LANES), 1)
        col = jnp.where(slot < hc + HALO, slot, slot - slots)
        ok = (row >= row_lo) & (row < row_hi) & (col >= col_lo) & (col < col_hi)
        return jnp.where(ok, 1.0, 0.0).astype(F32)

    def wrapped(ref, c, at, value):
        ref[c, at, 8 : 8 + slots, :] = value
        ref[c, at, 7:8, :] = value[:, slots - 1 : slots, :]
        ref[c, at, 8 + slots : 9 + slots, :] = value[:, 0:1, :]

    copies[1].wait()

    piece = 128

    def cast(n, acc):
        ph, at = n // (hid // piece), pl.ds(n % (hid // piece) * piece, piece)
        w = taps_full[ph, at, :]
        taps_ref[ph, at, :] = w.astype(BF16)
        return acc + jnp.sum((w * w).reshape(piece // 8, 8, hid), axis=0)

    sums_ref[2] = jnp.sum(lax.fori_loop(0, 4 * hid // piece, cast, jnp.zeros((8, hid), F32)))
    for j, ref in ((0, k1_ref), (1, p1_full), (3, k2_ref), (4, p2_full)):
        sums_ref[j] = jnp.sum(ref[...] * ref[...])
    half = er // 2

    @pl.loop(0, 2)
    def _(n):
        ok = inside(n * half - 2, half)
        for m in range(hid // 256):
            acc = None
            for ph in range(4):
                term = mm(
                    out_e[ph, pl.ds(n * (half * slots), half * slots), :],
                    taps_ref[ph, :, m * 256 : (m + 1) * 256],
                )
                acc = term if acc is None else acc + term
            acc = acc.astype(BF16).astype(F32).reshape(half, slots, 256)
            for j in range(2):
                wrapped(co, 2 * m + j, pl.ds(n * half, half), acc[:, :, lanes(j)] * ok)

    part = 10

    @pl.loop(0, fr // part)
    def _(n):
        pre = []
        for c in range(cb2):
            subs = []
            for first in range(0, part, 5):
                total = None
                for b in range(3):
                    col = co[c, pl.ds(n * part + first, 7), 7 + b : 7 + b + slots, :]
                    for a in range(3):
                        term = k2_ref[a, b : b + 1, lanes(c)] * col[a : a + 5]
                        total = term if total is None else total + term
                subs.append(total)
            total = jnp.concatenate(subs, axis=0)
            pre.append(total.reshape(part * slots, LANES))
        gate = [sigmoid(p) for p in pre]
        out = [p * g for p, g in zip(pre, gate)]
        low = jnp.concatenate([o.astype(BF16) for o in out], axis=1)
        for c in range(cb2):
            own = out[c].reshape(part, slots, LANES)[:, 0:hc, :].reshape(part * hc, LANES)
            ot_own[pl.ds(n * (part * hc), part * hc), lanes(c)] = own.astype(BF16)
        back = mm(low, p2_ref[...]).reshape(part, slots, chan)
        errs = []
        for c in range(cb1):
            own = back[:, :, lanes(c)]
            cout[c, pl.ds(n * part, part), :, :] = own[:, 0:hc, :]
            err = own + d2[c, pl.ds(n * part, part), :, :]
            errs.append(err.reshape(part * slots, LANES).astype(BF16))
            ce_own[pl.ds(n * (part * hc), part * hc), lanes(c)] = (
                err[:, 0:hc, :].reshape(part * hc, LANES).astype(BF16)
            )
        err = jnp.concatenate(errs, axis=1)
        ok = inside(n * part - 1, part)
        back_two = mm_t(err, p2_ref[...])
        for c in range(cb2):
            slope = back_two[:, lanes(c)] * (gate[c] * (1.0 + pre[c] * (1.0 - gate[c])))
            slope = slope.astype(BF16).astype(F32).reshape(part, slots, LANES) * ok
            wrapped(sl, c, pl.ds(n * part, part), slope)

    gp2 = t_mm(ot_own[hc : hc + hr * hc, :], ce_own[hc : hc + hr * hc, :])
    for c in range(cb1):
        emit(2 * c // cb1, p2_at + (c % (cb1 // 2)) * hid, gp2[:, lanes(c)])

    @pl.loop(0, hr // 4)
    def _(n):
        for c in range(cb1):
            block = cout[c, pl.ds(n * 4 + 1, 4), :, :]
            up[c, :, pl.ds(0, hc, stride=2), :] = block
            up[c, :, pl.ds(1, hc, stride=2), :] = block
            wide = up[c, :, :, :]
            wide = jnp.stack([wide, wide], axis=1).reshape(8, cols, LANES)
            fine = xf[c, pl.ds(n * 8 + ROWS, 8), 8 : 8 + cols, :]
            pred_ref[pl.ds(n * 8, 8), :, lanes(c)] = (wide + fine).astype(BF16)

    copies[2].start()

    for c in range(cb2):
        def body(n, acc, c=c):
            acc = list(acc)
            for i in range(2):
                row = n * 2 + i
                slope = sl[c, row + 1, 8 : 8 + hc, :]
                total = None
                for a in range(3):
                    for b in range(3):
                        p = slope * co[c, row + 1 + a, 7 + b : 7 + b + hc, :]
                        acc[3 * a + b] = acc[3 * a + b] + (p[0:8] + p[8:16])
                        term = k2_ref[a, b : b + 1, lanes(c)] * sl[c, row + 2 - a, 9 - b : 9 - b + hc, :]
                        total = term if total is None else total + term
                bc[pl.ds(row * hc, hc), lanes(c)] = total.astype(BF16)
            return tuple(acc)

        acc = lax.fori_loop(0, hr // 2, body, tuple(jnp.zeros((8, LANES), F32) for _ in range(9)))
        for j in range(9):
            at = 9 * (cb1 + c) + j
            small[at : at + 1, :] = jnp.sum(acc[j], axis=0, keepdims=True)

    skip = 2 * hc
    own_rows = slice(skip, skip + hr * hc)
    for ph in range(4):
        gst = t_mm(out_own[ph, own_rows, :], bc[...])
        for c in range(cb2):
            emit(ph // 2, (ph % 2) * st_rows + c * hid, gst[:, lanes(c)])
        back = mm_t(bc[...], taps_ref[ph])
        act = mm(pre_own[ph, own_rows, :], p1_half[...])
        turn = jnp.tanh(act)
        slope = (back * ((0.5 + 0.5 * turn) * (1.0 + act * (1.0 - turn)))).astype(BF16)
        term = t_mm(pre_own[ph, own_rows, :], slope)
        gp1 = term if ph == 0 else gp1 + term
        back_pre = mm_t(slope, p1_ref[...])
        for c in range(cb1):
            bp[ph, c] = back_pre[:, lanes(c)].reshape(hr, hc, LANES)

    for c in range(cb2):
        emit(2 * c // cb2, p1_at + (c % (cb2 // 2)) * chan, gp1[:, lanes(c)])
    copies[4].start()
    copies[5].start()

    for c in range(cb1):

        def body(n, acc, c=c):
            acc = list(acc)
            grads = [[bp[ph, c, 4 * n + i] for ph in range(4)] for i in range(4)]
            for s in range(10):
                e = 8 * n + ROWS + s - 1
                col = [xf[c, e, pl.ds(7 + o, hc, stride=2), :] for o in range(4)]
                for i in range(4):
                    for r in range(2):
                        a = s - 2 * i - r
                        if 0 <= a < 3:
                            for q in range(2):
                                for b in range(3):
                                    p = grads[i][2 * r + q] * col[q + b]
                                    acc[3 * a + b] = acc[3 * a + b] + (p[0:8] + p[8:16])
            return tuple(acc)

        acc = lax.fori_loop(0, hr // 4, body, tuple(jnp.zeros((8, LANES), F32) for _ in range(9)))
        for j in range(9):
            at = 9 * c + j
            small[at : at + 1, :] = jnp.sum(acc[j], axis=0, keepdims=True)


    for ref in (keep_ref, send_ref):
        ref[small_at : small_at + SMALL, :] = small[...].astype(BF16)
    copies[6].start()
    copies[7].start()
    for j in (2, 4, 5, 6, 7):
        copies[j].wait()


def vmem():
    return pl.BlockSpec(memory_space=pltpu.VMEM)


def hbm():
    return pl.BlockSpec(memory_space=pl.ANY)


def smem():
    return pl.BlockSpec(memory_space=pltpu.SMEM)


def tile_step(limits, x, t, halos, k1, p1, taps, k2, p2):
    rows, cols, chan = x.shape
    hid = k2.shape[2]
    hr, hc = rows // 2, cols // 2
    slots = hc + 2 * HALO
    cb1, cb2 = chan // LANES, hid // LANES
    grads = (p1.size + taps.size + p2.size) // (2 * LANES) + SMALL
    return pl.pallas_call(
        tile_kernel,
        out_shape=(
            jax.ShapeDtypeStruct(x.shape, BF16),
            jax.ShapeDtypeStruct((grads, LANES), BF16),
            jax.ShapeDtypeStruct((grads, LANES), BF16),
            jax.ShapeDtypeStruct((5,), F32),
        ),
        in_specs=[smem(), hbm(), hbm()]
        + [vmem()] * (len(halos) + 2)
        + [hbm(), vmem(), vmem()],
        out_specs=[hbm(), hbm(), hbm(), smem()],
        scratch_shapes=[
            pltpu.VMEM((grads, LANES), BF16),
            pltpu.VMEM((grads, LANES), BF16),
            pltpu.VMEM(x.shape, BF16),
            pltpu.VMEM(t.shape, BF16),
            pltpu.VMEM(taps.shape, F32),
            pltpu.VMEM(p1.shape, BF16),
            pltpu.VMEM(p1.shape, BF16),
            pltpu.VMEM(taps.shape, BF16),
            pltpu.VMEM(p2.shape, BF16),
            pltpu.VMEM(x.shape, BF16),
            pltpu.SemaphoreType.DMA((8,)),
            pltpu.VMEM((cb1, rows + 2 * ROWS, cols + 32, LANES), F32),
            pltpu.VMEM((cb1, 8, cols + 32, LANES), F32),
            pltpu.VMEM((cb1, hr + 2, slots, LANES), F32),
            pltpu.VMEM((4, (hr + 4) * slots, hid), BF16),
            pltpu.VMEM((4, (hr + 4) * hc, hid), BF16),
            pltpu.VMEM((4, (hr + 4) * hc, chan), BF16),
            pltpu.VMEM((cb2, hr + 4, slots + 16, LANES), F32),
            pltpu.VMEM((cb2, hr + 2, slots + 16, LANES), F32),
            pltpu.VMEM((cb1, hr + 2, hc, LANES), F32),
            pltpu.VMEM((cb1, 4, cols, LANES), F32),
            pltpu.VMEM(((hr + 2) * hc, hid), BF16),
            pltpu.VMEM(((hr + 2) * hc, chan), BF16),
            pltpu.VMEM((hr * hc, hid), BF16),
            pltpu.VMEM((4, cb1, hr, hc, LANES), F32),
            pltpu.VMEM((SMALL, LANES), F32),
        ],
        compiler_params=pltpu.CompilerParams(vmem_limit_bytes=63 * 1024 * 1024),
        cost_estimate=pl.CostEstimate(flops=9_000_000_000, bytes_accessed=20_000_000, transcendentals=0),
    )(limits, x, t, *halos, k1, p1, taps, k2, p2)


def edges_kernel(xt, tt, xb, tb, xl, tl, xr, tr, up, down, ahead, back):
    up[...] = jnp.concatenate([xt[0:ROWS], tt[0:2]], axis=0)
    down[...] = jnp.concatenate([xb[8 - ROWS : 8], tb[6:8]], axis=0)
    col = lax.broadcasted_iota(jnp.int32, ahead.shape, 1)
    x, t = xl[:, 0:8, :].astype(F32), tl[:, 0:8, :].astype(F32)
    ahead[...] = jnp.where((col >= 5) & (col < 7), pltpu.roll(t, 5, 1), x).astype(BF16)
    x, t = xr[:, 8:16, :].astype(F32), tr[:, 8:16, :].astype(F32)
    back[...] = jnp.where((col >= 1) & (col < 3), pltpu.roll(t, 3, 1), x).astype(BF16)


def edges(x, t):
    rows, cols, chan = x.shape
    specs = [
        pl.BlockSpec((8, cols, chan), lambda n: (0, 0, 0)),
        pl.BlockSpec((8, cols, chan), lambda n: (rows // 8 - 1, 0, 0)),
        pl.BlockSpec((rows, 16, chan), lambda n: (0, 0, 0)),
        pl.BlockSpec((rows, 16, chan), lambda n: (0, cols // 16 - 1, 0)),
    ]
    shapes = [(ROWS + 2, cols, chan)] * 2 + [(rows, 8, chan)] * 2
    return pl.pallas_call(
        edges_kernel,
        grid=(1,),
        out_shape=[jax.ShapeDtypeStruct(s, BF16) for s in shapes],
        in_specs=[s for s in specs for _ in range(2)],
        out_specs=[pl.BlockSpec(s, lambda n: (0, 0, 0)) for s in shapes],
    )(*[x, t] * 4)


def update_kernel(
    where,
    sums,
    small_ref,
    own_ref,
    other_ref,
    *refs,
):
    (
        k1_ref,
        p1_ref,
        st_hbm,
        k2_ref,
        p2_ref,
        nk1_ref,
        np1_ref,
        nst_ref,
        nk2_ref,
        np2_ref,
        sk1_ref,
        sp1_ref,
        sst_ref,
        sk2_ref,
        sp2_ref,
        g,
        small,
        scale,
        st_ref,
        sems,
    ) = refs
    chan, hid = p1_ref.shape
    cb1, cb2 = chan // LANES, hid // LANES
    parts, block = 4, st_ref.shape[1]
    step = pl.program_id(0)
    per = hid // block

    def fetch(n):
        at = pl.ds(n % per * block, block)
        return pltpu.make_async_copy(st_hbm.at[n // per, at, :], st_ref.at[n], sems.at[n])

    core = where[0]
    st_rows, p1_rows, p2_rows = hid * cb2, chan * cb2, hid * cb1
    p1_at = 2 * st_rows
    p2_at = p1_at + p1_rows // 2
    small_at = p2_at + p2_rows // 2
    sizes = (9 * chan, chan * hid, parts * hid * hid, 9 * hid, chan * hid)

    def root(v):
        r = lax.rsqrt(v)
        return v * (r * (1.5 - 0.5 * v * r * r))

    def squares(at, count):
        block = 256

        def body(n, acc):
            rows = pl.ds(pl.multiple_of(at + n * block, block), block)
            out = []
            for half, ref, a in ((core, own_ref, acc[0]), (1 - core, other_ref, acc[1])):
                v = ref[rows, :]
                g[half, rows, :] = v
                v = v.astype(F32)
                out.append(a + jnp.sum((v * v).reshape(block // 8, 8, LANES), axis=0))
            return tuple(out)

        zero = jnp.zeros((8, LANES), F32)
        both = lax.fori_loop(0, count // block, body, (zero, zero))
        return jnp.sum(both[0] + both[1], keepdims=True)

    def set_scale(j, total):
        mean = jnp.broadcast_to(total, (1, LANES)) / sizes[j]
        scale[j : j + 1, :] = 1.0 / root(mean + EPS)
        mean = jnp.full((1, LANES), sums[j] / sizes[j], F32)
        scale[5 + j : 6 + j, :] = RATE * root(mean + EPS)

    @pl.when(step == 0)
    def _():
        for n in range(parts * per):
            fetch(n).start()
        small[...] = small_ref[...].astype(F32)
        v = small[0 : 9 * cb1, :]
        set_scale(0, jnp.sum(v * v, keepdims=True))
        v = small[9 * cb1 : 9 * (cb1 + cb2), :]
        set_scale(3, jnp.sum(v * v, keepdims=True))
        set_scale(1, squares(p1_at, p1_rows // 2))
        set_scale(4, squares(p2_at, p2_rows // 2))
        set_scale(2, squares(0, 2 * st_rows))
        for j, first, blocks, w, new, out in (
            (0, 0, cb1, k1_ref, nk1_ref, sk1_ref),
            (3, 9 * cb1, cb2, k2_ref, nk2_ref, sk2_ref),
        ):
            for c in range(blocks):
                cut = slice(c * LANES, (c + 1) * LANES)
                for r in range(3):
                    at = first + 9 * c + 3 * r
                    normed = small[at : at + 3, :] * scale[j : j + 1, :]
                    out[r, :, cut] = normed
                    new[r, :, cut] = w[r, :, cut] - scale[5 + j : 6 + j, :] * normed
        for c in range(cb2):
            cut = slice(c * LANES, (c + 1) * LANES)
            at = p1_at + (c % (cb2 // 2)) * chan
            normed = g[2 * c // cb2, at : at + chan, :].astype(F32) * scale[1:2, :]
            sp1_ref[:, cut] = normed
            np1_ref[:, cut] = p1_ref[:, cut] - scale[6:7, :] * normed
        for c in range(cb1):
            cut = slice(c * LANES, (c + 1) * LANES)
            at = p2_at + (c % (cb1 // 2)) * hid
            normed = g[2 * c // cb1, at : at + hid, :].astype(F32) * scale[4:5, :]
            sp2_ref[:, cut] = normed
            np2_ref[:, cut] = p2_ref[:, cut] - scale[9:10, :] * normed

    fetch(step).wait()
    ph = step // per
    for c in range(cb2):
        cut = slice(c * LANES, (c + 1) * LANES)
        at = (ph % 2) * st_rows + c * hid + (step % per) * block
        normed = g[ph // 2, pl.ds(at, block), :].astype(F32) * scale[2:3, :]
        sst_ref[0, :, cut] = normed
        nst_ref[0, :, cut] = st_ref[step, :, cut] - scale[7:8, :] * normed


def update(where, sums, small, own, other, k1, p1, taps, k2, p2):
    hid = taps.shape[1]
    block = hid // 2
    per = hid // block

    def whole(w):
        return pl.BlockSpec(w.shape, lambda n: (0,) * w.ndim)

    st = pl.BlockSpec((1, block, hid), lambda n: (n // per, n % per, 0))
    specs = [whole(k1), whole(p1), st, whole(k2), whole(p2)]
    shapes = [jax.ShapeDtypeStruct(w.shape, F32) for w in (k1, p1, taps, k2, p2)]
    return pl.pallas_call(
        update_kernel,
        grid=(4 * per,),
        out_shape=shapes + shapes,
        in_specs=[smem(), smem(), whole(small)] + [whole(own), whole(other)]
        + specs[:2]
        + [hbm()]
        + specs[3:],
        out_specs=specs + specs,
        scratch_shapes=[
            pltpu.VMEM((2,) + own.shape, BF16),
            pltpu.VMEM((SMALL, LANES), F32),
            pltpu.VMEM((16, LANES), F32),
            pltpu.VMEM((4 * per, block, hid), F32),
            pltpu.SemaphoreType.DMA((4 * per,)),
        ],
        compiler_params=pltpu.CompilerParams(vmem_limit_bytes=40 * 1024 * 1024),
    )(where, sums, small, own, other, k1, p1, taps, k2, p2)


def shift(block, down, right):
    n, m = lax.axis_size("ty"), lax.axis_size("tx")
    pairs = [
        (i * m + j, (i + down) * m + j + right)
        for i in range(n)
        for j in range(m)
        if 0 <= i + down < n and 0 <= j + right < m
    ]
    return lax.ppermute(block, ("ty", "tx"), pairs)


class Ring:
    def __init__(self, names):
        sizes = {"x": lax.axis_size("tx") // 2, "y": lax.axis_size("rep"), "z": lax.axis_size("ty")}
        place = {"x": lax.axis_index("tx") // 2, "y": lax.axis_index("rep"), "z": lax.axis_index("ty")}
        self.names, self.sizes = names, sizes
        self.count = sizes[names[0]]
        assert sizes[names[1]] == self.count
        self.steps = range(1, self.count)
        self.me = jnp.where(lax.axis_index("tx") % 2 == 0, place[names[0]], place[names[1]])

    def send(self, block, step):
        sizes = self.sizes

        def flat(at, core):
            return ((at["y"] * sizes["z"] + at["z"]) * sizes["x"] + at["x"]) * 2 + core

        pairs = []
        for i in range(sizes["y"]):
            for j in range(sizes["z"]):
                for k in range(sizes["x"]):
                    for core in range(2):
                        at = {"y": i, "z": j, "x": k}
                        to = dict(at)
                        name = self.names[core]
                        to[name] = (at[name] + step) % sizes[name]
                        pairs.append((flat(at, core), flat(to, core)))
        return lax.ppermute(block, ("rep", "ty", "tx"), pairs)

    def scatter(self, block, extra):
        n = self.count
        shares = block.reshape((n, -1, LANES))
        share = lax.dynamic_index_in_dim(shares, self.me, 0, False)
        cut = share.shape[0]
        got = {}
        for d in self.steps:
            out = lax.dynamic_index_in_dim(shares, (self.me + d) % n, 0, False)
            got[d] = self.send(jnp.concatenate([out, extra], axis=0), d)
        total = sum([g[:cut].astype(F32) for g in got.values()], share.astype(F32))
        return total.astype(BF16), self.added([extra] + [got[d][cut:] for d in range(1, n)])

    def added(self, parts):
        n = self.count
        parts = jnp.stack(parts)
        total = None
        for k in range(n):
            part = lax.dynamic_index_in_dim(parts, (self.me + n - k) % n, 0, False).astype(F32)
            total = part if total is None else total + part
        return total.astype(BF16)

    def reduce(self, block):
        got = {d: self.send(block, d) for d in self.steps}
        return self.added([block] + [got[d] for d in range(1, self.count)])

    def gather(self, share):
        n = self.count
        out = jnp.zeros((n,) + share.shape, share.dtype)
        out = lax.dynamic_update_index_in_dim(out, share, self.me, 0)
        for d in self.steps:
            got = self.send(share, d)
            out = lax.dynamic_update_index_in_dim(out, got, (self.me + n - d) % n, 0)
        return out.reshape(-1, LANES)


def reduced(keep, send):
    rings = (Ring("yx"), Ring("xy"))
    cores = [(i, i ^ 1) for i in range(lax.axis_size("tx"))]
    got = lax.ppermute(send, "tx", cores)
    both = (keep.astype(F32) + got.astype(F32)).astype(BF16)
    share, small = both[: both.shape[0] - SMALL], both[both.shape[0] - SMALL :]
    for ring in rings:
        share, small = ring.scatter(share, small)
    both = Ring("zz").reduce(jnp.concatenate([share, small], axis=0))
    share, small = both[: share.shape[0]], both[share.shape[0] :]
    for ring in rings[::-1]:
        share = ring.gather(share)
    return small, share, lax.ppermute(share, "tx", cores)


def per_device(inputs, targets, kern_one, point_one, coarsening_taps, kern_two, point_two):
    x = jnp.transpose(inputs[0], (1, 2, 0))
    t = jnp.transpose(targets[0], (1, 2, 0))
    rows, cols, chan = x.shape
    hid = point_one.shape[1]
    hr, hc = rows // 2, cols // 2
    up, down, ahead, back = edges(x, t)
    top, bot = shift(down, 1, 0), shift(up, -1, 0)
    ends = jnp.concatenate([top, bot], axis=0)
    halos = [
        top,
        bot,
        shift(ahead, 0, -1),
        shift(back, 0, 1),
        shift(ends[:, :8], 0, -1),
        shift(ends[:, cols - 8 :], 0, 1),
    ]
    ty, tx = lax.axis_index("ty"), lax.axis_index("tx")
    big = 1 << 20
    limits = jnp.stack(
        [
            jnp.where(ty == 0, 0, -big),
            jnp.where(ty == lax.axis_size("ty") - 1, hr, big),
            jnp.where(tx == 0, 0, -big),
            jnp.where(tx == lax.axis_size("tx") - 1, hc, big),
            tx % 2,
        ]
    ).astype(jnp.int32)
    taps = coarsening_taps.reshape(4, hid, hid)
    weights = (kern_one, point_one, taps, kern_two, point_two)
    pred, keep, send, sums = tile_step(limits, x, t, halos, *weights)
    small, own, other = reduced(keep, send)
    outs = update((tx % 2)[None].astype(jnp.int32), sums, small, own, other, *weights)
    outs = [o.reshape(coarsening_taps.shape) if o.shape == taps.shape else o for o in outs]
    return (jnp.transpose(pred, (2, 0, 1))[None], *outs)


def solution(mesh):
    tile = P("rep", None, "ty", "tx")
    return jax.shard_map(
        per_device,
        mesh=mesh,
        in_specs=(tile, tile, P(), P(), P(), P(), P()),
        out_specs=(tile,) + (P(),) * 10,
        check_vma=False,
    )
```

```python
import jax
import jax.numpy as jnp
from jax import lax
from jax.experimental import pallas as pl
from jax.experimental.pallas import tpu as pltpu
from jax.sharding import PartitionSpec as P

EPS = 1e-05
RATE = 0.05
F32 = jnp.float32
BF16 = jnp.bfloat16
LANES = 128
HALO = 4
ROWS = 6
SMALL = 64


def mm(a, b):
    return jnp.dot(a, b, preferred_element_type=F32)


def mm_t(a, b):
    return lax.dot_general(a, b, (((1,), (1,)), ((), ())), preferred_element_type=F32)


def t_mm(a, b):
    return lax.dot_general(a, b, (((0,), (0,)), ((), ())), preferred_element_type=F32)


def sigmoid(v):
    return 0.5 + 0.5 * jnp.tanh(0.5 * v)


def tile_kernel(
    limits,
    x_hbm,
    t_hbm,
    top_ref,
    bot_ref,
    right_ref,
    left_ref,
    right_ends,
    left_ends,
    k1_ref,
    p1_full,
    taps_hbm,
    k2_ref,
    p2_full,
    pred_hbm,
    keep_hbm,
    send_hbm,
    sums_ref,
    keep_ref,
    send_ref,
    x_ref,
    t_ref,
    taps_full,
    p1_ref,
    p1_half,
    taps_ref,
    p2_ref,
    pred_ref,
    sems,
    xf,
    tf,
    d2,
    out_e,
    out_own,
    pre_own,
    co,
    sl,
    cout,
    up,
    ot_own,
    ce_own,
    bc,
    bp,
    small,
):
    rows, cols, chan = x_ref.shape
    hid = k2_ref.shape[2]
    hr, hc = rows // 2, cols // 2
    slots = hc + 2 * HALO
    cb1, cb2 = chan // LANES, hid // LANES
    er = hr + 4
    fr = hr + 2

    def lanes(c):
        return slice(c * LANES, (c + 1) * LANES)

    core = limits[4]
    st_rows, p1_rows, p2_rows = hid * (hid // LANES), chan * (hid // LANES), hid * (chan // LANES)
    p1_at = 2 * st_rows
    p2_at = p1_at + p1_rows // 2
    small_at = p2_at + p2_rows // 2

    def emit(half, at, value):
        value = value.astype(BF16)

        @pl.when(core == half)
        def _():
            keep_ref[at : at + value.shape[0], :] = value

        @pl.when(core != half)
        def _():
            send_ref[at : at + value.shape[0], :] = value

    large, last = slice(0, small_at), slice(small_at, small_at + SMALL)
    pairs = [
        (t_hbm, t_ref),
        (taps_hbm, taps_full),
        (pred_ref, pred_hbm),
        (x_hbm, x_ref),
        (keep_ref.at[large], keep_hbm.at[large]),
        (send_ref.at[large], send_hbm.at[large]),
        (keep_ref.at[last], keep_hbm.at[last]),
        (send_ref.at[last], send_hbm.at[last]),
    ]
    copies = [pltpu.make_async_copy(*pair, sems.at[j]) for j, pair in enumerate(pairs)]
    copies[3].start()
    copies[0].start()
    copies[1].start()
    small[...] = jnp.zeros_like(small)
    p1_ref[...] = p1_full[...].astype(BF16)
    p1_half[...] = (p1_full[...].astype(BF16).astype(F32) * 0.5).astype(BF16)
    p2_ref[...] = p2_full[...].astype(BF16)

    def put(row, count, block, c):
        block = block.astype(F32)
        xf[c, pl.ds(row, count), 8 : 8 + cols, :] = block
        xf[c, pl.ds(row, count), 24 + cols : 25 + cols, :] = block[:, 0:1, :]

    def put_sides(row, count, right, left, c):
        at = pl.ds(row, count)
        right, left = right.astype(F32), left.astype(F32)
        xf[c, at, 8 + cols : 16 + cols, :] = right
        xf[c, at, 16 + cols : 24 + cols, :] = left
        xf[c, at, 7:8, :] = left[:, 7:8, :]

    step = 12
    for c in range(cb1):
        put(0, ROWS, top_ref[0:ROWS, :, lanes(c)], c)
        put(rows + ROWS, ROWS, bot_ref[0:ROWS, :, lanes(c)], c)
        put_sides(0, ROWS, right_ends[0:ROWS, :, lanes(c)], left_ends[0:ROWS, :, lanes(c)], c)
        cut = (slice(ROWS + 2, 2 * ROWS + 2), slice(None), lanes(c))
        put_sides(rows + ROWS, ROWS, right_ends[cut], left_ends[cut], c)

    copies[3].wait()

    @pl.loop(0, rows // step)
    def _(n):
        at = pl.ds(n * step, step)
        for c in range(cb1):
            put(ROWS + n * step, step, x_ref[at, :, lanes(c)], c)
            put_sides(ROWS + n * step, step, right_ref[at, :, lanes(c)], left_ref[at, :, lanes(c)], c)

    copies[0].wait()

    def diff(first, count, block, right, left, ends, c):
        at = pl.ds(2 * first + ROWS, 2 * count)
        rcol, lcol = (cols, cols + 8) if ends else (cols - 5, cols + 13)
        tf[c, 0 : 2 * count, rcol : rcol + 8, :] = right.astype(F32)
        tf[c, 0 : 2 * count, lcol : lcol + 8, :] = left.astype(F32)
        tf[c, 0 : 2 * count, 0:cols, :] = block.astype(F32)
        both = xf[c, at, 8 : 24 + cols, :] - tf[c, 0 : 2 * count, 0 : 16 + cols, :]
        both = both.reshape(count, 2, 16 + cols, LANES)
        tf[c, 0:count, 0 : 16 + cols, :] = both[:, 0] + both[:, 1]
        even = tf[c, 0:count, pl.ds(0, slots, stride=2), :]
        odd = tf[c, 0:count, pl.ds(1, slots, stride=2), :]
        d2[c, pl.ds(first + 1, count), :, :] = (even + odd) * 0.25

    for c in range(cb1):
        own = (slice(ROWS, ROWS + 2), slice(None), lanes(c))
        diff(-1, 1, top_ref[own], right_ends[own], left_ends[own], True, c)
        cut = (slice(2 * ROWS + 2, 2 * ROWS + 4), slice(None), lanes(c))
        diff(hr, 1, bot_ref[own], right_ends[cut], left_ends[cut], True, c)

    @pl.loop(0, hr // 4)
    def _(n):
        for c in range(cb1):
            cut = (pl.ds(n * 8, 8), slice(None), lanes(c))
            diff(n * 4, 4, t_ref[cut], right_ref[cut], left_ref[cut], False, c)

    take = 4

    @pl.loop(0, er // take)
    def _(n):
        pres = []
        for c in range(cb1):
            per = [[None] * take for _ in range(4)]
            for i in range(take):
                e = 2 * (n * take + i) + ROWS - 4
                near = [
                    [xf[c, e + s - 1, pl.ds(7 + o, slots, stride=2), :] for o in range(4)]
                    for s in range(4)
                ]
                for r in range(2):
                    total = [None, None]
                    for a in range(3):
                        for q in range(2):
                            for b in range(3):
                                term = k1_ref[a, b : b + 1, lanes(c)] * near[r + a][q + b]
                                total[q] = term if total[q] is None else total[q] + term
                    for q in range(2):
                        per[2 * r + q][i] = total[q]
            pres.append([jnp.stack(p) for p in per])
        for ph in range(4):
            for c in range(cb1):
                own = pres[c][ph][:, 0:hc, :].reshape(take * hc, LANES).astype(BF16)
                pre_own[ph, pl.ds(n * (take * hc), take * hc), lanes(c)] = own
        low = [
            jnp.concatenate(
                [pres[c][ph].reshape(take * slots, LANES).astype(BF16) for c in range(cb1)], axis=1
            )
            for ph in range(4)
        ]
        for ph in range(4):
            act = mm(low[ph], p1_half[...])
            out = act + act * jnp.tanh(act)
            out_e[ph, pl.ds(n * (take * slots), take * slots), :] = out.astype(BF16)
            own = out.reshape(take, slots, hid)[:, 0:hc, :].reshape(take * hc, hid)
            out_own[ph, pl.ds(n * (take * hc), take * hc), :] = own.astype(BF16)

    row_lo, row_hi, col_lo, col_hi = limits[0], limits[1], limits[2], limits[3]

    def inside(first, count):
        row = lax.broadcasted_iota(jnp.int32, (count, slots, LANES), 0) + first
        slot = lax.broadcasted_iota(jnp.int32, (count, slots, LANES), 1)
        col = jnp.where(slot < hc + HALO, slot, slot - slots)
        ok = (row >= row_lo) & (row < row_hi) & (col >= col_lo) & (col < col_hi)
        return jnp.where(ok, 1.0, 0.0).astype(F32)

    def wrapped(ref, c, at, value):
        ref[c, at, 8 : 8 + slots, :] = value
        ref[c, at, 7:8, :] = value[:, slots - 1 : slots, :]
        ref[c, at, 8 + slots : 9 + slots, :] = value[:, 0:1, :]

    copies[1].wait()

    piece = 128

    def cast(n, acc):
        ph, at = n // (hid // piece), pl.ds(n % (hid // piece) * piece, piece)
        w = taps_full[ph, at, :]
        taps_ref[ph, at, :] = w.astype(BF16)
        return acc + jnp.sum((w * w).reshape(piece // 8, 8, hid), axis=0)

    sums_ref[2] = jnp.sum(lax.fori_loop(0, 4 * hid // piece, cast, jnp.zeros((8, hid), F32)))
    for j, ref in ((0, k1_ref), (1, p1_full), (3, k2_ref), (4, p2_full)):
        sums_ref[j] = jnp.sum(ref[...] * ref[...])
    half = er // 2

    @pl.loop(0, 2)
    def _(n):
        ok = inside(n * half - 2, half)
        for m in range(hid // 256):
            acc = None
            for ph in range(4):
                term = mm(
                    out_e[ph, pl.ds(n * (half * slots), half * slots), :],
                    taps_ref[ph, :, m * 256 : (m + 1) * 256],
                )
                acc = term if acc is None else acc + term
            acc = acc.astype(BF16).astype(F32).reshape(half, slots, 256)
            for j in range(2):
                wrapped(co, 2 * m + j, pl.ds(n * half, half), acc[:, :, lanes(j)] * ok)

    part = 10

    @pl.loop(0, fr // part)
    def _(n):
        pre = []
        for c in range(cb2):
            subs = []
            for first in range(0, part, 5):
                total = None
                for b in range(3):
                    col = co[c, pl.ds(n * part + first, 7), 7 + b : 7 + b + slots, :]
                    for a in range(3):
                        term = k2_ref[a, b : b + 1, lanes(c)] * col[a : a + 5]
                        total = term if total is None else total + term
                subs.append(total)
            total = jnp.concatenate(subs, axis=0)
            pre.append(total.reshape(part * slots, LANES))
        gate = [sigmoid(p) for p in pre]
        out = [p * g for p, g in zip(pre, gate)]
        low = jnp.concatenate([o.astype(BF16) for o in out], axis=1)
        for c in range(cb2):
            own = out[c].reshape(part, slots, LANES)[:, 0:hc, :].reshape(part * hc, LANES)
            ot_own[pl.ds(n * (part * hc), part * hc), lanes(c)] = own.astype(BF16)
        back = mm(low, p2_ref[...]).reshape(part, slots, chan)
        errs = []
        for c in range(cb1):
            own = back[:, :, lanes(c)]
            cout[c, pl.ds(n * part, part), :, :] = own[:, 0:hc, :]
            err = own + d2[c, pl.ds(n * part, part), :, :]
            errs.append(err.reshape(part * slots, LANES).astype(BF16))
            ce_own[pl.ds(n * (part * hc), part * hc), lanes(c)] = (
                err[:, 0:hc, :].reshape(part * hc, LANES).astype(BF16)
            )
        err = jnp.concatenate(errs, axis=1)
        ok = inside(n * part - 1, part)
        back_two = mm_t(err, p2_ref[...])
        for c in range(cb2):
            slope = back_two[:, lanes(c)] * (gate[c] * (1.0 + pre[c] * (1.0 - gate[c])))
            slope = slope.astype(BF16).astype(F32).reshape(part, slots, LANES) * ok
            wrapped(sl, c, pl.ds(n * part, part), slope)

    gp2 = t_mm(ot_own[hc : hc + hr * hc, :], ce_own[hc : hc + hr * hc, :])
    for c in range(cb1):
        emit(2 * c // cb1, p2_at + (c % (cb1 // 2)) * hid, gp2[:, lanes(c)])

    @pl.loop(0, hr // 4)
    def _(n):
        for c in range(cb1):
            block = cout[c, pl.ds(n * 4 + 1, 4), :, :]
            up[c, :, pl.ds(0, hc, stride=2), :] = block
            up[c, :, pl.ds(1, hc, stride=2), :] = block
            wide = up[c, :, 0:cols, :]
            wide = jnp.stack([wide, wide], axis=1).reshape(8, cols, LANES)
            fine = xf[c, pl.ds(n * 8 + ROWS, 8), 8 : 8 + cols, :]
            pred_ref[pl.ds(n * 8, 8), :, lanes(c)] = (wide + fine).astype(BF16)

    copies[2].start()

    for c in range(cb2):
        def body(n, acc, c=c):
            acc = list(acc)
            for i in range(2):
                row = n * 2 + i
                slope = sl[c, row + 1, 8 : 8 + hc, :]
                total = None
                for a in range(3):
                    for b in range(3):
                        p = slope * co[c, row + 1 + a, 7 + b : 7 + b + hc, :]
                        acc[3 * a + b] = acc[3 * a + b] + (p[0:8] + p[8:16])
                        term = k2_ref[a, b : b + 1, lanes(c)] * sl[c, row + 2 - a, 9 - b : 9 - b + hc, :]
                        total = term if total is None else total + term
                bc[pl.ds(row * hc, hc), lanes(c)] = total.astype(BF16)
            return tuple(acc)

        acc = lax.fori_loop(0, hr // 2, body, tuple(jnp.zeros((8, LANES), F32) for _ in range(9)))
        for j in range(9):
            at = 9 * (cb1 + c) + j
            small[at : at + 1, :] = jnp.sum(acc[j], axis=0, keepdims=True)

    skip = 2 * hc
    own_rows = slice(skip, skip + hr * hc)
    for ph in range(4):
        gst = t_mm(out_own[ph, own_rows, :], bc[...])
        for c in range(cb2):
            emit(ph // 2, (ph % 2) * st_rows + c * hid, gst[:, lanes(c)])
        back = mm_t(bc[...], taps_ref[ph])
        act = mm(pre_own[ph, own_rows, :], p1_half[...])
        turn = jnp.tanh(act)
        slope = (back * ((0.5 + 0.5 * turn) * (1.0 + act * (1.0 - turn)))).astype(BF16)
        term = t_mm(pre_own[ph, own_rows, :], slope)
        gp1 = term if ph == 0 else gp1 + term
        back_pre = mm_t(slope, p1_ref[...])
        for c in range(cb1):
            bp[ph, c] = back_pre[:, lanes(c)].reshape(hr, hc, LANES)

    for c in range(cb2):
        emit(2 * c // cb2, p1_at + (c % (cb2 // 2)) * chan, gp1[:, lanes(c)])
    copies[4].start()
    copies[5].start()

    for c in range(cb1):

        def body(n, acc, c=c):
            acc = list(acc)
            grads = [[bp[ph, c, 4 * n + i] for ph in range(4)] for i in range(4)]
            for s in range(10):
                e = 8 * n + ROWS + s - 1
                col = [xf[c, e, pl.ds(7 + o, hc, stride=2), :] for o in range(4)]
                for i in range(4):
                    for r in range(2):
                        a = s - 2 * i - r
                        if 0 <= a < 3:
                            for q in range(2):
                                for b in range(3):
                                    p = grads[i][2 * r + q] * col[q + b]
                                    acc[3 * a + b] = acc[3 * a + b] + (p[0:8] + p[8:16])
            return tuple(acc)

        acc = lax.fori_loop(0, hr // 4, body, tuple(jnp.zeros((8, LANES), F32) for _ in range(9)))
        for j in range(9):
            at = 9 * c + j
            small[at : at + 1, :] = jnp.sum(acc[j], axis=0, keepdims=True)


    for ref in (keep_ref, send_ref):
        ref[small_at : small_at + SMALL, :] = small[...].astype(BF16)
    copies[6].start()
    copies[7].start()
    for j in (2, 4, 5, 6, 7):
        copies[j].wait()


def vmem():
    return pl.BlockSpec(memory_space=pltpu.VMEM)


def hbm():
    return pl.BlockSpec(memory_space=pl.ANY)


def smem():
    return pl.BlockSpec(memory_space=pltpu.SMEM)


def tile_step(limits, x, t, halos, k1, p1, taps, k2, p2):
    rows, cols, chan = x.shape
    hid = k2.shape[2]
    hr, hc = rows // 2, cols // 2
    slots = hc + 2 * HALO
    cb1, cb2 = chan // LANES, hid // LANES
    grads = (p1.size + taps.size + p2.size) // (2 * LANES) + SMALL
    return pl.pallas_call(
        tile_kernel,
        out_shape=(
            jax.ShapeDtypeStruct(x.shape, BF16),
            jax.ShapeDtypeStruct((grads, LANES), BF16),
            jax.ShapeDtypeStruct((grads, LANES), BF16),
            jax.ShapeDtypeStruct((5,), F32),
        ),
        in_specs=[smem(), hbm(), hbm()]
        + [vmem()] * (len(halos) + 2)
        + [hbm(), vmem(), vmem()],
        out_specs=[hbm(), hbm(), hbm(), smem()],
        scratch_shapes=[
            pltpu.VMEM((grads, LANES), BF16),
            pltpu.VMEM((grads, LANES), BF16),
            pltpu.VMEM(x.shape, BF16),
            pltpu.VMEM(t.shape, BF16),
            pltpu.VMEM(taps.shape, F32),
            pltpu.VMEM(p1.shape, BF16),
            pltpu.VMEM(p1.shape, BF16),
            pltpu.VMEM(taps.shape, BF16),
            pltpu.VMEM(p2.shape, BF16),
            pltpu.VMEM(x.shape, BF16),
            pltpu.SemaphoreType.DMA((8,)),
            pltpu.VMEM((cb1, rows + 2 * ROWS, cols + 32, LANES), F32),
            pltpu.VMEM((cb1, 8, cols + 32, LANES), F32),
            pltpu.VMEM((cb1, hr + 2, slots, LANES), F32),
            pltpu.VMEM((4, (hr + 4) * slots, hid), BF16),
            pltpu.VMEM((4, (hr + 4) * hc, hid), BF16),
            pltpu.VMEM((4, (hr + 4) * hc, chan), BF16),
            pltpu.VMEM((cb2, hr + 4, slots + 16, LANES), F32),
            pltpu.VMEM((cb2, hr + 2, slots + 16, LANES), F32),
            pltpu.VMEM((cb1, hr + 2, hc, LANES), F32),
            pltpu.VMEM((cb1, 4, cols + 8, LANES), F32),
            pltpu.VMEM(((hr + 2) * hc, hid), BF16),
            pltpu.VMEM(((hr + 2) * hc, chan), BF16),
            pltpu.VMEM((hr * hc, hid), BF16),
            pltpu.VMEM((4, cb1, hr, hc, LANES), F32),
            pltpu.VMEM((SMALL, LANES), F32),
        ],
        compiler_params=pltpu.CompilerParams(vmem_limit_bytes=63 * 1024 * 1024),
        cost_estimate=pl.CostEstimate(flops=9_000_000_000, bytes_accessed=20_000_000, transcendentals=0),
    )(limits, x, t, *halos, k1, p1, taps, k2, p2)


def edges_kernel(xt, tt, xb, tb, xl, tl, xr, tr, up, down, ahead, back):
    up[...] = jnp.concatenate([xt[0:ROWS], tt[0:2]], axis=0)
    down[...] = jnp.concatenate([xb[8 - ROWS : 8], tb[6:8]], axis=0)
    col = lax.broadcasted_iota(jnp.int32, ahead.shape, 1)
    x, t = xl[:, 0:8, :].astype(F32), tl[:, 0:8, :].astype(F32)
    ahead[...] = jnp.where((col >= 5) & (col < 7), pltpu.roll(t, 5, 1), x).astype(BF16)
    x, t = xr[:, 8:16, :].astype(F32), tr[:, 8:16, :].astype(F32)
    back[...] = jnp.where((col >= 1) & (col < 3), pltpu.roll(t, 3, 1), x).astype(BF16)


def edges(x, t):
    rows, cols, chan = x.shape
    specs = [
        pl.BlockSpec((8, cols, chan), lambda n: (0, 0, 0)),
        pl.BlockSpec((8, cols, chan), lambda n: (rows // 8 - 1, 0, 0)),
        pl.BlockSpec((rows, 16, chan), lambda n: (0, 0, 0)),
        pl.BlockSpec((rows, 16, chan), lambda n: (0, cols // 16 - 1, 0)),
    ]
    shapes = [(ROWS + 2, cols, chan)] * 2 + [(rows, 8, chan)] * 2
    return pl.pallas_call(
        edges_kernel,
        grid=(1,),
        out_shape=[jax.ShapeDtypeStruct(s, BF16) for s in shapes],
        in_specs=[s for s in specs for _ in range(2)],
        out_specs=[pl.BlockSpec(s, lambda n: (0, 0, 0)) for s in shapes],
    )(*[x, t] * 4)


def update_kernel(
    where,
    sums,
    small_ref,
    own_ref,
    other_ref,
    *refs,
):
    (
        k1_ref,
        p1_ref,
        st_hbm,
        k2_ref,
        p2_ref,
        nk1_ref,
        np1_ref,
        nst_ref,
        nk2_ref,
        np2_ref,
        sk1_ref,
        sp1_ref,
        sst_ref,
        sk2_ref,
        sp2_ref,
        g,
        small,
        scale,
        st_ref,
        sems,
    ) = refs
    chan, hid = p2_ref.shape[1], p1_ref.shape[1]
    cb1, cb2 = chan // LANES, hid // LANES
    parts, block = 4, st_ref.shape[1]
    step = pl.program_id(0)
    per = hid // block

    def fetch(n):
        at = pl.ds(n % per * block, block)
        return pltpu.make_async_copy(st_hbm.at[n // per, at, :], st_ref.at[n], sems.at[n])

    core = where[0]
    st_rows, p1_rows, p2_rows = hid * cb2, chan * cb2, hid * cb1
    p1_at = 2 * st_rows
    p2_at = p1_at + p1_rows // 2
    small_at = p2_at + p2_rows // 2
    sizes = (9 * chan, chan * hid, parts * hid * hid, 9 * hid, chan * hid)

    def root(v):
        r = lax.rsqrt(v)
        return v * (r * (1.5 - 0.5 * v * r * r))

    def squares(at, count):
        block = 256

        def body(n, acc):
            rows = pl.ds(pl.multiple_of(at + n * block, block), block)
            out = []
            for half, ref, a in ((core, own_ref, acc[0]), (1 - core, other_ref, acc[1])):
                v = ref[rows, :]
                g[half, rows, :] = v
                v = v.astype(F32)
                out.append(a + jnp.sum((v * v).reshape(block // 8, 8, LANES), axis=0))
            return tuple(out)

        zero = jnp.zeros((8, LANES), F32)
        both = lax.fori_loop(0, count // block, body, (zero, zero))
        return jnp.sum(both[0] + both[1], keepdims=True)

    def set_scale(j, total):
        mean = jnp.broadcast_to(total, (1, LANES)) / sizes[j]
        scale[j : j + 1, :] = 1.0 / root(mean + EPS)
        mean = jnp.full((1, LANES), sums[j] / sizes[j], F32)
        scale[5 + j : 6 + j, :] = RATE * root(mean + EPS)

    @pl.when(step == 0)
    def _():
        for n in range(parts * per):
            fetch(n).start()
        small[...] = small_ref[...].astype(F32)
        v = small[0 : 9 * cb1, :]
        set_scale(0, jnp.sum(v * v, keepdims=True))
        v = small[9 * cb1 : 9 * (cb1 + cb2), :]
        set_scale(3, jnp.sum(v * v, keepdims=True))
        set_scale(1, squares(p1_at, p1_rows // 2))
        set_scale(4, squares(p2_at, p2_rows // 2))
        set_scale(2, squares(0, 2 * st_rows))
        for j, first, blocks, w, new, out in (
            (0, 0, cb1, k1_ref, nk1_ref, sk1_ref),
            (3, 9 * cb1, cb2, k2_ref, nk2_ref, sk2_ref),
        ):
            for c in range(blocks):
                cut = slice(c * LANES, (c + 1) * LANES)
                for r in range(3):
                    at = first + 9 * c + 3 * r
                    normed = small[at : at + 3, :] * scale[j : j + 1, :]
                    out[r, :, cut] = normed
                    new[r, :, cut] = w[r, :, cut] - scale[5 + j : 6 + j, :] * normed

    for j, at, height, blocks, w, new, out in (
        (1, p1_at, chan, cb2, p1_ref, np1_ref, sp1_ref),
        (4, p2_at, hid, cb1, p2_ref, np2_ref, sp2_ref),
    ):
        count = w.shape[0]
        for c in range(blocks):
            cut = slice(c * LANES, (c + 1) * LANES)
            first = at + (c % (blocks // 2)) * height + step * count
            rows = pl.ds(pl.multiple_of(first, count), count)
            normed = g[2 * c // blocks, rows, :].astype(F32) * scale[j : j + 1, :]
            out[:, cut] = normed
            new[:, cut] = w[:, cut] - scale[5 + j : 6 + j, :] * normed

    fetch(step).wait()
    ph = step // per
    for c in range(cb2):
        cut = slice(c * LANES, (c + 1) * LANES)
        at = (ph % 2) * st_rows + c * hid + (step % per) * block
        normed = g[ph // 2, pl.ds(at, block), :].astype(F32) * scale[2:3, :]
        sst_ref[0, :, cut] = normed
        nst_ref[0, :, cut] = st_ref[step, :, cut] - scale[7:8, :] * normed


def update(where, sums, small, own, other, k1, p1, taps, k2, p2):
    hid = taps.shape[1]
    block = hid // 2
    per = hid // block

    def whole(w):
        return pl.BlockSpec(w.shape, lambda n: (0,) * w.ndim)

    st = pl.BlockSpec((1, block, hid), lambda n: (n // per, n % per, 0))
    steps = 4 * per
    p1_spec, p2_spec = [
        pl.BlockSpec((p.shape[0] // steps, p.shape[1]), lambda n: (n, 0)) for p in (p1, p2)
    ]
    specs = [whole(k1), p1_spec, st, whole(k2), p2_spec]
    shapes = [jax.ShapeDtypeStruct(w.shape, F32) for w in (k1, p1, taps, k2, p2)]
    return pl.pallas_call(
        update_kernel,
        grid=(4 * per,),
        out_shape=shapes + shapes,
        in_specs=[smem(), smem(), whole(small)] + [whole(own), whole(other)]
        + specs[:2]
        + [hbm()]
        + specs[3:],
        out_specs=specs + specs,
        scratch_shapes=[
            pltpu.VMEM((2,) + own.shape, BF16),
            pltpu.VMEM((SMALL, LANES), F32),
            pltpu.VMEM((16, LANES), F32),
            pltpu.VMEM((4 * per, block, hid), F32),
            pltpu.SemaphoreType.DMA((4 * per,)),
        ],
        compiler_params=pltpu.CompilerParams(vmem_limit_bytes=50 * 1024 * 1024),
    )(where, sums, small, own, other, k1, p1, taps, k2, p2)


def shift(block, down, right):
    n, m = lax.axis_size("ty"), lax.axis_size("tx")
    pairs = [
        (i * m + j, (i + down) * m + j + right)
        for i in range(n)
        for j in range(m)
        if 0 <= i + down < n and 0 <= j + right < m
    ]
    return lax.ppermute(block, ("ty", "tx"), pairs)


class Ring:
    def __init__(self, names):
        sizes = {"x": lax.axis_size("tx") // 2, "y": lax.axis_size("rep"), "z": lax.axis_size("ty")}
        place = {"x": lax.axis_index("tx") // 2, "y": lax.axis_index("rep"), "z": lax.axis_index("ty")}
        self.names, self.sizes = names, sizes
        self.count = sizes[names[0]]
        assert sizes[names[1]] == self.count
        self.me = jnp.where(lax.axis_index("tx") % 2 == 0, place[names[0]], place[names[1]])

    def send(self, block, step):
        sizes = self.sizes

        def flat(at, core):
            return ((at["y"] * sizes["z"] + at["z"]) * sizes["x"] + at["x"]) * 2 + core

        pairs = []
        for i in range(sizes["y"]):
            for j in range(sizes["z"]):
                for k in range(sizes["x"]):
                    for core in range(2):
                        at = {"y": i, "z": j, "x": k}
                        to = dict(at)
                        name = self.names[core]
                        to[name] = (at[name] + step) % sizes[name]
                        pairs.append((flat(at, core), flat(to, core)))
        return lax.ppermute(block, ("rep", "ty", "tx"), pairs)

    def scatter(self, block, extra):
        n = self.count
        shares = block.reshape((n, -1, LANES))
        share = lax.dynamic_index_in_dim(shares, self.me, 0, False)
        cut = share.shape[0]
        got = {}
        for d in range(1, n):
            out = lax.dynamic_index_in_dim(shares, (self.me + d) % n, 0, False)
            got[d] = self.send(jnp.concatenate([out, extra], axis=0), d)
        total = sum([g[:cut].astype(F32) for g in got.values()], share.astype(F32))
        return total.astype(BF16), self.added([extra] + [got[d][cut:] for d in range(1, n)])

    def added(self, parts):
        n = self.count
        parts = jnp.stack(parts)
        total = None
        for k in range(n):
            part = lax.dynamic_index_in_dim(parts, (self.me + n - k) % n, 0, False).astype(F32)
            total = part if total is None else total + part
        return total.astype(BF16)

    def reduce(self, block):
        got = {d: self.send(block, d) for d in range(1, self.count)}
        return self.added([block] + [got[d] for d in range(1, self.count)])

    def gather(self, share):
        n = self.count
        out = jnp.zeros((n,) + share.shape, share.dtype)
        out = lax.dynamic_update_index_in_dim(out, share, self.me, 0)
        for d in range(1, n):
            got = self.send(share, d)
            out = lax.dynamic_update_index_in_dim(out, got, (self.me + n - d) % n, 0)
        return out.reshape(-1, LANES)


def reduced(keep, send):
    rings = (Ring("yx"), Ring("xy"))
    cores = [(i, i ^ 1) for i in range(lax.axis_size("tx"))]
    got = lax.ppermute(send, "tx", cores)
    both = (keep.astype(F32) + got.astype(F32)).astype(BF16)
    share, small = both[: both.shape[0] - SMALL], both[both.shape[0] - SMALL :]
    for ring in rings:
        share, small = ring.scatter(share, small)
    both = Ring("zz").reduce(jnp.concatenate([share, small], axis=0))
    share, small = both[: share.shape[0]], both[share.shape[0] :]
    for ring in rings[::-1]:
        share = ring.gather(share)
    return small, share, lax.ppermute(share, "tx", cores)


def per_device(inputs, targets, kern_one, point_one, coarsening_taps, kern_two, point_two):
    x = jnp.transpose(inputs[0], (1, 2, 0))
    t = jnp.transpose(targets[0], (1, 2, 0))
    rows, cols, chan = x.shape
    hid = point_one.shape[1]
    hr, hc = rows // 2, cols // 2
    up, down, ahead, back = edges(x, t)
    top, bot = shift(down, 1, 0), shift(up, -1, 0)
    ends = jnp.concatenate([top, bot], axis=0)
    halos = [
        top,
        bot,
        shift(ahead, 0, -1),
        shift(back, 0, 1),
        shift(ends[:, :8], 0, -1),
        shift(ends[:, cols - 8 :], 0, 1),
    ]
    ty, tx = lax.axis_index("ty"), lax.axis_index("tx")
    big = 1 << 20
    limits = jnp.stack(
        [
            jnp.where(ty == 0, 0, -big),
            jnp.where(ty == lax.axis_size("ty") - 1, hr, big),
            jnp.where(tx == 0, 0, -big),
            jnp.where(tx == lax.axis_size("tx") - 1, hc, big),
            tx % 2,
        ]
    ).astype(jnp.int32)
    taps = coarsening_taps.reshape(4, hid, hid)
    weights = (kern_one, point_one, taps, kern_two, point_two)
    pred, keep, send, sums = tile_step(limits, x, t, halos, *weights)
    small, own, other = reduced(keep, send)
    outs = update((tx % 2)[None].astype(jnp.int32), sums, small, own, other, *weights)
    outs = [o.reshape(coarsening_taps.shape) if o.shape == taps.shape else o for o in outs]
    return (jnp.transpose(pred, (2, 0, 1))[None], *outs)


def solution(mesh):
    tile = P("rep", None, "ty", "tx")
    return jax.shard_map(
        per_device,
        mesh=mesh,
        in_specs=(tile, tile, P(), P(), P(), P(), P()),
        out_specs=(tile,) + (P(),) * 10,
        check_vma=False,
    )
```

```python
import jax
import jax.numpy as jnp
from jax import lax
from jax.experimental import pallas as pl
from jax.experimental.pallas import tpu as pltpu
from jax.sharding import PartitionSpec as P

EPS = 1e-05
RATE = 0.05
F32 = jnp.float32
BF16 = jnp.bfloat16
LANES = 128
HALO = 4
ROWS = 6
SMALL = 64


def mm(a, b):
    return jnp.dot(a, b, preferred_element_type=F32)


def mm_t(a, b):
    return lax.dot_general(a, b, (((1,), (1,)), ((), ())), preferred_element_type=F32)


def t_mm(a, b):
    return lax.dot_general(a, b, (((0,), (0,)), ((), ())), preferred_element_type=F32)


def sigmoid(v):
    return 0.5 + 0.5 * jnp.tanh(0.5 * v)


def tile_kernel(
    limits,
    x_hbm,
    t_hbm,
    top_ref,
    bot_ref,
    right_ref,
    left_ref,
    right_ends,
    left_ends,
    k1_ref,
    p1_full,
    taps_hbm,
    k2_ref,
    p2_full,
    pred_hbm,
    keep_hbm,
    send_hbm,
    sums_ref,
    keep_ref,
    send_ref,
    x_ref,
    t_ref,
    taps_full,
    p1_ref,
    p1_half,
    taps_ref,
    p2_ref,
    pred_ref,
    sems,
    xf,
    tf,
    d2,
    out_e,
    out_own,
    pre_own,
    co,
    sl,
    cout,
    up,
    ot_own,
    ce_own,
    bc,
    bp,
    small,
):
    rows, cols, chan = x_ref.shape
    hid = k2_ref.shape[2]
    hr, hc = rows // 2, cols // 2
    slots = hc + 2 * HALO
    cb1, cb2 = chan // LANES, hid // LANES
    er = hr + 4
    fr = hr + 2

    def lanes(c):
        return slice(c * LANES, (c + 1) * LANES)

    core = limits[4]
    st_rows, p1_rows, p2_rows = hid * (hid // LANES), chan * (hid // LANES), hid * (chan // LANES)
    p1_at = 2 * st_rows
    p2_at = p1_at + p1_rows // 2
    small_at = p2_at + p2_rows // 2

    def emit(half, at, value):
        value = value.astype(BF16)

        @pl.when(core == half)
        def _():
            keep_ref[at : at + value.shape[0], :] = value

        @pl.when(core != half)
        def _():
            send_ref[at : at + value.shape[0], :] = value

    large, last = slice(0, small_at), slice(small_at, small_at + SMALL)
    pairs = [
        (t_hbm, t_ref),
        (taps_hbm, taps_full),
        (pred_ref, pred_hbm),
        (x_hbm, x_ref),
        (keep_ref.at[large], keep_hbm.at[large]),
        (send_ref.at[large], send_hbm.at[large]),
        (keep_ref.at[last], keep_hbm.at[last]),
        (send_ref.at[last], send_hbm.at[last]),
    ]
    copies = [pltpu.make_async_copy(*pair, sems.at[j]) for j, pair in enumerate(pairs)]
    copies[3].start()
    copies[0].start()
    copies[1].start()
    small[...] = jnp.zeros_like(small)
    p1_ref[...] = p1_full[...].astype(BF16)
    p1_half[...] = (p1_full[...].astype(BF16).astype(F32) * 0.5).astype(BF16)
    p2_ref[...] = p2_full[...].astype(BF16)

    def put(row, count, block, c):
        block = block.astype(F32)
        xf[c, pl.ds(row, count), 8 : 8 + cols, :] = block
        xf[c, pl.ds(row, count), 24 + cols : 25 + cols, :] = block[:, 0:1, :]

    def put_sides(row, count, right, left, c):
        at = pl.ds(row, count)
        right, left = right.astype(F32), left.astype(F32)
        xf[c, at, 8 + cols : 16 + cols, :] = right
        xf[c, at, 16 + cols : 24 + cols, :] = left
        xf[c, at, 7:8, :] = left[:, 7:8, :]

    step = 12
    for c in range(cb1):
        put(0, ROWS, top_ref[0:ROWS, :, lanes(c)], c)
        put(rows + ROWS, ROWS, bot_ref[0:ROWS, :, lanes(c)], c)
        put_sides(0, ROWS, right_ends[0:ROWS, :, lanes(c)], left_ends[0:ROWS, :, lanes(c)], c)
        cut = (slice(ROWS + 2, 2 * ROWS + 2), slice(None), lanes(c))
        put_sides(rows + ROWS, ROWS, right_ends[cut], left_ends[cut], c)

    copies[3].wait()

    @pl.loop(0, rows // step)
    def _(n):
        at = pl.ds(n * step, step)
        for c in range(cb1):
            put(ROWS + n * step, step, x_ref[at, :, lanes(c)], c)
            put_sides(ROWS + n * step, step, right_ref[at, :, lanes(c)], left_ref[at, :, lanes(c)], c)

    copies[0].wait()

    def diff(first, count, block, right, left, ends, c):
        at = pl.ds(2 * first + ROWS, 2 * count)
        rcol, lcol = (cols, cols + 8) if ends else (cols - 5, cols + 13)
        tf[c, 0 : 2 * count, rcol : rcol + 8, :] = right.astype(F32)
        tf[c, 0 : 2 * count, lcol : lcol + 8, :] = left.astype(F32)
        tf[c, 0 : 2 * count, 0:cols, :] = block.astype(F32)
        both = xf[c, at, 8 : 24 + cols, :] - tf[c, 0 : 2 * count, 0 : 16 + cols, :]
        both = both.reshape(count, 2, 16 + cols, LANES)
        tf[c, 0:count, 0 : 16 + cols, :] = both[:, 0] + both[:, 1]
        even = tf[c, 0:count, pl.ds(0, slots, stride=2), :]
        odd = tf[c, 0:count, pl.ds(1, slots, stride=2), :]
        d2[c, pl.ds(first + 1, count), :, :] = (even + odd) * 0.25

    for c in range(cb1):
        own = (slice(ROWS, ROWS + 2), slice(None), lanes(c))
        diff(-1, 1, top_ref[own], right_ends[own], left_ends[own], True, c)
        cut = (slice(2 * ROWS + 2, 2 * ROWS + 4), slice(None), lanes(c))
        diff(hr, 1, bot_ref[own], right_ends[cut], left_ends[cut], True, c)

    @pl.loop(0, hr // 4)
    def _(n):
        for c in range(cb1):
            cut = (pl.ds(n * 8, 8), slice(None), lanes(c))
            diff(n * 4, 4, t_ref[cut], right_ref[cut], left_ref[cut], False, c)

    take = 4

    @pl.loop(0, er // take)
    def _(n):
        pres = []
        for c in range(cb1):
            per = [[None] * take for _ in range(4)]
            for i in range(take):
                e = 2 * (n * take + i) + ROWS - 4
                near = [
                    [xf[c, e + s - 1, pl.ds(7 + o, slots, stride=2), :] for o in range(4)]
                    for s in range(4)
                ]
                for r in range(2):
                    total = [None, None]
                    for a in range(3):
                        for q in range(2):
                            for b in range(3):
                                term = k1_ref[a, b : b + 1, lanes(c)] * near[r + a][q + b]
                                total[q] = term if total[q] is None else total[q] + term
                    for q in range(2):
                        per[2 * r + q][i] = total[q]
            pres.append([jnp.stack(p) for p in per])
        for ph in range(4):
            for c in range(cb1):
                own = pres[c][ph][:, 0:hc, :].reshape(take * hc, LANES).astype(BF16)
                pre_own[ph, pl.ds(n * (take * hc), take * hc), lanes(c)] = own
        low = [
            jnp.concatenate(
                [pres[c][ph].reshape(take * slots, LANES).astype(BF16) for c in range(cb1)], axis=1
            )
            for ph in range(4)
        ]
        for ph in range(4):
            act = mm(low[ph], p1_half[...])
            out = act + act * jnp.tanh(act)
            out_e[ph, pl.ds(n * (take * slots), take * slots), :] = out.astype(BF16)
            own = out.reshape(take, slots, hid)[:, 0:hc, :].reshape(take * hc, hid)
            out_own[ph, pl.ds(n * (take * hc), take * hc), :] = own.astype(BF16)

    row_lo, row_hi, col_lo, col_hi = limits[0], limits[1], limits[2], limits[3]

    def inside(first, count):
        row = lax.broadcasted_iota(jnp.int32, (count, slots, LANES), 0) + first
        slot = lax.broadcasted_iota(jnp.int32, (count, slots, LANES), 1)
        col = jnp.where(slot < hc + HALO, slot, slot - slots)
        ok = (row >= row_lo) & (row < row_hi) & (col >= col_lo) & (col < col_hi)
        return jnp.where(ok, 1.0, 0.0).astype(F32)

    def wrapped(ref, c, at, value):
        ref[c, at, 8 : 8 + slots, :] = value
        ref[c, at, 7:8, :] = value[:, slots - 1 : slots, :]
        ref[c, at, 8 + slots : 9 + slots, :] = value[:, 0:1, :]

    copies[1].wait()

    piece = 128

    def cast(n, acc):
        ph, at = n // (hid // piece), pl.ds(n % (hid // piece) * piece, piece)
        w = taps_full[ph, at, :]
        taps_ref[ph, at, :] = w.astype(BF16)
        return acc + jnp.sum((w * w).reshape(piece // 8, 8, hid), axis=0)

    sums_ref[2] = jnp.sum(lax.fori_loop(0, 4 * hid // piece, cast, jnp.zeros((8, hid), F32)))
    for j, ref in ((0, k1_ref), (1, p1_full), (3, k2_ref), (4, p2_full)):
        sums_ref[j] = jnp.sum(ref[...] * ref[...])
    half = er // 2

    @pl.loop(0, 2)
    def _(n):
        ok = inside(n * half - 2, half)
        for m in range(hid // 256):
            acc = None
            for ph in range(4):
                term = mm(
                    out_e[ph, pl.ds(n * (half * slots), half * slots), :],
                    taps_ref[ph, :, m * 256 : (m + 1) * 256],
                )
                acc = term if acc is None else acc + term
            acc = acc.astype(BF16).astype(F32).reshape(half, slots, 256)
            for j in range(2):
                wrapped(co, 2 * m + j, pl.ds(n * half, half), acc[:, :, lanes(j)] * ok)

    part = 10

    @pl.loop(0, fr // part)
    def _(n):
        pre = []
        for c in range(cb2):
            subs = []
            for first in range(0, part, 5):
                total = None
                for b in range(3):
                    col = co[c, pl.ds(n * part + first, 7), 7 + b : 7 + b + slots, :]
                    for a in range(3):
                        term = k2_ref[a, b : b + 1, lanes(c)] * col[a : a + 5]
                        total = term if total is None else total + term
                subs.append(total)
            total = jnp.concatenate(subs, axis=0)
            pre.append(total.reshape(part * slots, LANES))
        gate = [sigmoid(p) for p in pre]
        out = [p * g for p, g in zip(pre, gate)]
        low = jnp.concatenate([o.astype(BF16) for o in out], axis=1)
        for c in range(cb2):
            own = out[c].reshape(part, slots, LANES)[:, 0:hc, :].reshape(part * hc, LANES)
            ot_own[pl.ds(n * (part * hc), part * hc), lanes(c)] = own.astype(BF16)
        back = mm(low, p2_ref[...]).reshape(part, slots, chan)
        errs = []
        for c in range(cb1):
            own = back[:, :, lanes(c)]
            cout[c, pl.ds(n * part, part), :, :] = own[:, 0:hc, :]
            err = own + d2[c, pl.ds(n * part, part), :, :]
            errs.append(err.reshape(part * slots, LANES).astype(BF16))
            ce_own[pl.ds(n * (part * hc), part * hc), lanes(c)] = (
                err[:, 0:hc, :].reshape(part * hc, LANES).astype(BF16)
            )
        err = jnp.concatenate(errs, axis=1)
        ok = inside(n * part - 1, part)
        back_two = mm_t(err, p2_ref[...])
        for c in range(cb2):
            slope = back_two[:, lanes(c)] * (gate[c] * (1.0 + pre[c] * (1.0 - gate[c])))
            slope = slope.astype(BF16).astype(F32).reshape(part, slots, LANES) * ok
            wrapped(sl, c, pl.ds(n * part, part), slope)

    gp2 = t_mm(ot_own[hc : hc + hr * hc, :], ce_own[hc : hc + hr * hc, :])
    for c in range(cb1):
        emit(2 * c // cb1, p2_at + (c % (cb1 // 2)) * hid, gp2[:, lanes(c)])

    @pl.loop(0, hr // 4)
    def _(n):
        for c in range(cb1):
            block = cout[c, pl.ds(n * 4 + 1, 4), :, :]
            up[c, :, pl.ds(0, hc, stride=2), :] = block
            up[c, :, pl.ds(1, hc, stride=2), :] = block
            wide = up[c, :, 0:cols, :]
            wide = jnp.stack([wide, wide], axis=1).reshape(8, cols, LANES)
            fine = xf[c, pl.ds(n * 8 + ROWS, 8), 8 : 8 + cols, :]
            pred_ref[pl.ds(n * 8, 8), :, lanes(c)] = (wide + fine).astype(BF16)

    copies[2].start()

    for c in range(cb2):
        def body(n, acc, c=c):
            acc = list(acc)
            for i in range(2):
                row = n * 2 + i
                slope = sl[c, row + 1, 8 : 8 + hc, :]
                total = None
                for a in range(3):
                    for b in range(3):
                        p = slope * co[c, row + 1 + a, 7 + b : 7 + b + hc, :]
                        acc[3 * a + b] = acc[3 * a + b] + (p[0:8] + p[8:16])
                        term = k2_ref[a, b : b + 1, lanes(c)] * sl[c, row + 2 - a, 9 - b : 9 - b + hc, :]
                        total = term if total is None else total + term
                bc[pl.ds(row * hc, hc), lanes(c)] = total.astype(BF16)
            return tuple(acc)

        acc = lax.fori_loop(0, hr // 2, body, tuple(jnp.zeros((8, LANES), F32) for _ in range(9)))
        for j in range(9):
            at = 9 * (cb1 + c) + j
            small[at : at + 1, :] = jnp.sum(acc[j], axis=0, keepdims=True)

    skip = 2 * hc
    own_rows = slice(skip, skip + hr * hc)
    for ph in range(4):
        gst = t_mm(out_own[ph, own_rows, :], bc[...])
        for c in range(cb2):
            emit(ph // 2, (ph % 2) * st_rows + c * hid, gst[:, lanes(c)])
        back = mm_t(bc[...], taps_ref[ph])
        act = mm(pre_own[ph, own_rows, :], p1_half[...])
        turn = jnp.tanh(act)
        slope = (back * ((0.5 + 0.5 * turn) * (1.0 + act * (1.0 - turn)))).astype(BF16)
        term = t_mm(pre_own[ph, own_rows, :], slope)
        gp1 = term if ph == 0 else gp1 + term
        back_pre = mm_t(slope, p1_ref[...])
        for c in range(cb1):
            bp[ph, c] = back_pre[:, lanes(c)].reshape(hr, hc, LANES)

    for c in range(cb2):
        emit(2 * c // cb2, p1_at + (c % (cb2 // 2)) * chan, gp1[:, lanes(c)])
    copies[4].start()
    copies[5].start()

    for c in range(cb1):

        def body(n, acc, c=c):
            acc = list(acc)
            grads = [[bp[ph, c, 4 * n + i] for ph in range(4)] for i in range(4)]
            for s in range(10):
                e = 8 * n + ROWS + s - 1
                col = [xf[c, e, pl.ds(7 + o, hc, stride=2), :] for o in range(4)]
                for i in range(4):
                    for r in range(2):
                        a = s - 2 * i - r
                        if 0 <= a < 3:
                            for q in range(2):
                                for b in range(3):
                                    p = grads[i][2 * r + q] * col[q + b]
                                    acc[3 * a + b] = acc[3 * a + b] + (p[0:8] + p[8:16])
            return tuple(acc)

        acc = lax.fori_loop(0, hr // 4, body, tuple(jnp.zeros((8, LANES), F32) for _ in range(9)))
        for j in range(9):
            at = 9 * c + j
            small[at : at + 1, :] = jnp.sum(acc[j], axis=0, keepdims=True)


    for ref in (keep_ref, send_ref):
        ref[small_at : small_at + SMALL, :] = small[...].astype(BF16)
    copies[6].start()
    copies[7].start()
    for j in (2, 4, 5, 6, 7):
        copies[j].wait()


def vmem():
    return pl.BlockSpec(memory_space=pltpu.VMEM)


def hbm():
    return pl.BlockSpec(memory_space=pl.ANY)


def smem():
    return pl.BlockSpec(memory_space=pltpu.SMEM)


def tile_step(limits, x, t, halos, k1, p1, taps, k2, p2):
    rows, cols, chan = x.shape
    hid = k2.shape[2]
    hr, hc = rows // 2, cols // 2
    slots = hc + 2 * HALO
    cb1, cb2 = chan // LANES, hid // LANES
    grads = (p1.size + taps.size + p2.size) // (2 * LANES) + SMALL
    return pl.pallas_call(
        tile_kernel,
        out_shape=(
            jax.ShapeDtypeStruct(x.shape, BF16),
            jax.ShapeDtypeStruct((grads, LANES), BF16),
            jax.ShapeDtypeStruct((grads, LANES), BF16),
            jax.ShapeDtypeStruct((5,), F32),
        ),
        in_specs=[smem(), hbm(), hbm()]
        + [vmem()] * (len(halos) + 2)
        + [hbm(), vmem(), vmem()],
        out_specs=[hbm(), hbm(), hbm(), smem()],
        scratch_shapes=[
            pltpu.VMEM((grads, LANES), BF16),
            pltpu.VMEM((grads, LANES), BF16),
            pltpu.VMEM(x.shape, BF16),
            pltpu.VMEM(t.shape, BF16),
            pltpu.VMEM(taps.shape, F32),
            pltpu.VMEM(p1.shape, BF16),
            pltpu.VMEM(p1.shape, BF16),
            pltpu.VMEM(taps.shape, BF16),
            pltpu.VMEM(p2.shape, BF16),
            pltpu.VMEM(x.shape, BF16),
            pltpu.SemaphoreType.DMA((8,)),
            pltpu.VMEM((cb1, rows + 2 * ROWS, cols + 32, LANES), F32),
            pltpu.VMEM((cb1, 8, cols + 32, LANES), F32),
            pltpu.VMEM((cb1, hr + 2, slots, LANES), F32),
            pltpu.VMEM((4, (hr + 4) * slots, hid), BF16),
            pltpu.VMEM((4, (hr + 4) * hc, hid), BF16),
            pltpu.VMEM((4, (hr + 4) * hc, chan), BF16),
            pltpu.VMEM((cb2, hr + 4, slots + 16, LANES), F32),
            pltpu.VMEM((cb2, hr + 2, slots + 16, LANES), F32),
            pltpu.VMEM((cb1, hr + 2, hc, LANES), F32),
            pltpu.VMEM((cb1, 4, cols + 8, LANES), F32),
            pltpu.VMEM(((hr + 2) * hc, hid), BF16),
            pltpu.VMEM(((hr + 2) * hc, chan), BF16),
            pltpu.VMEM((hr * hc, hid), BF16),
            pltpu.VMEM((4, cb1, hr, hc, LANES), F32),
            pltpu.VMEM((SMALL, LANES), F32),
        ],
        compiler_params=pltpu.CompilerParams(vmem_limit_bytes=63 * 1024 * 1024),
        cost_estimate=pl.CostEstimate(flops=9_000_000_000, bytes_accessed=20_000_000, transcendentals=0),
    )(limits, x, t, *halos, k1, p1, taps, k2, p2)


def rows_kernel(xt, tt, xb, tb, up, down):
    up[...] = jnp.concatenate([xt[0:ROWS], tt[0:2]], axis=0)
    down[...] = jnp.concatenate([xb[8 - ROWS : 8], tb[6:8]], axis=0)


def columns_kernel(xl, tl, xr, tr, ahead, back):
    col = lax.broadcasted_iota(jnp.int32, ahead.shape, 1)
    x, t = xl[:, 0:8, :].astype(F32), tl[:, 0:8, :].astype(F32)
    ahead[...] = jnp.where((col >= 5) & (col < 7), pltpu.roll(t, 5, 1), x).astype(BF16)
    x, t = xr[:, 8:16, :].astype(F32), tr[:, 8:16, :].astype(F32)
    back[...] = jnp.where((col >= 1) & (col < 3), pltpu.roll(t, 3, 1), x).astype(BF16)


def edges(x, t):
    rows, cols, chan = x.shape
    specs = [
        pl.BlockSpec((8, cols, chan), lambda n: (0, 0, 0)),
        pl.BlockSpec((8, cols, chan), lambda n: (rows // 8 - 1, 0, 0)),
        pl.BlockSpec((rows, 16, chan), lambda n: (0, 0, 0)),
        pl.BlockSpec((rows, 16, chan), lambda n: (0, cols // 16 - 1, 0)),
    ]
    outs = []
    for kernel, pair, shape in (
        (rows_kernel, specs[:2], (ROWS + 2, cols, chan)),
        (columns_kernel, specs[2:], (rows, 8, chan)),
    ):
        outs += pl.pallas_call(
            kernel,
            grid=(1,),
            out_shape=[jax.ShapeDtypeStruct(shape, BF16)] * 2,
            in_specs=[s for s in pair for _ in range(2)],
            out_specs=[pl.BlockSpec(shape, lambda n: (0, 0, 0))] * 2,
        )(x, t, x, t)
    return outs


def update_kernel(
    where,
    sums,
    small_ref,
    own_ref,
    other_ref,
    *refs,
):
    (
        k1_ref,
        p1_ref,
        st_hbm,
        k2_ref,
        p2_ref,
        nk1_ref,
        np1_ref,
        nst_ref,
        nk2_ref,
        np2_ref,
        sk1_ref,
        sp1_ref,
        sst_ref,
        sk2_ref,
        sp2_ref,
        g,
        small,
        scale,
        st_ref,
        sems,
    ) = refs
    chan, hid = p2_ref.shape[1], p1_ref.shape[1]
    cb1, cb2 = chan // LANES, hid // LANES
    parts, block = 4, st_ref.shape[1]
    step = pl.program_id(0)
    per = hid // block

    def fetch(n):
        at = pl.ds(n % per * block, block)
        return pltpu.make_async_copy(st_hbm.at[n // per, at, :], st_ref.at[n], sems.at[n])

    core = where[0]
    st_rows, p1_rows, p2_rows = hid * cb2, chan * cb2, hid * cb1
    p1_at = 2 * st_rows
    p2_at = p1_at + p1_rows // 2
    small_at = p2_at + p2_rows // 2
    sizes = (9 * chan, chan * hid, parts * hid * hid, 9 * hid, chan * hid)

    def root(v):
        r = lax.rsqrt(v)
        return v * (r * (1.5 - 0.5 * v * r * r))

    def squares(at, count):
        block = 256

        def body(n, acc):
            rows = pl.ds(pl.multiple_of(at + n * block, block), block)
            out = []
            for half, ref, a in ((core, own_ref, acc[0]), (1 - core, other_ref, acc[1])):
                v = ref[rows, :]
                g[half, rows, :] = v
                v = v.astype(F32)
                out.append(a + jnp.sum((v * v).reshape(block // 8, 8, LANES), axis=0))
            return tuple(out)

        zero = jnp.zeros((8, LANES), F32)
        both = lax.fori_loop(0, count // block, body, (zero, zero))
        return jnp.sum(both[0] + both[1], keepdims=True)

    def set_scale(j, total):
        mean = jnp.broadcast_to(total, (1, LANES)) / sizes[j]
        scale[j : j + 1, :] = 1.0 / root(mean + EPS)
        mean = jnp.full((1, LANES), sums[j] / sizes[j], F32)
        scale[5 + j : 6 + j, :] = RATE * root(mean + EPS)

    @pl.when(step == 0)
    def _():
        for n in range(parts * per):
            fetch(n).start()
        small[...] = small_ref[...].astype(F32)
        v = small[0 : 9 * cb1, :]
        set_scale(0, jnp.sum(v * v, keepdims=True))
        v = small[9 * cb1 : 9 * (cb1 + cb2), :]
        set_scale(3, jnp.sum(v * v, keepdims=True))
        set_scale(1, squares(p1_at, p1_rows // 2))
        set_scale(4, squares(p2_at, p2_rows // 2))
        set_scale(2, squares(0, 2 * st_rows))
        for j, first, blocks, w, new, out in (
            (0, 0, cb1, k1_ref, nk1_ref, sk1_ref),
            (3, 9 * cb1, cb2, k2_ref, nk2_ref, sk2_ref),
        ):
            for c in range(blocks):
                cut = slice(c * LANES, (c + 1) * LANES)
                for r in range(3):
                    at = first + 9 * c + 3 * r
                    normed = small[at : at + 3, :] * scale[j : j + 1, :]
                    out[r, :, cut] = normed
                    new[r, :, cut] = w[r, :, cut] - scale[5 + j : 6 + j, :] * normed

    for j, at, height, blocks, w, new, out in (
        (1, p1_at, chan, cb2, p1_ref, np1_ref, sp1_ref),
        (4, p2_at, hid, cb1, p2_ref, np2_ref, sp2_ref),
    ):
        count = w.shape[0]
        for c in range(blocks):
            cut = slice(c * LANES, (c + 1) * LANES)
            first = at + (c % (blocks // 2)) * height + step * count
            rows = pl.ds(pl.multiple_of(first, count), count)
            normed = g[2 * c // blocks, rows, :].astype(F32) * scale[j : j + 1, :]
            out[:, cut] = normed
            new[:, cut] = w[:, cut] - scale[5 + j : 6 + j, :] * normed

    fetch(step).wait()
    ph = step // per
    for c in range(cb2):
        cut = slice(c * LANES, (c + 1) * LANES)
        at = (ph % 2) * st_rows + c * hid + (step % per) * block
        normed = g[ph // 2, pl.ds(at, block), :].astype(F32) * scale[2:3, :]
        sst_ref[0, :, cut] = normed
        nst_ref[0, :, cut] = st_ref[step, :, cut] - scale[7:8, :] * normed


def update(where, sums, small, own, other, k1, p1, taps, k2, p2):
    hid = taps.shape[1]
    block = hid // 2
    per = hid // block

    def whole(w):
        return pl.BlockSpec(w.shape, lambda n: (0,) * w.ndim)

    st = pl.BlockSpec((1, block, hid), lambda n: (n // per, n % per, 0))
    steps = 4 * per
    p1_spec, p2_spec = [
        pl.BlockSpec((p.shape[0] // steps, p.shape[1]), lambda n: (n, 0)) for p in (p1, p2)
    ]
    specs = [whole(k1), p1_spec, st, whole(k2), p2_spec]
    shapes = [jax.ShapeDtypeStruct(w.shape, F32) for w in (k1, p1, taps, k2, p2)]
    return pl.pallas_call(
        update_kernel,
        grid=(4 * per,),
        out_shape=shapes + shapes,
        in_specs=[smem(), smem(), whole(small)] + [whole(own), whole(other)]
        + specs[:2]
        + [hbm()]
        + specs[3:],
        out_specs=specs + specs,
        scratch_shapes=[
            pltpu.VMEM((2,) + own.shape, BF16),
            pltpu.VMEM((SMALL, LANES), F32),
            pltpu.VMEM((16, LANES), F32),
            pltpu.VMEM((4 * per, block, hid), F32),
            pltpu.SemaphoreType.DMA((4 * per,)),
        ],
        compiler_params=pltpu.CompilerParams(vmem_limit_bytes=50 * 1024 * 1024),
    )(where, sums, small, own, other, k1, p1, taps, k2, p2)


def shift(block, down, right):
    n, m = lax.axis_size("ty"), lax.axis_size("tx")
    pairs = [
        (i * m + j, (i + down) * m + j + right)
        for i in range(n)
        for j in range(m)
        if 0 <= i + down < n and 0 <= j + right < m
    ]
    return lax.ppermute(block, ("ty", "tx"), pairs)


class Ring:
    def __init__(self, names):
        sizes = {"x": lax.axis_size("tx") // 2, "y": lax.axis_size("rep"), "z": lax.axis_size("ty")}
        place = {"x": lax.axis_index("tx") // 2, "y": lax.axis_index("rep"), "z": lax.axis_index("ty")}
        self.names, self.sizes = names, sizes
        self.count = sizes[names[0]]
        assert sizes[names[1]] == self.count
        self.me = jnp.where(lax.axis_index("tx") % 2 == 0, place[names[0]], place[names[1]])

    def send(self, block, step):
        sizes = self.sizes

        def flat(at, core):
            return ((at["y"] * sizes["z"] + at["z"]) * sizes["x"] + at["x"]) * 2 + core

        pairs = []
        for i in range(sizes["y"]):
            for j in range(sizes["z"]):
                for k in range(sizes["x"]):
                    for core in range(2):
                        at = {"y": i, "z": j, "x": k}
                        to = dict(at)
                        name = self.names[core]
                        to[name] = (at[name] + step) % sizes[name]
                        pairs.append((flat(at, core), flat(to, core)))
        return lax.ppermute(block, ("rep", "ty", "tx"), pairs)

    def scatter(self, block, extra):
        n = self.count
        shares = block.reshape((n, -1, LANES))
        share = lax.dynamic_index_in_dim(shares, self.me, 0, False)
        cut = share.shape[0]
        got = {}
        for d in range(1, n):
            out = lax.dynamic_index_in_dim(shares, (self.me + d) % n, 0, False)
            got[d] = self.send(jnp.concatenate([out, extra], axis=0), d)
        total = sum([g[:cut].astype(F32) for g in got.values()], share.astype(F32))
        return total.astype(BF16), self.added([extra] + [got[d][cut:] for d in range(1, n)])

    def added(self, parts):
        n = self.count
        parts = jnp.stack(parts)
        total = None
        for k in range(n):
            part = lax.dynamic_index_in_dim(parts, (self.me + n - k) % n, 0, False).astype(F32)
            total = part if total is None else total + part
        return total.astype(BF16)

    def reduce(self, block):
        got = {d: self.send(block, d) for d in range(1, self.count)}
        return self.added([block] + [got[d] for d in range(1, self.count)])

    def gather(self, share):
        n = self.count
        out = jnp.zeros((n,) + share.shape, share.dtype)
        out = lax.dynamic_update_index_in_dim(out, share, self.me, 0)
        for d in range(1, n):
            got = self.send(share, d)
            out = lax.dynamic_update_index_in_dim(out, got, (self.me + n - d) % n, 0)
        return out.reshape(-1, LANES)


def reduced(keep, send):
    rings = (Ring("yx"), Ring("xy"))
    cores = [(i, i ^ 1) for i in range(lax.axis_size("tx"))]
    got = lax.ppermute(send, "tx", cores)
    both = (keep.astype(F32) + got.astype(F32)).astype(BF16)
    share, small = both[: both.shape[0] - SMALL], both[both.shape[0] - SMALL :]
    for ring in rings:
        share, small = ring.scatter(share, small)
    both = Ring("zz").reduce(jnp.concatenate([share, small], axis=0))
    share, small = both[: share.shape[0]], both[share.shape[0] :]
    for ring in rings[::-1]:
        share = ring.gather(share)
    return small, share, lax.ppermute(share, "tx", cores)


def per_device(inputs, targets, kern_one, point_one, coarsening_taps, kern_two, point_two):
    x = jnp.transpose(inputs[0], (1, 2, 0))
    t = jnp.transpose(targets[0], (1, 2, 0))
    rows, cols, chan = x.shape
    hid = point_one.shape[1]
    hr, hc = rows // 2, cols // 2
    up, down, ahead, back = edges(x, t)
    top, bot = shift(down, 1, 0), shift(up, -1, 0)
    ends = jnp.concatenate([top, bot], axis=0)
    halos = [
        top,
        bot,
        shift(ahead, 0, -1),
        shift(back, 0, 1),
        shift(ends[:, :8], 0, -1),
        shift(ends[:, cols - 8 :], 0, 1),
    ]
    ty, tx = lax.axis_index("ty"), lax.axis_index("tx")
    big = 1 << 20
    limits = jnp.stack(
        [
            jnp.where(ty == 0, 0, -big),
            jnp.where(ty == lax.axis_size("ty") - 1, hr, big),
            jnp.where(tx == 0, 0, -big),
            jnp.where(tx == lax.axis_size("tx") - 1, hc, big),
            tx % 2,
        ]
    ).astype(jnp.int32)
    taps = coarsening_taps.reshape(4, hid, hid)
    weights = (kern_one, point_one, taps, kern_two, point_two)
    pred, keep, send, sums = tile_step(limits, x, t, halos, *weights)
    small, own, other = reduced(keep, send)
    outs = update((tx % 2)[None].astype(jnp.int32), sums, small, own, other, *weights)
    outs = [o.reshape(coarsening_taps.shape) if o.shape == taps.shape else o for o in outs]
    return (jnp.transpose(pred, (2, 0, 1))[None], *outs)


def solution(mesh):
    tile = P("rep", None, "ty", "tx")
    return jax.shard_map(
        per_device,
        mesh=mesh,
        in_specs=(tile, tile, P(), P(), P(), P(), P()),
        out_specs=(tile,) + (P(),) * 10,
        check_vma=False,
    )
```
